32 devices in a mesh: seq: 8 (over z, y), head: 4 (over x, core).
Axes of the slice: x: 2, y: 2, z: 4, core: 2. Of those that a mesh axis runs over, the one named last changes fastest.
Arguments:
- tokens: bfloat16 [4096, 2048], P(('seq', 'head'))
- ln_gain: float32 [2048], replicated, may hold values from 0.1 to 1.9
- w_qkv: bfloat16 [2048, 3, 2048], P(None, None, 'head')
- slopes: float32 [16], P('head')
- w_out: bfloat16 [2048, 2048], P('head'), may hold values from -0.125 to 0.125
- seg_ids: int32 [4096], P('seq'), may hold values from 0 to 3, never falling along the last dimension, each value on 1 to 2048 neighbouring positions
Outputs:
- hidden: bfloat16 [4096, 2048], P(('seq', 'head'))
- key_cache: bfloat16 [4096, 2048], P('seq', 'head')
- value_cache: bfloat16 [4096, 2048], P('seq', 'head')
The draws below stay inside these ranges and needn't reach their ends.
Inputs may be any that keep to these rules, and one draw needn't show every extreme that they name: `seg_ids`: Non-decreasing along the stream; each prompt number names 1 to 2048 consecutive tokens, one prompt exactly 2048.
All inputs are finite; a program needn't handle non-finite values.
Results may differ from the reference program's by a relative error of at most 0.0075.
Values may be sent and summed in bfloat16 or wider, within the bound.
No kernel may reach another device: no remote copies, remote signals or barrier semaphores. Data moves between devices by JAX's collectives and lax.ppermute only.
A program may use at most 128 MiB of HBM per device.

```python
import math
import jax
import jax.numpy as jnp
import numpy as np
from jax import lax

D = 2048
HEADS = 16
HD = 128
TOK_DEV = 512
SPAN = 4
HEADS_DEV = 4
TOKENS = 4096
SEG_MOST = 2048
PROMPTS = 4
N_SEQ = 8
N_HEAD = 4


def draw_tokens(key, part):
    k_rough = jax.random.fold_in(key, 31)
    k_period = jax.random.fold_in(key, 32)
    k_phase = jax.random.fold_in(key, 33)
    positions = jnp.arange(TOKENS, dtype=jnp.float32)[:, None]
    periods = jnp.exp(jax.random.uniform(k_period, (1, D), jnp.float32, math.log(300.0), math.log(6000.0)))
    phases = jax.random.uniform(k_phase, (1, D), jnp.float32, -math.pi, math.pi)
    smooth = jnp.sin(2.0 * math.pi * positions / periods + phases)
    values = jax.random.normal(k_rough, (TOKENS, D), jnp.float32) + smooth
    return values.astype(jnp.bfloat16)


def draw_w_qkv(key, part):
    base = jax.random.normal(jax.random.fold_in(key, 41), (D, 3, HEADS * HD), jnp.float32) * D ** (-0.5)
    values = base
    return values.astype(jnp.bfloat16)


def draw_slopes(key, part):
    values = jnp.exp(jax.random.uniform(jax.random.fold_in(key, 51), (HEADS,), jnp.float32, math.log(0.0002), math.log(0.4)))
    return values.astype(jnp.float32)


def levels(key, shape, pieces, smallest, largest):
    factor_of = 1.0
    for dim, parts in pieces:
        draws = jax.random.uniform(jax.random.fold_in(jax.random.fold_in(key, 6), dim), (parts,), jnp.float32, smallest / len(pieces), largest / len(pieces))
        factor_of = factor_of * jnp.repeat(jnp.exp(draws), shape[dim] // parts).reshape((-1,) + (1,) * (len(shape) - 1 - dim))
    return factor_of


def split_up(number_of, total, limit, lean):
    loads = [(1 << 20) // math.isqrt(grade ** lean) + 1 for grade in range(2, number_of + 1)]
    rest, given = total - limit - (number_of - 1), [1] * (number_of - 1)
    while rest > 0:
        free = [i for i in range(number_of - 1) if given[i] < limit]
        pool, budget = sum([loads[i] for i in free]), rest
        for i in free:
            more = min(limit - given[i], max(1, budget * loads[i] // pool), rest)
            given[i] = given[i] + more
            rest = rest - more
    return np.array([limit] + given)


def ragged(rng, amount, total, bound, slope):
    if amount == 2:
        one = jax.random.randint(rng, (), max(1, total - bound), min(bound, total - 1) + 1)
        return jnp.stack([one, total - one])
    sizes = jnp.asarray(split_up(amount, total, bound, slope), jnp.int32)
    twos = (amount - 1) // 2
    donor, sink = sizes[1:1 + 2 * twos:2], sizes[2:2 + 2 * twos:2]
    slack = jnp.minimum(donor - 1, bound - sink)
    passed = jax.random.randint(jax.random.fold_in(rng, 1), (twos,), 0, 1 << 20) % (slack + 1)
    sizes = sizes.at[1:1 + 2 * twos:2].set(donor - passed).at[2:2 + 2 * twos:2].set(sink + passed)
    return sizes[jax.random.permutation(jax.random.fold_in(rng, 2), amount)]


def noise(rng, shape, scale, limit, cuts=(), kind=jnp.bfloat16):
    result = scale * jax.random.normal(rng, shape, jnp.float32)
    if cuts:
        result = result * levels(rng, shape, cuts, -0.22, 0.18)
    return jnp.clip(result, -limit, limit).astype(kind)


def setup_inputs(seed: int = 0) -> dict:
    arg_keys = jax.random.split(jax.random.key(seed), 7)
    return {
        "tokens": draw_tokens(jax.random.fold_in(arg_keys[6], 71), 0),
        "ln_gain": jnp.clip(1.0 + 0.18 * jax.random.normal(arg_keys[1], (D,), jnp.float32), 0.1, 1.9),
        "w_qkv": draw_w_qkv(jax.random.fold_in(arg_keys[6], 71), 0),
        "slopes": draw_slopes(jax.random.fold_in(arg_keys[6], 71), 0),
        "w_out": noise(arg_keys[4], (HEADS * HD, D), (HEADS * HD) ** -0.5, 0.125, ((0, 4),)),
        "seg_ids": jnp.searchsorted(jnp.cumsum(ragged(arg_keys[5], PROMPTS, TOKENS, SEG_MOST, 2)), jnp.arange(TOKENS), side="right").astype(jnp.int32),
    }


EPSILON = 1e-05
NEG_FILL = -1e+30

def attend_block(block_num, query, key_pad, value_pad, seg_pad, seg_ids, slopes):
    first = (block_num * TOK_DEV).astype(jnp.int32)
    reach = (SPAN + 1) * TOK_DEV
    q_block = lax.dynamic_slice_in_dim(query, first, TOK_DEV, 0).reshape(TOK_DEV, HEADS, HD).astype(jnp.float32)
    k_block = lax.dynamic_slice_in_dim(key_pad, first, reach, 0).reshape(reach, HEADS, HD).astype(jnp.float32)
    v_block = lax.dynamic_slice_in_dim(value_pad, first, reach, 0).reshape(reach, HEADS, HD).astype(jnp.float32)
    seg_key = lax.dynamic_slice_in_dim(seg_pad, first, reach, 0)
    seg_query = lax.dynamic_slice_in_dim(seg_ids, first, TOK_DEV, 0)
    q_pos = first + jnp.arange(TOK_DEV, dtype=jnp.int32)
    k_pos = first - SPAN * TOK_DEV + jnp.arange(reach, dtype=jnp.int32)
    scores = jnp.einsum('qhe,khe->qhk', q_block, k_block) * HD ** (-0.5)
    distance = (q_pos[:, None] - k_pos[None, :]).astype(jnp.float32)
    scores = scores - slopes.astype(jnp.float32)[None, :, None] * distance[:, None, :]
    valid_mask = ((seg_query[:, None] == seg_key[None, :]) & (k_pos[None, :] <= q_pos[:, None]) & (k_pos[None, :] >= 0))[:, None, :]
    scores = jnp.where(valid_mask, scores, NEG_FILL)
    row_max = lax.optimization_barrier(jnp.max(scores, axis=-1, keepdims=True))
    expo = jnp.where(valid_mask, jnp.exp(scores - row_max), 0.0)
    denominator = lax.optimization_barrier(jnp.sum(expo, axis=-1))
    probs = lax.optimization_barrier(expo.astype(jnp.bfloat16)).astype(jnp.float32)
    context = jnp.einsum('qhk,khe->qhe', probs, v_block) / denominator[..., None]
    return context.astype(jnp.bfloat16).reshape(TOK_DEV, HEADS * HD)

def reference(tokens, ln_gain, w_qkv, slopes, w_out, seg_ids):
    inputs = tokens.astype(jnp.float32)
    row_mean = lax.optimization_barrier(jnp.mean(inputs, axis=-1, keepdims=True))
    centred = inputs - row_mean
    variance = lax.optimization_barrier(jnp.mean(centred * centred, axis=-1, keepdims=True))
    normed = (centred * lax.rsqrt(variance + EPSILON) * ln_gain.astype(jnp.float32)).astype(jnp.bfloat16)
    width = HEADS * HD
    qkv_rows = jnp.dot(normed, w_qkv.reshape(D, 3 * width), preferred_element_type=jnp.float32).astype(jnp.bfloat16)
    query = qkv_rows[:, :width]
    key_cache = qkv_rows[:, width:2 * width]
    value_cache = qkv_rows[:, 2 * width:]
    key_pad = jnp.concatenate([jnp.zeros((SPAN * TOK_DEV, width), jnp.bfloat16), key_cache], axis=0)
    value_pad = jnp.concatenate([jnp.zeros((SPAN * TOK_DEV, width), jnp.bfloat16), value_cache], axis=0)
    seg_pad = jnp.concatenate([jnp.full((SPAN * TOK_DEV,), -1, jnp.int32), seg_ids.astype(jnp.int32)], axis=0)
    context = lax.map(lambda block_num: attend_block(block_num, query, key_pad, value_pad, seg_pad, seg_ids.astype(jnp.int32), slopes), jnp.arange(N_SEQ, dtype=jnp.int32))
    context = context.reshape(TOKENS, width)
    group_cols = HEADS_DEV * HD
    summed = inputs
    for group in range(N_HEAD):
        partial_g = jnp.dot(context[:, group * group_cols:(group + 1) * group_cols], w_out[group * group_cols:(group + 1) * group_cols, :], preferred_element_type=jnp.float32)
        summed = summed + lax.optimization_barrier(partial_g.astype(jnp.bfloat16)).astype(jnp.float32)
    return (summed.astype(jnp.bfloat16), key_cache, value_cache)
```

```python
import functools

import jax
import jax.numpy as jnp
from jax import lax
from jax.experimental import pallas as pl
from jax.experimental.pallas import tpu as pltpu
from jax.sharding import PartitionSpec as P

HD = 128
PIECE = 128
EPSILON = 1e-05
NEG_FILL = -1e30
MASKED = -2e38
LOG2E = 1.4426950408889634
VMEM_LIMIT = 56 * 2**20

BF16 = jnp.bfloat16
F32 = jnp.float32
ANY = pl.BlockSpec(memory_space=pl.ANY)
SMEM = pl.BlockSpec(memory_space=pltpu.SMEM)
VMEM = pl.BlockSpec(memory_space=pltpu.VMEM)


def params():
    return pltpu.CompilerParams(vmem_limit_bytes=VMEM_LIMIT)


def cost(macs, nbytes, exps=0):
    return pl.CostEstimate(flops=2 * macs, bytes_accessed=nbytes, transcendentals=exps)


def dot(lhs, rhs):
    return jnp.dot(lhs, rhs, preferred_element_type=F32)


def layer_norm(tokens, ln_gain):
    def body(tokens_ref, gain_ref, out_ref):
        inputs = tokens_ref[...].astype(F32)
        centred = inputs - jnp.mean(inputs, axis=-1, keepdims=True)
        variance = jnp.mean(centred * centred, axis=-1, keepdims=True)
        out_ref[...] = (centred * lax.rsqrt(variance + EPSILON) * gain_ref[...]).astype(BF16)

    return pl.pallas_call(
        body,
        out_shape=jax.ShapeDtypeStruct(tokens.shape, BF16),
        in_specs=[VMEM, VMEM],
        out_specs=VMEM,
        compiler_params=params(),
        cost_estimate=cost(0, 2 * tokens.size * 2, tokens.size),
    )(tokens, ln_gain.reshape(1, -1))


def set_masks(info_ref, lo_ref, key_base, keys, mask_ref, dist_ref):
    block_base = info_ref[0]
    lane = lax.broadcasted_iota(jnp.int32, (1, PIECE), 1)
    row = lax.broadcasted_iota(jnp.int32, (PIECE, PIECE), 0)
    for piece in range(keys):
        k_pos = row + key_base(piece)
        rows = pl.ds(piece * PIECE, PIECE)
        dist_ref[rows, :] = (k_pos - block_base).astype(F32)
        for place in range(4):
            head = info_ref[1 + place]
            q_pos = lane + (block_base + head * PIECE)
            first = lo_ref[pl.ds(head, 1), :]
            kept = (k_pos >= first) & (k_pos <= q_pos)
            mask_ref[rows, pl.ds(place * PIECE, PIECE)] = jnp.where(kept, 0.0, MASKED)


def attend(group, k_rows, v_t, q_ref, slopes_ref, mask_ref, dist_ref, stat_ref, acc_ref, fresh):
    heads = k_rows.shape[1] // HD
    for local in range(heads):
        head = group * heads + local
        cols = slice(local * HD, (local + 1) * HD)
        wide = pl.ds(head * HD, HD)
        bias = dist_ref[...] * (slopes_ref[head] * LOG2E)
        bias = jnp.concatenate([bias] * (q_ref.shape[1] // PIECE), axis=1)
        scores = dot(k_rows[:, cols], q_ref[wide, :]) * (HD**-0.5 * LOG2E)
        scores = scores + bias + mask_ref[...]
        top = jnp.max(scores, axis=0, keepdims=True)
        prev = jnp.full_like(top, NEG_FILL) if fresh else stat_ref[head : head + 1, :]
        row_max = jnp.maximum(prev, top)
        expo = jnp.exp2(scores - row_max)
        total = jnp.sum(expo, axis=0, keepdims=True)
        update = dot(v_t[cols, :], expo.astype(BF16))
        stat_ref[head : head + 1, :] = row_max
        if fresh:
            stat_ref[8 + head : 9 + head, :] = total
            acc_ref[wide, :] = update
        else:
            rescale = jnp.exp2(prev - row_max)
            stat_ref[8 + head : 9 + head, :] = stat_ref[8 + head : 9 + head, :] * rescale + total
            acc_ref[wide, :] = acc_ref[wide, :] * rescale + update


def own_block(info, slopes, lo, pieces, w_own, w_pair):
    depth, width = w_own.shape[1:]
    block = 4 * PIECE

    def body(info_ref, slopes_ref, lo_ref, a, b, c, d, w0, w1, q_out, stat_out, acc_out, k_out, v_out,
             x, w, q, k_cache, v_cache, stat, acc, mask, dist, sems, out_sems):
        loads = [pltpu.make_async_copy(src, x.at[pl.ds(i * PIECE, PIECE)], sems.at[i])
                 for i, src in enumerate((a, b, c, d))]
        w_loads = [pltpu.make_async_copy(src.at[part], w.at[3 * g + part], sems.at[4 + 3 * g + part])
                   for g, src in enumerate((w0, w1)) for part in range(3)]
        for copy in loads + w_loads:
            copy.start()
        set_masks(info_ref, lo_ref, lambda i: info_ref[0] + info_ref[1 + i] * PIECE, 2, mask, dist)
        for copy in loads:
            copy.wait()
        for group in range(2):
            rows = block if group == 0 else 2 * PIECE
            w_loads[3 * group].wait()
            q[pl.ds(group * width, width), :] = dot(x[...], w[3 * group]).T.astype(BF16)
            w_loads[3 * group + 1].wait()
            keys = dot(x[:rows, :], w[3 * group + 1]).astype(BF16)
            w_loads[3 * group + 2].wait()
            values = dot(x[:rows, :], w[3 * group + 2])
            if group == 0:
                for place in range(4):
                    to = pl.ds(pl.multiple_of(info_ref[1 + place] * PIECE, PIECE), PIECE)
                    k_cache[to, :] = keys[place * PIECE : (place + 1) * PIECE]
                    v_cache[to, :] = values[place * PIECE : (place + 1) * PIECE].astype(BF16)
                caches = [pltpu.make_async_copy(k_cache, k_out, out_sems.at[0]),
                          pltpu.make_async_copy(v_cache, v_out, out_sems.at[1])]
                for copy in caches:
                    copy.start()
            v_t = values[: 2 * PIECE].T.astype(BF16)
            attend(group, keys[: 2 * PIECE], v_t, q, slopes_ref, mask, dist, stat, acc, True)
        last = [pltpu.make_async_copy(q, q_out, out_sems.at[2]),
                pltpu.make_async_copy(stat, stat_out, out_sems.at[3]),
                pltpu.make_async_copy(acc, acc_out, out_sems.at[4])]
        for copy in last:
            copy.start()
        for copy in caches + last:
            copy.wait()

    return pl.pallas_call(
        body,
        out_shape=(
            jax.ShapeDtypeStruct((2 * width, block), BF16),
            jax.ShapeDtypeStruct((16, block), F32),
            jax.ShapeDtypeStruct((2 * width, block), F32),
            jax.ShapeDtypeStruct((block, width), BF16),
            jax.ShapeDtypeStruct((block, width), BF16),
        ),
        in_specs=[SMEM, SMEM, VMEM] + [ANY] * 6,
        out_specs=(ANY,) * 5,
        scratch_shapes=[
            pltpu.VMEM((block, depth), BF16),
            pltpu.VMEM((6, depth, width), BF16),
            pltpu.VMEM((2 * width, block), BF16),
            pltpu.VMEM((block, width), BF16),
            pltpu.VMEM((block, width), BF16),
            pltpu.VMEM((16, block), F32),
            pltpu.VMEM((2 * width, block), F32),
            pltpu.VMEM((2 * PIECE, block), F32),
            pltpu.VMEM((2 * PIECE, PIECE), F32),
            pltpu.SemaphoreType.DMA((10,)),
            pltpu.SemaphoreType.DMA((5,)),
        ],
        compiler_params=params(),
        cost_estimate=cost(5 * block * depth * width, 20 * 2**20, 8 * block * 2 * PIECE),
    )(info, slopes, lo, *pieces, w_own, w_pair)


def earlier_pieces(info, bases, slopes, lo, pieces, w_own, w_pair, q_t, stat_in, acc_in):
    depth, width = w_own.shape[1:]
    block = 4 * PIECE
    count = len(pieces)
    rows = count * PIECE

    def body(info_ref, bases_ref, slopes_ref, lo_ref, *refs):
        sources, refs = refs[:count], refs[count:]
        w0, w1, q_in, stat_src, acc_src, stat_out, acc_out, x, w, q, stat, acc, mask, dist, sems = refs
        live = bases_ref[0] + PIECE > info_ref[5]
        for i in range(1, count):
            live = live | (bases_ref[i] + PIECE > info_ref[5])

        keep = [pltpu.make_async_copy(stat_src, stat, sems.at[0]),
                pltpu.make_async_copy(acc_src, acc, sems.at[1])]
        for copy in keep:
            copy.start()

        @pl.when(live)
        def _():
            loads = [pltpu.make_async_copy(src, x.at[pl.ds(i * PIECE, PIECE)], sems.at[7 + i])
                     for i, src in enumerate(sources)]
            w_loads = [pltpu.make_async_copy(src.at[1 + part], w.at[2 * g + part], sems.at[3 + 2 * g + part])
                       for g, src in enumerate((w0, w1)) for part in range(2)]
            q_load = pltpu.make_async_copy(q_in, q, sems.at[2])
            for copy in loads + w_loads[:2] + [q_load] + w_loads[2:]:
                copy.start()
            set_masks(info_ref, lo_ref, lambda i: bases_ref[i], count, mask, dist)
            for copy in loads:
                copy.wait()
            for group in range(2):
                w_loads[2 * group].wait()
                keys = dot(x[...], w[2 * group]).astype(BF16)
                w_loads[2 * group + 1].wait()
                v_t = dot(x[...], w[2 * group + 1]).T.astype(BF16)
                if group == 0:
                    for copy in keep + [q_load]:
                        copy.wait()
                attend(group, keys, v_t, q, slopes_ref, mask, dist, stat, acc, False)

        @pl.when(jnp.logical_not(live))
        def _():
            for copy in keep:
                copy.wait()

        last = [pltpu.make_async_copy(stat, stat_out, sems.at[0]),
                pltpu.make_async_copy(acc, acc_out, sems.at[1])]
        for copy in last:
            copy.start()
        for copy in last:
            copy.wait()

    return pl.pallas_call(
        body,
        out_shape=(
            jax.ShapeDtypeStruct(stat_in.shape, F32),
            jax.ShapeDtypeStruct(acc_in.shape, F32),
        ),
        in_specs=[SMEM, SMEM, SMEM, VMEM] + [ANY] * (count + 5),
        out_specs=(ANY,) * 2,
        scratch_shapes=[
            pltpu.VMEM((rows, depth), BF16),
            pltpu.VMEM((4, depth, width), BF16),
            pltpu.VMEM((2 * width, block), BF16),
            pltpu.VMEM((16, block), F32),
            pltpu.VMEM((2 * width, block), F32),
            pltpu.VMEM((rows, block), F32),
            pltpu.VMEM((rows, PIECE), F32),
            pltpu.SemaphoreType.DMA((7 + count,)),
        ],
        compiler_params=params(),
        cost_estimate=cost(4 * rows * depth * width, 16 * 2**20, 8 * block * rows),
    )(info, bases, slopes, lo, *pieces, w_own, w_pair, q_t, stat_in, acc_in)


def close_half(stat, acc):
    wide, block = acc.shape
    half = block // 2

    def body(stat_ref, acc_ref, send_ref, lse_ref, out_ref):
        total = stat_ref[8:16, :]
        some = total > 0.0
        lse = jnp.where(some, stat_ref[0:8, :] + jnp.log2(jnp.where(some, total, 1.0)), NEG_FILL)
        scale = jnp.where(some, 1.0 / jnp.where(some, total, 1.0), 0.0)
        lse_ref[...] = lse[:, :half]
        for head in range(8):
            rows = pl.ds(head * HD, HD)
            normal = acc_ref[rows, :] * scale[head : head + 1, :]
            out_ref[rows, :] = normal[:, :half]
            send_ref[rows, :] = normal[:, half:].astype(BF16)
        rest = lse[:, half:]
        high = rest.astype(BF16)
        rest = rest - high.astype(F32)
        middle = rest.astype(BF16)
        low = (rest - middle.astype(F32)).astype(BF16)
        parts = [part.astype(F32) for part in (high, middle, low)]
        parts.append(jnp.zeros_like(parts[0]))
        send_ref[pl.ds(wide, 32), :] = jnp.concatenate(parts, axis=0).astype(BF16)

    return pl.pallas_call(
        body,
        out_shape=(
            jax.ShapeDtypeStruct((wide + 32, half), BF16),
            jax.ShapeDtypeStruct((8, half), F32),
            jax.ShapeDtypeStruct((wide, half), F32),
        ),
        in_specs=[VMEM] * 2,
        out_specs=(VMEM,) * 3,
        compiler_params=params(),
        cost_estimate=cost(0, 4 * 2**20, 0),
    )(stat, acc)


def project(place, lse, out, got, wo_own, wo_pair, tokens):
    wide = out.shape[0]
    width, model = wo_own.shape

    def body(lse_ref, out_ref, got_ref, w0, w1, *refs):
        tokens_ref, (y_ref, w, ctx, sems) = (refs[0], refs[1:]) if tokens is not None else (None, refs)
        loads = [pltpu.make_async_copy(src, w.at[pl.ds(i * width, width)], sems.at[i])
                 for i, src in enumerate((w0, w1))]
        for copy in loads:
            copy.start()
        lanes = pl.ds(place * PIECE, PIECE)
        other = got_ref[pl.ds(wide, 32), lanes].astype(F32)
        other = other[0:8] + other[8:16] + other[16:24]
        for head in range(8):
            swapped = (head + 4) % 8
            mine, theirs = lse_ref[head : head + 1, lanes], other[swapped : swapped + 1]
            top = jnp.maximum(mine, theirs)
            weigh, weigh_other = jnp.exp2(mine - top), jnp.exp2(theirs - top)
            joined = (out_ref[pl.ds(head * HD, HD), lanes] * weigh
                      + got_ref[pl.ds(swapped * HD, HD), lanes].astype(F32) * weigh_other)
            joined = joined / (weigh + weigh_other)
            ctx[:, head * HD : (head + 1) * HD] = joined.T.astype(BF16)
        for copy in loads:
            copy.wait()
        result = dot(ctx[...], w[...])
        if tokens is not None:
            result = result + tokens_ref[...].astype(F32)
        y_ref[...] = result.astype(y_ref.dtype)

    extra = () if tokens is None else (tokens,)
    return pl.pallas_call(
        body,
        out_shape=jax.ShapeDtypeStruct((PIECE, model), BF16 if tokens is None else F32),
        in_specs=[VMEM] * 3 + [ANY] * 2 + [VMEM] * len(extra),
        out_specs=VMEM,
        scratch_shapes=[
            pltpu.VMEM((2 * width, model), BF16),
            pltpu.VMEM((PIECE, wide), BF16),
            pltpu.SemaphoreType.DMA((2,)),
        ],
        compiler_params=params(),
        cost_estimate=cost(PIECE * wide * model, 6 * 2**20, 0),
    )(lse, out, got, wo_own, wo_pair, *extra)


def on_device(tokens, ln_gain, w_qkv, slopes, w_out, seg_ids):
    blocks = lax.axis_size("seq")
    block_num = lax.axis_index("seq")
    head_num = lax.axis_index("head")
    block = seg_ids.shape[0]
    odd = (block_num % 2) == 1

    def over_core(value):
        return lax.ppermute(value, "head", [(i, i ^ 1) for i in range(4)])

    def over_x(value):
        return lax.ppermute(value, "head", [(i, i ^ 2) for i in range(4)])

    def over_seq(value, pairs):
        return lax.ppermute(value, "seq", pairs)

    two_on = [(i, i + 2) for i in range(blocks - 2)]
    even_to_odd = [(i, i + 1) for i in range(0, blocks, 2)]
    odd_to_even = [(i + 1, i) for i in range(0, blocks, 2)]

    w_own = jnp.transpose(w_qkv, (1, 0, 2))

    base = block_num * block
    all_seg = lax.all_gather(seg_ids, "seq", axis=0, tiled=True)
    all_slopes = lax.all_gather(slopes, "head", axis=0, tiled=True)
    first_seg = seg_ids[0]
    start = jnp.sum((all_seg < first_seg).astype(jnp.int32))
    inside = base + jnp.sum((seg_ids[None, :] < seg_ids[:, None]).astype(jnp.int32), axis=1)
    lo = jnp.where(seg_ids == first_seg, start, inside).reshape(4, PIECE)
    heads = [head_num, head_num ^ 2, head_num ^ 1, head_num ^ 3]
    info = jnp.stack([base] + heads + [start]).astype(jnp.int32)
    slopes_pair = jnp.concatenate([
        slopes, lax.dynamic_slice_in_dim(all_slopes, (head_num ^ 1) * 4, 4)])

    def key_base(steps, place):
        return (block_num - steps) * block + heads[place] * PIECE

    def bases(*which):
        return jnp.stack([key_base(*w) for w in which]).astype(jnp.int32)

    a0 = layer_norm(tokens, ln_gain)
    a2 = over_seq(a0, two_on)
    b0 = over_x(a0)
    a1_odd = over_seq(a0, even_to_odd)
    c0 = over_core(a0)
    w_tied, wo_tied, _ = lax.optimization_barrier((w_own, w_out, a0))
    w_pair = over_core(w_tied)
    wo_pair = over_core(wo_tied)
    d0 = over_core(b0)

    a4 = over_seq(a2, two_on)
    b2 = over_x(a2)
    crossed = over_seq(a2, even_to_odd + odd_to_even)
    a1 = jnp.where(odd, a1_odd, crossed)

    b1 = over_x(a1)
    b4 = over_seq(b2, two_on)
    a3_even = over_seq(a4, odd_to_even)
    a3 = jnp.where(odd, crossed, a3_even)
    b3 = over_x(a3)

    q_t, stat, acc, key_cache, value_cache = own_block(
        info, slopes_pair, lo, (a0, b0, c0, d0), w_own, w_pair)
    for pieces, which in (
        ((a2, b2, a1, a4), ((2, 0), (2, 1), (1, 0), (4, 0))),
        ((b1, b4, a3), ((1, 1), (4, 1), (3, 0))),
        ((b3,), ((3, 1),)),
    ):
        stat, acc = earlier_pieces(
            info, bases(*which), slopes_pair, lo, pieces, w_own, w_pair, q_t, stat, acc)
    send, lse, out = close_half(stat, acc)
    got = over_core(send)
    y_pair = project(1, lse, out, got, w_out, wo_pair, None)
    y_got = over_x(y_pair)
    y_own = project(0, lse, out, got, w_out, wo_pair, tokens)
    hidden = (y_own + y_got.astype(F32)).astype(BF16)
    return (hidden, key_cache, value_cache)


def solution(mesh):
    in_specs = (
        P(("seq", "head"), None),
        P(),
        P(None, None, "head"),
        P("head"),
        P("head", None),
        P("seq"),
    )
    out_specs = (P(("seq", "head"), None), P("seq", "head"), P("seq", "head"))
    return jax.shard_map(
        on_device, mesh=mesh, in_specs=in_specs, out_specs=out_specs, check_vma=False
    )
```

```python
import jax
import jax.numpy as jnp
from jax import lax
from jax.experimental import pallas as pl
from jax.experimental.pallas import tpu as pltpu
from jax.sharding import PartitionSpec as P

HD = 128
SPAN = 4
PIECE = 128
EPSILON = 1e-05
NEG_FILL = -1e30
MASKED = -2e38
LOG2E = 1.4426950408889634

BF16 = jnp.bfloat16
F32 = jnp.float32
SMEM = pl.BlockSpec(memory_space=pltpu.SMEM)
VMEM = pl.BlockSpec(memory_space=pltpu.VMEM)


def params(mebibytes):
    return pltpu.CompilerParams(vmem_limit_bytes=mebibytes * 2**20)


def cost(macs, nbytes, exps=0):
    return pl.CostEstimate(flops=2 * macs, bytes_accessed=nbytes, transcendentals=exps)


def dot(lhs, rhs):
    return jnp.dot(lhs, rhs, preferred_element_type=F32)


def layer_norm(tokens, ln_gain):
    def body(tokens_ref, gain_ref, out_ref):
        inputs = tokens_ref[...].astype(F32)
        centred = inputs - jnp.mean(inputs, axis=-1, keepdims=True)
        variance = jnp.mean(centred * centred, axis=-1, keepdims=True)
        out_ref[...] = (centred * lax.rsqrt(variance + EPSILON) * gain_ref[...]).astype(BF16)

    return pl.pallas_call(
        body,
        out_shape=jax.ShapeDtypeStruct(tokens.shape, BF16),
        in_specs=[VMEM, VMEM],
        out_specs=VMEM,
        compiler_params=params(8),
        cost_estimate=cost(0, 2 * tokens.size * 2, tokens.size),
    )(tokens, ln_gain.reshape(1, -1))


def place_of(place):
    return lax.axis_index("head") ^ (0, 2, 1, 3)[place]


def set_distance(block_base, key_base, keys, dist_ref):
    row = lax.broadcasted_iota(jnp.int32, (PIECE, PIECE), 0)
    for piece in range(keys):
        dist_ref[pl.ds(piece * PIECE, PIECE), :] = (row + (key_base(piece) - block_base)).astype(F32)


def set_own_masks(seg_ref, mask_ref, dist_ref):
    lane = lax.broadcasted_iota(jnp.int32, (1, PIECE), 1)
    row = lax.broadcasted_iota(jnp.int32, (PIECE, PIECE), 0)
    set_distance(0, lambda i: place_of(i) * PIECE, 2, dist_ref)
    for piece in range(2):
        rows = pl.ds(piece * PIECE, PIECE)
        k_pos = row + place_of(piece) * PIECE
        key_seg = seg_ref[pl.ds(place_of(piece), 1), :]
        key_seg = jnp.broadcast_to(key_seg, (PIECE, PIECE)).T
        for place in range(4):
            q_pos = lane + place_of(place) * PIECE
            kept = (key_seg == seg_ref[pl.ds(place_of(place), 1), :]) & (k_pos <= q_pos)
            mask_ref[rows, pl.ds(place * PIECE, PIECE)] = jnp.where(kept, 0.0, MASKED)


def set_earlier_masks(seg_ref, start, block_base, key_base, keys, mask_ref, dist_ref):
    row = lax.broadcasted_iota(jnp.int32, (PIECE, PIECE), 0)
    set_distance(block_base, key_base, keys, dist_ref)
    first_seg = seg_ref[0:1, 0:1]
    for piece in range(keys):
        rows = pl.ds(piece * PIECE, PIECE)
        late = row + key_base(piece) >= start
        for place in range(4):
            kept = late & (seg_ref[pl.ds(place_of(place), 1), :] == first_seg)
            mask_ref[rows, pl.ds(place * PIECE, PIECE)] = jnp.where(kept, 0.0, MASKED)


def attend(group, k_rows, v_t, q_ref, slopes_ref, mask_ref, dist_ref, before, stat_ref, acc_ref):
    heads = k_rows.shape[1] // HD
    for local in range(heads):
        head = group * heads + local
        cols = slice(local * HD, (local + 1) * HD)
        wide = pl.ds(head * HD, HD)
        bias = dist_ref[...] * (slopes_ref[local] * LOG2E)
        bias = jnp.concatenate([bias] * (q_ref.shape[1] // PIECE), axis=1)
        scores = dot(k_rows[:, cols], q_ref[wide, :]) * (HD**-0.5 * LOG2E)
        scores = scores + bias + mask_ref[...]
        top = jnp.max(scores, axis=0, keepdims=True)
        prev = jnp.full_like(top, NEG_FILL) if before is None else before[0][head : head + 1, :]
        row_max = jnp.maximum(prev, top)
        expo = jnp.exp2(scores - row_max)
        total = jnp.sum(expo, axis=0, keepdims=True)
        update = dot(v_t[cols, :], expo.astype(BF16))
        if before is not None:
            rescale = jnp.exp2(prev - row_max)
            total = before[0][8 + head : 9 + head, :] * rescale + total
            update = before[1][wide, :] * rescale + update
        stat_ref[head : head + 1, :] = row_max
        stat_ref[8 + head : 9 + head, :] = total
        acc_ref[wide, :] = update


def own_block(slopes, slopes_pair, seg, pieces, w_own, w_pair):
    depth, width = w_own.shape[1:]
    block = 4 * PIECE

    def body(s0, s1, seg_ref, a, b, c, d, w0, w1, q, stat, acc, k_cache, v_cache, mask, dist):
        set_own_masks(seg_ref, mask, dist)
        x = jnp.concatenate([a[...], b[...], c[...], d[...]], axis=0)
        for group, w in enumerate((w0, w1)):
            rows = block if group == 0 else 2 * PIECE
            q[pl.ds(group * width, width), :] = dot(x, w[0]).T.astype(BF16)
            keys = dot(x[:rows], w[1]).astype(BF16)
            values = dot(x[:rows], w[2])
            if group == 0:
                for place in range(4):
                    to = pl.ds(pl.multiple_of(place_of(place) * PIECE, PIECE), PIECE)
                    k_cache[to, :] = keys[place * PIECE : (place + 1) * PIECE]
                    v_cache[to, :] = values[place * PIECE : (place + 1) * PIECE].astype(BF16)
            v_t = values[: 2 * PIECE].T.astype(BF16)
            attend(group, keys[: 2 * PIECE], v_t, q, (s0, s1)[group], mask, dist, None, stat, acc)

    return pl.pallas_call(
        body,
        out_shape=(
            jax.ShapeDtypeStruct((2 * width, block), BF16),
            jax.ShapeDtypeStruct((16, block), F32),
            jax.ShapeDtypeStruct((2 * width, block), F32),
            jax.ShapeDtypeStruct((block, width), BF16),
            jax.ShapeDtypeStruct((block, width), BF16),
        ),
        in_specs=[SMEM, SMEM] + [VMEM] * 7,
        out_specs=(VMEM,) * 5,
        scratch_shapes=[
            pltpu.VMEM((2 * PIECE, block), F32),
            pltpu.VMEM((2 * PIECE, PIECE), F32),
        ],
        compiler_params=params(26),
        cost_estimate=cost(5 * block * depth * width, 2**20, 0),
    )(slopes, slopes_pair, seg, *pieces, w_own, w_pair)


def write_closed(stat, acc, send_ref, lse_ref, out_ref):
    wide, block = acc.shape
    half = block // 2
    total = stat[8:16, :]
    some = total > 0.0
    lse = jnp.where(some, stat[0:8, :] + jnp.log2(jnp.where(some, total, 1.0)), NEG_FILL)
    scale = jnp.where(some, 1.0 / jnp.where(some, total, 1.0), 0.0)
    lse_ref[...] = lse[:, :half]
    for head in range(8):
        rows = pl.ds(head * HD, HD)
        normal = acc[rows, :] * scale[head : head + 1, :]
        out_ref[rows, :] = normal[:, :half]
        send_ref[rows, :] = normal[:, half:].astype(BF16)
    rest = lse[:, half:]
    high = rest.astype(BF16)
    rest = rest - high.astype(F32)
    middle = rest.astype(BF16)
    low = (rest - middle.astype(F32)).astype(BF16)
    parts = [part.astype(F32) for part in (high, middle, low)]
    parts.append(jnp.zeros_like(parts[0]))
    send_ref[pl.ds(wide, 32), :] = jnp.concatenate(parts, axis=0).astype(BF16)


def earlier_pieces(which, closing, slopes, slopes_pair, seg, segs, pieces, w_own, w_pair, q_t, stat_in, acc_in):
    depth, width = w_own.shape[1:]
    block = 4 * PIECE
    count = len(pieces)
    rows = count * PIECE
    n_out = 3 if closing else 2

    def body(s0, s1, seg_ref, *refs):
        seg_refs, refs = refs[: len(segs)], refs[len(segs) :]
        sources, refs = refs[:count], refs[count:]
        (w0, w1, q, stat_src, acc_src), refs = refs[:5], refs[5:]
        outs, scratch = refs[:n_out], refs[n_out:]
        mask, dist = scratch[:2]
        stat, acc = scratch[2:] if closing else outs
        block_num = lax.axis_index("seq")
        block_base = block_num * block
        same = jnp.zeros(seg_ref.shape, jnp.int32)
        for back, ref in enumerate(seg_refs, 1):
            same = same + jnp.where((ref[...] == seg_ref[0:1, 0:1]) & (block_num >= back), 1, 0)
        start = block_base - jnp.sum(same)

        def key_base(i):
            back, place = which[i]
            return block_base - back * block + place_of(place) * PIECE

        live = key_base(0) + PIECE > start
        for i in range(1, count):
            live = live | (key_base(i) + PIECE > start)

        @pl.when(live)
        def _():
            set_earlier_masks(seg_ref, start, block_base, key_base, count, mask, dist)
            x = jnp.concatenate([source[...] for source in sources], axis=0)
            for group, w in enumerate((w0, w1)):
                keys = dot(x, w[1]).astype(BF16)
                v_t = dot(x, w[2]).T.astype(BF16)
                attend(group, keys, v_t, q, (s0, s1)[group], mask, dist, (stat_src, acc_src), stat, acc)

        @pl.when(jnp.logical_not(live))
        def _():
            stat[...] = stat_src[...]
            acc[...] = acc_src[...]

        if closing:
            write_closed(stat, acc, *outs)

    scratch = [pltpu.VMEM((rows, block), F32), pltpu.VMEM((rows, PIECE), F32)]
    if closing:
        scratch += [pltpu.VMEM(stat_in.shape, F32), pltpu.VMEM(acc_in.shape, F32)]
        out_shape = (
            jax.ShapeDtypeStruct((2 * width + 32, block // 2), BF16),
            jax.ShapeDtypeStruct((8, block // 2), F32),
            jax.ShapeDtypeStruct((2 * width, block // 2), F32),
        )
    else:
        out_shape = (
            jax.ShapeDtypeStruct(stat_in.shape, F32),
            jax.ShapeDtypeStruct(acc_in.shape, F32),
        )
    return pl.pallas_call(
        body,
        out_shape=out_shape,
        in_specs=[SMEM, SMEM] + [VMEM] * (6 + len(segs) + count),
        out_specs=(VMEM,) * n_out,
        scratch_shapes=scratch,
        compiler_params=params(26),
        cost_estimate=cost(4 * rows * depth * width, 2**20, 0),
    )(slopes, slopes_pair, seg, *segs, *pieces, w_own, w_pair, q_t, stat_in, acc_in)


def project(place, lse, out, got, wo_own, wo_pair, tokens):
    wide = out.shape[0]
    width, model = wo_own.shape

    def body(lse_ref, out_ref, got_ref, w0, w1, *refs):
        y_ref, ctx = refs[-2:]
        lanes = pl.ds(place * PIECE, PIECE)
        other = got_ref[pl.ds(wide, 32), lanes].astype(F32)
        other = other[0:8] + other[8:16] + other[16:24]
        for head in range(8):
            swapped = (head + 4) % 8
            mine, theirs = lse_ref[head : head + 1, lanes], other[swapped : swapped + 1]
            top = jnp.maximum(mine, theirs)
            weigh, weigh_other = jnp.exp2(mine - top), jnp.exp2(theirs - top)
            joined = (out_ref[pl.ds(head * HD, HD), lanes] * weigh
                      + got_ref[pl.ds(swapped * HD, HD), lanes].astype(F32) * weigh_other)
            joined = joined / (weigh + weigh_other)
            ctx[:, head * HD : (head + 1) * HD] = joined.T.astype(BF16)
        result = dot(ctx[:, :width], w0[...]) + dot(ctx[:, width:], w1[...])
        if tokens is not None:
            result = result + refs[0][...].astype(F32)
        y_ref[...] = result.astype(y_ref.dtype)

    extra = () if tokens is None else (tokens,)
    return pl.pallas_call(
        body,
        out_shape=jax.ShapeDtypeStruct((PIECE, model), BF16 if tokens is None else F32),
        in_specs=[VMEM] * (5 + len(extra)),
        out_specs=VMEM,
        scratch_shapes=[pltpu.VMEM((PIECE, wide), BF16)],
        compiler_params=params(16),
        cost_estimate=cost(PIECE * wide * model, 2**20, 0),
    )(lse, out, got, wo_own, wo_pair, *extra)


def on_device(tokens, ln_gain, w_qkv, slopes, w_out, seg_ids):
    blocks = lax.axis_size("seq")
    block_num = lax.axis_index("seq")
    odd = (block_num % 2) == 1

    def over_core(value):
        return lax.ppermute(value, "head", [(i, i ^ 1) for i in range(4)])

    def over_x(value):
        return lax.ppermute(value, "head", [(i, i ^ 2) for i in range(4)])

    def over_seq(value, pairs):
        return lax.ppermute(value, "seq", pairs)

    two_on = [(i, i + 2) for i in range(blocks - 2)]
    even_to_odd = [(i, i + 1) for i in range(0, blocks, 2)]
    odd_to_even = [(i + 1, i) for i in range(0, blocks, 2)]

    w_own = jnp.transpose(w_qkv, (1, 0, 2))
    w_pair = over_core(w_own)
    a0 = layer_norm(tokens, ln_gain)
    a2 = over_seq(a0, two_on)
    b0 = over_x(a0)
    a1_odd = over_seq(a0, even_to_odd)
    c0 = over_core(a0)
    wo_tied, slopes_tied, seg, _ = lax.optimization_barrier(
        (w_out, slopes, seg_ids.reshape(4, PIECE), c0))
    slopes_pair = over_core(slopes_tied)
    segs = [over_seq(seg, [(i, i + back) for i in range(blocks - back)]) for back in range(1, SPAN + 1)]
    wo_pair = over_core(wo_tied)
    d0 = over_core(b0)

    a4 = over_seq(a2, two_on)
    b2 = over_x(a2)
    crossed = over_seq(a2, even_to_odd + odd_to_even)
    a1 = jnp.where(odd, a1_odd, crossed)

    def merge(closing, pieces, which, state):
        return earlier_pieces(
            which, closing, slopes, slopes_pair, seg, segs, pieces, w_own, w_pair, q_t, *state)

    q_t, stat, acc, key_cache, value_cache = own_block(
        slopes, slopes_pair, seg, (a0, b0, c0, d0), w_own, w_pair)
    a1, b2, a4, stat = lax.optimization_barrier((a1, b2, a4, stat))
    b1 = over_x(a1)
    b4 = over_seq(b2, two_on)
    a3_even = over_seq(a4, odd_to_even)
    a3 = jnp.where(odd, crossed, a3_even)
    state = merge(False, (a2, b2, a1, a4), ((2, 0), (2, 1), (1, 0), (4, 0)), (stat, acc))
    a3, tied = lax.optimization_barrier((a3, state[0]))
    b3 = over_x(a3)
    state = (tied, state[1])
    state = merge(False, (b1, b4, a3), ((1, 1), (4, 1), (3, 0)), state)
    state = merge(True, (b3,), ((3, 1),), state)
    send, lse, out = state
    got = over_core(send)
    y_pair = project(1, lse, out, got, w_out, wo_pair, None)
    y_got = over_x(y_pair)
    y_own = project(0, lse, out, got, w_out, wo_pair, tokens)
    hidden = (y_own + y_got.astype(F32)).astype(BF16)
    return (hidden, key_cache, value_cache)


def solution(mesh):
    in_specs = (
        P(("seq", "head"), None),
        P(),
        P(None, None, "head"),
        P("head"),
        P("head", None),
        P("seq"),
    )
    out_specs = (P(("seq", "head"), None), P("seq", "head"), P("seq", "head"))
    return jax.shard_map(
        on_device, mesh=mesh, in_specs=in_specs, out_specs=out_specs, check_vma=False
    )
```

```python
import jax
import jax.numpy as jnp
from jax import lax
from jax.experimental import pallas as pl
from jax.experimental.pallas import tpu as pltpu
from jax.sharding import PartitionSpec as P

HD = 128
SPAN = 4
PIECE = 128
EPSILON = 1e-05
NEG_FILL = -1e30
MASKED = -2e38
LOG2E = 1.4426950408889634

BF16 = jnp.bfloat16
F32 = jnp.float32
SMEM = pl.BlockSpec(memory_space=pltpu.SMEM)
ANY = pl.BlockSpec(memory_space=pl.ANY)
VMEM = pl.BlockSpec(memory_space=pltpu.VMEM)


def params(mebibytes):
    return pltpu.CompilerParams(vmem_limit_bytes=mebibytes * 2**20)


def cost(macs, nbytes, exps=0):
    return pl.CostEstimate(flops=2 * macs, bytes_accessed=nbytes, transcendentals=exps)


def dot(lhs, rhs):
    return jnp.dot(lhs, rhs, preferred_element_type=F32)


def three_addends(value):
    high = value.astype(BF16).astype(F32)
    middle = (value - high).astype(BF16).astype(F32)
    return high, middle, value - high - middle


def layer_norm(tokens, ln_gain, slopes):
    rows, model = tokens.shape

    def body(slopes_ref, tokens_ref, gain_ref, out_ref, long_ref):
        inputs = tokens_ref[...].astype(F32)
        centred = inputs - jnp.mean(inputs, axis=-1, keepdims=True)
        variance = jnp.mean(centred * centred, axis=-1, keepdims=True)
        normed = (centred * lax.rsqrt(variance + EPSILON) * gain_ref[...]).astype(BF16)
        out_ref[...] = normed
        long_ref[:rows, :] = normed
        row = lax.broadcasted_iota(jnp.int32, (16, model), 0)
        spread = jnp.zeros((16, model), F32)
        for head in range(4):
            spread = jnp.where(row % 4 == head, slopes_ref[head], spread)
        high, middle, low = three_addends(spread)
        part = jnp.where(row < 4, high, jnp.where(row < 8, middle, jnp.where(row < 12, low, 0.0)))
        long_ref[pl.ds(rows, 16), :] = part.astype(BF16)

    return pl.pallas_call(
        body,
        out_shape=(
            jax.ShapeDtypeStruct((rows, model), BF16),
            jax.ShapeDtypeStruct((rows + 16, model), BF16),
        ),
        in_specs=[SMEM, VMEM, VMEM],
        out_specs=(VMEM, VMEM),
        compiler_params=params(8),
        cost_estimate=cost(0, 2 * tokens.size * 2, tokens.size),
    )(slopes, tokens, ln_gain.reshape(1, -1))


def stage(weights):
    def body(source, out_ref, sem):
        copy = pltpu.make_async_copy(source, out_ref, sem)
        copy.start()
        copy.wait()

    return pl.pallas_call(
        body,
        out_shape=jax.ShapeDtypeStruct(weights.shape, weights.dtype),
        in_specs=[ANY],
        out_specs=VMEM,
        scratch_shapes=[pltpu.SemaphoreType.DMA],
        compiler_params=params(10),
        cost_estimate=cost(0, 2 * weights.size * 2),
    )(weights)


def place_of(place):
    return lax.axis_index("head") ^ (0, 2, 1, 3)[place]


def set_distance(block_base, key_base, keys, dist_ref):
    row = lax.broadcasted_iota(jnp.int32, (PIECE, PIECE), 0)
    for piece in range(keys):
        dist_ref[pl.ds(piece * PIECE, PIECE), :] = (row + (key_base(piece) - block_base)).astype(F32)


def set_own_masks(seg_ref, mask_ref, dist_ref):
    lane = lax.broadcasted_iota(jnp.int32, (1, PIECE), 1)
    row = lax.broadcasted_iota(jnp.int32, (PIECE, PIECE), 0)
    set_distance(0, lambda i: place_of(i) * PIECE, 2, dist_ref)
    for piece in range(2):
        rows = pl.ds(piece * PIECE, PIECE)
        k_pos = row + place_of(piece) * PIECE
        key_seg = seg_ref[pl.ds(place_of(piece), 1), :]
        key_seg = jnp.broadcast_to(key_seg, (PIECE, PIECE)).T
        for place in range(4):
            q_pos = lane + place_of(place) * PIECE
            kept = (key_seg == seg_ref[pl.ds(place_of(place), 1), :]) & (k_pos <= q_pos)
            mask_ref[rows, pl.ds(place * PIECE, PIECE)] = jnp.where(kept, 0.0, MASKED)


def set_earlier_masks(seg_ref, start, block_base, key_base, keys, mask_ref, dist_ref):
    row = lax.broadcasted_iota(jnp.int32, (PIECE, PIECE), 0)
    set_distance(block_base, key_base, keys, dist_ref)
    first_seg = seg_ref[0:1, 0:1]
    for piece in range(keys):
        rows = pl.ds(piece * PIECE, PIECE)
        late = row + key_base(piece) >= start
        for place in range(4):
            kept = late & (seg_ref[pl.ds(place_of(place), 1), :] == first_seg)
            mask_ref[rows, pl.ds(place * PIECE, PIECE)] = jnp.where(kept, 0.0, MASKED)


def attend(group, k_rows, v_t, q_ref, slopes_ref, mask_ref, dist_ref, before, stat_ref, acc_ref):
    heads = k_rows.shape[1] // HD
    for head in range(heads):
        cols = slice(head * HD, (head + 1) * HD)
        wide = pl.ds(head * HD, HD)
        place = heads * group + head
        bias = dist_ref[...] * (slopes_ref[place : place + 1, :] * LOG2E)
        bias = jnp.concatenate([bias] * (q_ref.shape[1] // PIECE), axis=1)
        scores = dot(k_rows[:, cols], q_ref[wide, :]) * (HD**-0.5 * LOG2E)
        scores = scores + bias + mask_ref[...]
        top = jnp.max(scores, axis=0, keepdims=True)
        prev = jnp.full_like(top, NEG_FILL) if before is None else before[0][head : head + 1, :]
        row_max = jnp.maximum(prev, top)
        expo = jnp.exp2(scores - row_max)
        total = jnp.sum(expo, axis=0, keepdims=True)
        update = dot(v_t[cols, :], expo.astype(BF16))
        if before is not None:
            rescale = jnp.exp2(prev - row_max)
            total = before[0][4 + head : 5 + head, :] * rescale + total
            update = before[1][wide, :] * rescale + update
        stat_ref[head : head + 1, :] = row_max
        stat_ref[4 + head : 5 + head, :] = total
        acc_ref[wide, :] = update


def state_shapes(width, block):
    return (jax.ShapeDtypeStruct((8, block), F32), jax.ShapeDtypeStruct((width, block), F32))


def load_weights(own, sources, held, sems):
    copies = [pltpu.make_async_copy(source, held.at[i], sems.at[i]) for i, source in enumerate(sources)]
    for copy in copies:
        copy.start()

    def ready(i):
        if i < len(copies):
            return own[i]
        copies[i - len(copies)].wait()
        return held[i - len(copies)]

    return ready


def own_block(slopes, seg, pieces, w_own, w_pair):
    depth, width = w_own.shape[1:]
    block = 4 * PIECE

    def body(s0, seg_ref, a, b, c, d, w0, w1, q0, q1, stat0, acc0, stat1, acc1, k_cache, v_cache, slopes_out,
             held, mask, dist, sems):
        ready = load_weights(w0, [w1.at[part] for part in range(3)], held, sems)
        set_own_masks(seg_ref, mask, dist)
        tail = c[PIECE : PIECE + 16, :PIECE].astype(F32)
        for head in range(4):
            slopes_out[head : head + 1, :] = jnp.full((1, PIECE), s0[head], F32)
        slopes_out[4:8, :] = tail[0:4] + tail[4:8] + tail[8:12]
        x = jnp.concatenate([a[...], b[...], c[:PIECE, :], d[...]], axis=0)
        for group, (q, stat, acc) in enumerate(((q0, stat0, acc0), (q1, stat1, acc1))):
            rows = block if group == 0 else 2 * PIECE
            q[...] = dot(x, ready(3 * group)).T.astype(BF16)
            keys = dot(x[:rows], ready(3 * group + 1)).astype(BF16)
            values = dot(x[:rows], ready(3 * group + 2))
            if group == 0:
                for place in range(4):
                    to = pl.ds(pl.multiple_of(place_of(place) * PIECE, PIECE), PIECE)
                    k_cache[to, :] = keys[place * PIECE : (place + 1) * PIECE]
                    v_cache[to, :] = values[place * PIECE : (place + 1) * PIECE].astype(BF16)
            v_t = values[: 2 * PIECE].T.astype(BF16)
            attend(group, keys[: 2 * PIECE], v_t, q, slopes_out, mask, dist, None, stat, acc)

    return pl.pallas_call(
        body,
        out_shape=(jax.ShapeDtypeStruct((width, block), BF16),) * 2 + state_shapes(width, block) * 2 + (
            jax.ShapeDtypeStruct((block, width), BF16),
            jax.ShapeDtypeStruct((block, width), BF16),
            jax.ShapeDtypeStruct((8, PIECE), F32),
        ),
        in_specs=[SMEM] + [VMEM] * 6 + [ANY],
        out_specs=(VMEM,) * 9,
        scratch_shapes=[
            pltpu.VMEM((3, depth, width), BF16),
            pltpu.VMEM((2 * PIECE, block), F32),
            pltpu.VMEM((2 * PIECE, PIECE), F32),
            pltpu.SemaphoreType.DMA((3,)),
        ],
        compiler_params=params(26),
        cost_estimate=cost(5 * block * depth * width, 2**20, 0),
    )(slopes, seg, *pieces, w_own, w_pair)


def write_closed(states, send_ref, lse_ref, out_ref):
    width, block = states[0][1].shape
    half = block // 2
    sent = []
    for group, (stat, acc) in enumerate(states):
        total = stat[4:8, :]
        some = total > 0.0
        lse = jnp.where(some, stat[0:4, :] + jnp.log2(jnp.where(some, total, 1.0)), NEG_FILL)
        scale = jnp.where(some, 1.0 / jnp.where(some, total, 1.0), 0.0)
        lse_ref[4 * group : 4 * group + 4, :] = lse[:, :half]
        sent.append(lse[:, half:])
        for head in range(4):
            rows = pl.ds(head * HD, HD)
            to = pl.ds(group * width + head * HD, HD)
            normal = acc[rows, :] * scale[head : head + 1, :]
            out_ref[to, :] = normal[:, :half]
            send_ref[to, :] = normal[:, half:].astype(BF16)
    parts = list(three_addends(jnp.concatenate(sent, axis=0)))
    parts.append(jnp.zeros_like(parts[0]))
    send_ref[pl.ds(2 * width, 32), :] = jnp.concatenate(parts, axis=0).astype(BF16)


def earlier_pieces(which, closing, slopes8, seg, segs, pieces, w_own, w_pair, q_own, q_pair, state):
    depth, width = w_own.shape[1:]
    block = 4 * PIECE
    count = len(pieces)
    rows = count * PIECE
    n_out = 3 if closing else 4

    def body(slopes_ref, seg_ref, *refs):
        seg_refs, refs = refs[: len(segs)], refs[len(segs) :]
        sources, refs = refs[:count], refs[count:]
        (w0, w1, q0, q1), before, refs = refs[:4], (refs[4:6], refs[6:8]), refs[8:]
        outs, (mask, dist, held, sems, *inner) = refs[:n_out], refs[n_out:]
        after = inner if closing else outs
        after = (after[0:2], after[2:4])
        block_num = lax.axis_index("seq")
        block_base = block_num * block
        same = jnp.zeros(seg_ref.shape, jnp.int32)
        for back, ref in enumerate(seg_refs, 1):
            same = same + jnp.where((ref[...] == seg_ref[0:1, 0:1]) & (block_num >= back), 1, 0)
        start = block_base - jnp.sum(same)

        def key_base(i):
            back, place = which[i]
            return block_base - back * block + place_of(place) * PIECE

        live = key_base(0) + PIECE > start
        for i in range(1, count):
            live = live | (key_base(i) + PIECE > start)

        @pl.when(live)
        def _():
            ready = load_weights(w0.at[1:3], [w1.at[part] for part in (1, 2)], held, sems)
            set_earlier_masks(seg_ref, start, block_base, key_base, count, mask, dist)
            x = jnp.concatenate([source[...] for source in sources], axis=0)
            for group, q in enumerate((q0, q1)):
                keys = dot(x, ready(2 * group)).astype(BF16)
                v_t = dot(x, ready(2 * group + 1)).T.astype(BF16)
                attend(group, keys, v_t, q, slopes_ref, mask, dist, before[group], *after[group])

        @pl.when(jnp.logical_not(live))
        def _():
            for old, new in zip(before, after):
                new[0][...] = old[0][...]
                new[1][...] = old[1][...]

        if closing:
            write_closed(after, *outs)

    shapes = state_shapes(width, block) * 2
    scratch = [
        pltpu.VMEM((rows, block), F32),
        pltpu.VMEM((rows, PIECE), F32),
        pltpu.VMEM((2, depth, width), BF16),
        pltpu.SemaphoreType.DMA((2,)),
    ]
    if closing:
        scratch += [pltpu.VMEM(shape.shape, F32) for shape in shapes]
        shapes = (
            jax.ShapeDtypeStruct((2 * width + 32, block // 2), BF16),
            jax.ShapeDtypeStruct((8, block // 2), F32),
            jax.ShapeDtypeStruct((2 * width, block // 2), F32),
        )
    return pl.pallas_call(
        body,
        out_shape=shapes,
        in_specs=[VMEM] * (3 + len(segs) + count) + [ANY] + [VMEM] * 6,
        out_specs=(VMEM,) * n_out,
        scratch_shapes=scratch,
        compiler_params=params(24),
        cost_estimate=cost(4 * rows * depth * width, 2**20, 0),
    )(slopes8, seg, *segs, *pieces, w_own, w_pair, q_own, q_pair, *state)


def project(place, lse, out, got, wo_own, wo_pair, tokens):
    wide = out.shape[0]
    width, model = wo_own.shape

    def body(lse_ref, out_ref, got_ref, w0, w1, *refs):
        y_ref, ctx = refs[-2:]
        lanes = pl.ds(place * PIECE, PIECE)
        other = got_ref[pl.ds(wide, 32), lanes].astype(F32)
        other = other[0:8] + other[8:16] + other[16:24]
        for head in range(8):
            swapped = (head + 4) % 8
            mine, theirs = lse_ref[head : head + 1, lanes], other[swapped : swapped + 1]
            top = jnp.maximum(mine, theirs)
            weigh, weigh_other = jnp.exp2(mine - top), jnp.exp2(theirs - top)
            joined = (out_ref[pl.ds(head * HD, HD), lanes] * weigh
                      + got_ref[pl.ds(swapped * HD, HD), lanes].astype(F32) * weigh_other)
            joined = joined / (weigh + weigh_other)
            ctx[:, head * HD : (head + 1) * HD] = joined.T.astype(BF16)
        result = dot(ctx[:, :width], w0[...]) + dot(ctx[:, width:], w1[...])
        if tokens is not None:
            result = result + refs[0][...].astype(F32)
        y_ref[...] = result.astype(y_ref.dtype)

    extra = () if tokens is None else (tokens,)
    return pl.pallas_call(
        body,
        out_shape=jax.ShapeDtypeStruct((PIECE, model), BF16 if tokens is None else F32),
        in_specs=[VMEM] * (5 + len(extra)),
        out_specs=VMEM,
        scratch_shapes=[pltpu.VMEM((PIECE, wide), BF16)],
        compiler_params=params(16),
        cost_estimate=cost(PIECE * wide * model, 2**20, 0),
    )(lse, out, got, wo_own, wo_pair, *extra)


def on_device(tokens, ln_gain, w_qkv, slopes, w_out, seg_ids):
    blocks = lax.axis_size("seq")
    block_num = lax.axis_index("seq")
    odd = (block_num % 2) == 1

    def over_core(value):
        return lax.ppermute(value, "head", [(i, i ^ 1) for i in range(4)])

    def over_x(value):
        return lax.ppermute(value, "head", [(i, i ^ 2) for i in range(4)])

    def over_seq(value, pairs):
        return lax.ppermute(value, "seq", pairs)

    two_on = [(i, i + 2) for i in range(blocks - 2)]
    even_to_odd = [(i, i + 1) for i in range(0, blocks, 2)]
    odd_to_even = [(i + 1, i) for i in range(0, blocks, 2)]

    tie = lax.optimization_barrier
    w_all = jnp.transpose(w_qkv, (1, 0, 2))
    seg = seg_ids.reshape(4, PIECE)
    w_pair = over_core(w_all)
    a0, a0_long = layer_norm(tokens, ln_gain, slopes)

    def back(steps):
        return [(i, i + steps) for i in range(blocks - steps)]

    a2 = over_seq(a0, two_on)
    b0 = over_x(a0)
    a1_odd = over_seq(a0, even_to_odd)
    c0 = over_core(a0_long)
    seg_sent, w_staged, c0 = tie((seg, w_all, c0))
    w_staged = stage(w_staged)
    seg1 = over_seq(seg_sent, back(1))
    seg4 = over_seq(seg_sent, back(SPAN))

    a2, b0, a1_odd, w_pair, w_staged, seg1, seg4 = tie((a2, b0, a1_odd, w_pair, w_staged, seg1, seg4))
    a4 = over_seq(a2, two_on)
    b2 = over_x(a2)
    crossed = over_seq(a2, even_to_odd + odd_to_even)
    d0 = over_core(b0)
    seg23 = over_seq(jnp.concatenate([seg, seg1], axis=0), back(2))
    segs = [seg1, seg23[:4], seg23[4:], seg4]
    q_own, q_pair, *state, key_cache, value_cache, slopes8 = own_block(
        slopes, seg, (a0, b0, c0, d0), w_staged, w_pair)

    crossed, b2, a4, segs, state[0] = tie((crossed, b2, a4, segs, state[0]))
    a1 = jnp.where(odd, a1_odd, crossed)
    b1 = over_x(a1)
    b4 = over_seq(b2, two_on)
    a3_even = over_seq(a4, odd_to_even)

    def merge(closing, pieces, which, state):
        return earlier_pieces(
            which, closing, slopes8, seg, segs, pieces, w_staged, w_pair, q_own, q_pair, state)

    state = merge(False, (a2, b2, a1, a4), ((2, 0), (2, 1), (1, 0), (4, 0)), state)

    a3_even, b1, b4, wo_sent, held = tie((a3_even, b1, b4, w_out, state[0]))
    state = (held, *state[1:])
    a3 = jnp.where(odd, crossed, a3_even)
    b3 = over_x(a3)
    wo_pair = over_core(wo_sent)
    state = merge(False, (b1, b4, a3), ((1, 1), (4, 1), (3, 0)), state)
    send, lse, out = merge(True, (b3,), ((3, 1),), state)
    got = over_core(send)
    y_pair = project(1, lse, out, got, w_out, wo_pair, None)
    y_got = over_x(y_pair)
    y_own = project(0, lse, out, got, w_out, wo_pair, tokens)
    hidden = (y_own + y_got.astype(F32)).astype(BF16)
    return (hidden, key_cache, value_cache)


def solution(mesh):
    in_specs = (
        P(("seq", "head"), None),
        P(),
        P(None, None, "head"),
        P("head"),
        P("head", None),
        P("seq"),
    )
    out_specs = (P(("seq", "head"), None), P("seq", "head"), P("seq", "head"))
    return jax.shard_map(
        on_device, mesh=mesh, in_specs=in_specs, out_specs=out_specs, check_vma=False
    )
```

```python
import jax
import jax.numpy as jnp
from jax import lax
from jax.experimental import pallas as pl
from jax.experimental.pallas import tpu as pltpu
from jax.sharding import PartitionSpec as P

HD = 128
SPAN = 4
PIECE = 128
EPSILON = 1e-05
NEG_FILL = -1e30
MASKED = -2e38
OWN_MIB = 14
EARLIER_MIB = 14
LOG2E = 1.4426950408889634

BF16 = jnp.bfloat16
F32 = jnp.float32
SMEM = pl.BlockSpec(memory_space=pltpu.SMEM)
HBM = pl.BlockSpec(memory_space=pltpu.HBM)
VMEM = pl.BlockSpec(memory_space=pltpu.VMEM)


def params(mebibytes):
    return pltpu.CompilerParams(vmem_limit_bytes=mebibytes * 2**20)


def cost(macs, nbytes, exps=0):
    return pl.CostEstimate(flops=2 * macs, bytes_accessed=nbytes, transcendentals=exps)


def dot(lhs, rhs):
    return jnp.dot(lhs, rhs, preferred_element_type=F32)


def three_addends(value):
    high = value.astype(BF16).astype(F32)
    middle = (value - high).astype(BF16).astype(F32)
    return high, middle, value - high - middle


def layer_norm(tokens, ln_gain, slopes):
    rows, model = tokens.shape

    def body(slopes_ref, tokens_hbm, gain_hbm, out_ref, long_ref, tokens_ref, gain_ref, sems):
        loads = [pltpu.make_async_copy(tokens_hbm, tokens_ref, sems.at[0]),
                 pltpu.make_async_copy(gain_hbm, gain_ref, sems.at[1])]
        for copy in loads:
            copy.start()
        for copy in loads:
            copy.wait()
        inputs = tokens_ref[...].astype(F32)
        centred = inputs - jnp.mean(inputs, axis=-1, keepdims=True)
        variance = jnp.mean(centred * centred, axis=-1, keepdims=True)
        normed = (centred * lax.rsqrt(variance + EPSILON) * gain_ref[...]).astype(BF16)
        out_ref[...] = normed
        long_ref[:rows, :] = normed
        row = lax.broadcasted_iota(jnp.int32, (16, model), 0)
        spread = jnp.zeros((16, model), F32)
        for head in range(4):
            spread = jnp.where(row % 4 == head, slopes_ref[head], spread)
        high, middle, low = three_addends(spread)
        part = jnp.where(row < 4, high, jnp.where(row < 8, middle, jnp.where(row < 12, low, 0.0)))
        long_ref[pl.ds(rows, 16), :] = part.astype(BF16)

    return pl.pallas_call(
        body,
        out_shape=(
            jax.ShapeDtypeStruct((rows, model), BF16),
            jax.ShapeDtypeStruct((rows + 16, model), BF16),
        ),
        in_specs=[SMEM, HBM, HBM],
        out_specs=(VMEM, VMEM),
        scratch_shapes=[
            pltpu.VMEM((rows, model), BF16),
            pltpu.VMEM((1, model), F32),
            pltpu.SemaphoreType.DMA((2,)),
        ],
        compiler_params=params(8),
        cost_estimate=cost(0, 2 * tokens.size * 2, tokens.size),
    )(slopes, tokens, ln_gain.reshape(1, -1))


def stage(weights):
    def body(source, out_ref, sem):
        copy = pltpu.make_async_copy(source, out_ref, sem)
        copy.start()
        copy.wait()

    return pl.pallas_call(
        body,
        out_shape=jax.ShapeDtypeStruct(weights.shape, weights.dtype),
        in_specs=[HBM],
        out_specs=VMEM,
        scratch_shapes=[pltpu.SemaphoreType.DMA],
        compiler_params=params(8),
        cost_estimate=cost(0, 2 * weights.size * 2),
    )(weights)


def place_of(place):
    return lax.axis_index("head") ^ (0, 2, 1, 3)[place]


def set_distance(block_base, key_base, keys, dist_ref):
    row = lax.broadcasted_iota(jnp.int32, (PIECE, PIECE), 0)
    for piece in range(keys):
        dist_ref[pl.ds(piece * PIECE, PIECE), :] = (row + (key_base(piece) - block_base)).astype(F32)


def set_own_masks(seg_ref, mask_ref, dist_ref):
    lane = lax.broadcasted_iota(jnp.int32, (1, PIECE), 1)
    row = lax.broadcasted_iota(jnp.int32, (PIECE, PIECE), 0)
    set_distance(0, lambda i: place_of(i) * PIECE, 2, dist_ref)
    for piece in range(2):
        rows = pl.ds(piece * PIECE, PIECE)
        k_pos = row + place_of(piece) * PIECE
        key_seg = seg_ref[pl.ds(place_of(piece), 1), :]
        key_seg = jnp.broadcast_to(key_seg, (PIECE, PIECE)).T
        for place in range(4):
            q_pos = lane + place_of(place) * PIECE
            kept = (key_seg == seg_ref[pl.ds(place_of(place), 1), :]) & (k_pos <= q_pos)
            mask_ref[rows, pl.ds(place * PIECE, PIECE)] = jnp.where(kept, 0.0, MASKED)


def set_earlier_masks(seg_ref, start, block_base, key_base, keys, mask_ref, dist_ref):
    row = lax.broadcasted_iota(jnp.int32, (PIECE, PIECE), 0)
    set_distance(block_base, key_base, keys, dist_ref)
    first_seg = seg_ref[0:1, 0:1]
    for piece in range(keys):
        rows = pl.ds(piece * PIECE, PIECE)
        late = row + key_base(piece) >= start
        for place in range(4):
            kept = late & (seg_ref[pl.ds(place_of(place), 1), :] == first_seg)
            mask_ref[rows, pl.ds(place * PIECE, PIECE)] = jnp.where(kept, 0.0, MASKED)


def attend(group, k_rows, v_t, q_ref, slopes_ref, mask_ref, dist_ref, before, stat_ref, acc_ref):
    heads = k_rows.shape[1] // HD
    for head in range(heads):
        cols = slice(head * HD, (head + 1) * HD)
        wide = pl.ds(head * HD, HD)
        place = heads * group + head
        bias = dist_ref[...] * (slopes_ref[place : place + 1, :] * LOG2E)
        bias = jnp.concatenate([bias] * (q_ref.shape[1] // PIECE), axis=1)
        scores = dot(k_rows[:, cols], q_ref[wide, :]) * (HD**-0.5 * LOG2E)
        scores = scores + bias + mask_ref[...]
        top = jnp.max(scores, axis=0, keepdims=True)
        prev = jnp.full_like(top, NEG_FILL) if before is None else before[0][head : head + 1, :]
        row_max = jnp.maximum(prev, top)
        expo = jnp.exp2(scores - row_max)
        total = jnp.sum(expo, axis=0, keepdims=True)
        update = dot(v_t[cols, :], expo.astype(BF16))
        if before is not None:
            rescale = jnp.exp2(prev - row_max)
            total = before[0][4 + head : 5 + head, :] * rescale + total
            update = before[1][wide, :] * rescale + update
        stat_ref[head : head + 1, :] = row_max
        stat_ref[4 + head : 5 + head, :] = total
        acc_ref[wide, :] = update


def state_shapes(width, block):
    return (jax.ShapeDtypeStruct((8, block), F32), jax.ShapeDtypeStruct((width, block), F32))


def own_block(slopes, seg, pieces, w_own, w_pair):
    depth, width = w_own.shape[1:]
    block = 4 * PIECE

    def body(s0, seg_ref, a, b, c, d, w0, w1, q0, q1, stat0, acc0, stat1, acc1, k_cache, v_cache, slopes_out,
             mask, dist):
        set_own_masks(seg_ref, mask, dist)
        tail = c[PIECE : PIECE + 16, :PIECE].astype(F32)
        for head in range(4):
            slopes_out[head : head + 1, :] = jnp.full((1, PIECE), s0[head], F32)
        slopes_out[4:8, :] = tail[0:4] + tail[4:8] + tail[8:12]
        x = jnp.concatenate([a[...], b[...], c[:PIECE, :], d[...]], axis=0)
        for group, (w, q, stat, acc) in enumerate(((w0, q0, stat0, acc0), (w1, q1, stat1, acc1))):
            rows = block if group == 0 else 2 * PIECE
            q[...] = dot(x, w[0]).T.astype(BF16)
            keys = dot(x[:rows], w[1]).astype(BF16)
            values = dot(x[:rows], w[2])
            if group == 0:
                for place in range(4):
                    to = pl.ds(pl.multiple_of(place_of(place) * PIECE, PIECE), PIECE)
                    k_cache[to, :] = keys[place * PIECE : (place + 1) * PIECE]
                    v_cache[to, :] = values[place * PIECE : (place + 1) * PIECE].astype(BF16)
            v_t = values[: 2 * PIECE].T.astype(BF16)
            attend(group, keys[: 2 * PIECE], v_t, q, slopes_out, mask, dist, None, stat, acc)

    return pl.pallas_call(
        body,
        out_shape=(jax.ShapeDtypeStruct((width, block), BF16),) * 2 + state_shapes(width, block) * 2 + (
            jax.ShapeDtypeStruct((block, width), BF16),
            jax.ShapeDtypeStruct((block, width), BF16),
            jax.ShapeDtypeStruct((8, PIECE), F32),
        ),
        in_specs=[SMEM] + [VMEM] * 7,
        out_specs=(VMEM,) * 9,
        scratch_shapes=[
            pltpu.VMEM((2 * PIECE, block), F32),
            pltpu.VMEM((2 * PIECE, PIECE), F32),
        ],
        compiler_params=params(OWN_MIB),
        cost_estimate=cost(5 * block * depth * width, 2**20, 0),
    )(slopes, seg, *pieces, w_own, w_pair)


def write_closed(states, send_ref, lse_ref, out_ref):
    width, block = states[0][1].shape
    half = block // 2
    sent = []
    for group, (stat, acc) in enumerate(states):
        total = stat[4:8, :]
        some = total > 0.0
        lse = jnp.where(some, stat[0:4, :] + jnp.log2(jnp.where(some, total, 1.0)), NEG_FILL)
        scale = jnp.where(some, 1.0 / jnp.where(some, total, 1.0), 0.0)
        lse_ref[4 * group : 4 * group + 4, :] = lse[:, :half]
        sent.append(lse[:, half:])
        for head in range(4):
            rows = pl.ds(head * HD, HD)
            to = pl.ds(group * width + head * HD, HD)
            normal = acc[rows, :] * scale[head : head + 1, :]
            out_ref[to, :] = normal[:, :half]
            send_ref[to, :] = normal[:, half:].astype(BF16)
    parts = list(three_addends(jnp.concatenate(sent, axis=0)))
    parts.append(jnp.zeros_like(parts[0]))
    send_ref[pl.ds(2 * width, 32), :] = jnp.concatenate(parts, axis=0).astype(BF16)


def earlier_pieces(which, closing, slopes8, seg, segs, pieces, w_own, w_pair, q_own, q_pair, state):
    depth, width = w_own.shape[1:]
    block = 4 * PIECE
    count = len(pieces)
    rows = count * PIECE
    n_out = 3 if closing else 4

    def body(slopes_ref, seg_ref, *refs):
        seg_refs, refs = refs[: len(segs)], refs[len(segs) :]
        sources, refs = refs[:count], refs[count:]
        (w0, w1, q0, q1), before, refs = refs[:4], (refs[4:6], refs[6:8]), refs[8:]
        outs, (mask, dist, *inner) = refs[:n_out], refs[n_out:]
        after = inner if closing else outs
        after = (after[0:2], after[2:4])
        block_num = lax.axis_index("seq")
        block_base = block_num * block
        same = jnp.zeros(seg_ref.shape, jnp.int32)
        for back, ref in enumerate(seg_refs, 1):
            same = same + jnp.where((ref[...] == seg_ref[0:1, 0:1]) & (block_num >= back), 1, 0)
        start = block_base - jnp.sum(same)

        def key_base(i):
            back, place = which[i]
            return block_base - back * block + place_of(place) * PIECE

        live = key_base(0) + PIECE > start
        for i in range(1, count):
            live = live | (key_base(i) + PIECE > start)

        @pl.when(live)
        def _():
            set_earlier_masks(seg_ref, start, block_base, key_base, count, mask, dist)
            x = jnp.concatenate([source[...] for source in sources], axis=0)
            for group, (w, q) in enumerate(((w0, q0), (w1, q1))):
                keys = dot(x, w[1]).astype(BF16)
                v_t = dot(x, w[2]).T.astype(BF16)
                attend(group, keys, v_t, q, slopes_ref, mask, dist, before[group], *after[group])

        @pl.when(jnp.logical_not(live))
        def _():
            for old, new in zip(before, after):
                new[0][...] = old[0][...]
                new[1][...] = old[1][...]

        if closing:
            write_closed(after, *outs)

    shapes = state_shapes(width, block) * 2
    scratch = [
        pltpu.VMEM((rows, block), F32),
        pltpu.VMEM((rows, PIECE), F32),
    ]
    if closing:
        scratch += [pltpu.VMEM(shape.shape, F32) for shape in shapes]
        shapes = (
            jax.ShapeDtypeStruct((2 * width + 32, block // 2), BF16),
            jax.ShapeDtypeStruct((8, block // 2), F32),
            jax.ShapeDtypeStruct((2 * width, block // 2), F32),
        )
    return pl.pallas_call(
        body,
        out_shape=shapes,
        in_specs=[VMEM] * (10 + len(segs) + count),
        out_specs=(VMEM,) * n_out,
        scratch_shapes=scratch,
        compiler_params=params(EARLIER_MIB),
        cost_estimate=cost(4 * rows * depth * width, 2**20, 0),
    )(slopes8, seg, *segs, *pieces, w_own, w_pair, q_own, q_pair, *state)


def project(place, lse, out, got, wo_own, wo_pair, tokens):
    wide = out.shape[0]
    width, model = wo_own.shape

    def body(lse_ref, out_ref, got_ref, w0, w1, *refs):
        y_ref, ctx = refs[-2:]
        lanes = pl.ds(place * PIECE, PIECE)
        other = got_ref[pl.ds(wide, 32), lanes].astype(F32)
        other = other[0:8] + other[8:16] + other[16:24]
        for head in range(8):
            swapped = (head + 4) % 8
            mine, theirs = lse_ref[head : head + 1, lanes], other[swapped : swapped + 1]
            top = jnp.maximum(mine, theirs)
            weigh, weigh_other = jnp.exp2(mine - top), jnp.exp2(theirs - top)
            joined = (out_ref[pl.ds(head * HD, HD), lanes] * weigh
                      + got_ref[pl.ds(swapped * HD, HD), lanes].astype(F32) * weigh_other)
            joined = joined / (weigh + weigh_other)
            ctx[:, head * HD : (head + 1) * HD] = joined.T.astype(BF16)
        result = dot(ctx[:, :width], w0[...]) + dot(ctx[:, width:], w1[...])
        if tokens is not None:
            result = result + refs[0][...].astype(F32)
        y_ref[...] = result.astype(y_ref.dtype)

    extra = () if tokens is None else (tokens,)
    return pl.pallas_call(
        body,
        out_shape=jax.ShapeDtypeStruct((PIECE, model), BF16 if tokens is None else F32),
        in_specs=[VMEM] * (5 + len(extra)),
        out_specs=VMEM,
        scratch_shapes=[pltpu.VMEM((PIECE, wide), BF16)],
        compiler_params=params(16),
        cost_estimate=cost(PIECE * wide * model, 2**20, 0),
    )(lse, out, got, wo_own, wo_pair, *extra)


def on_device(tokens, ln_gain, w_qkv, slopes, w_out, seg_ids):
    blocks = lax.axis_size("seq")
    block_num = lax.axis_index("seq")
    odd = (block_num % 2) == 1

    def over_core(value):
        return lax.ppermute(value, "head", [(i, i ^ 1) for i in range(4)])

    def over_x(value):
        return lax.ppermute(value, "head", [(i, i ^ 2) for i in range(4)])

    def over_seq(value, pairs):
        return lax.ppermute(value, "seq", pairs)

    two_on = [(i, i + 2) for i in range(blocks - 2)]
    even_to_odd = [(i, i + 1) for i in range(0, blocks, 2)]
    odd_to_even = [(i + 1, i) for i in range(0, blocks, 2)]

    tie = lax.optimization_barrier
    w_all = jnp.transpose(w_qkv, (1, 0, 2))
    seg = seg_ids.reshape(4, PIECE)
    w_pair = over_core(w_all)
    a0, a0_long = layer_norm(tokens, ln_gain, slopes)

    a2 = over_seq(a0, two_on)
    b0 = over_x(a0)
    a1_odd = over_seq(a0, even_to_odd)
    c0 = over_core(a0_long)
    seg_sent, w_staged, c0 = tie((seg, w_all, c0))
    w_staged = stage(w_staged)
    seg1 = over_seq(seg_sent, [(i, i + 1) for i in range(blocks - 1)])

    a2, b0, a1_odd, w_pair, w_staged, seg1 = tie((a2, b0, a1_odd, w_pair, w_staged, seg1))
    a4 = over_seq(a2, two_on)
    b2 = over_x(a2)
    crossed = over_seq(a2, even_to_odd + odd_to_even)
    d0 = over_core(b0)
    seg23 = over_seq(jnp.concatenate([seg, seg1], axis=0), two_on)
    segs = [seg1, seg23[:4], seg23[4:]]
    q_own, q_pair, *state, key_cache, value_cache, slopes8 = own_block(
        slopes, seg, (a0, b0, c0, d0), w_staged, w_pair)

    crossed, b2, a4, segs, state[0] = tie((crossed, b2, a4, segs, state[0]))
    a1 = jnp.where(odd, a1_odd, crossed)
    b1 = over_x(a1)
    b4 = over_seq(b2, two_on)
    a3_even = over_seq(a4, odd_to_even)
    seg4 = over_seq(segs[1], two_on)

    def merge(closing, segs, pieces, which, state):
        return earlier_pieces(
            which, closing, slopes8, seg, segs, pieces, w_staged, w_pair, q_own, q_pair, state)

    state = merge(False, segs, (a2, b2, a1), ((2, 0), (2, 1), (1, 0)), state)

    a3_even, b1, b4, seg4, wo_sent, held = tie((a3_even, b1, b4, seg4, w_out, state[0]))
    segs = [*segs, seg4]
    state = (held, *state[1:])
    a3 = jnp.where(odd, crossed, a3_even)
    b3 = over_x(a3)
    wo_pair = over_core(wo_sent)
    state = merge(False, segs, (b1, a4, b4, a3), ((1, 1), (4, 0), (4, 1), (3, 0)), state)
    send, lse, out = merge(True, segs, (b3,), ((3, 1),), state)
    got = over_core(send)
    y_pair = project(1, lse, out, got, w_out, wo_pair, None)
    y_got = over_x(y_pair)
    y_own = project(0, lse, out, got, w_out, wo_pair, tokens)
    hidden = (y_own + y_got.astype(F32)).astype(BF16)
    return (hidden, key_cache, value_cache)


def solution(mesh):
    in_specs = (
        P(("seq", "head"), None),
        P(),
        P(None, None, "head"),
        P("head"),
        P("head", None),
        P("seq"),
    )
    out_specs = (P(("seq", "head"), None), P("seq", "head"), P("seq", "head"))
    return jax.shard_map(
        on_device, mesh=mesh, in_specs=in_specs, out_specs=out_specs, check_vma=False
    )
```

```python
import jax
import jax.numpy as jnp
from jax import lax
from jax.experimental import pallas as pl
from jax.experimental.pallas import tpu as pltpu
from jax.sharding import PartitionSpec as P

HD = 128
SPAN = 4
PIECE = 128
EPSILON = 1e-05
NEG_FILL = -1e30
MASKED = -2e38
OWN_MIB = 14
EARLIER_MIB = 14
LOG2E = 1.4426950408889634

BF16 = jnp.bfloat16
F32 = jnp.float32
SMEM = pl.BlockSpec(memory_space=pltpu.SMEM)
HBM = pl.BlockSpec(memory_space=pltpu.HBM)
VMEM = pl.BlockSpec(memory_space=pltpu.VMEM)


def params(mebibytes):
    return pltpu.CompilerParams(vmem_limit_bytes=mebibytes * 2**20)


def cost(macs, nbytes, exps=0):
    return pl.CostEstimate(flops=2 * macs, bytes_accessed=nbytes, transcendentals=exps)


def dot(lhs, rhs):
    return jnp.dot(lhs, rhs, preferred_element_type=F32)


def three_addends(value):
    high = value.astype(BF16).astype(F32)
    middle = (value - high).astype(BF16).astype(F32)
    return high, middle, value - high - middle


def layer_norm(tokens, ln_gain, slopes):
    rows, model = tokens.shape

    def body(slopes_ref, tokens_hbm, gain_hbm, out_ref, long_ref, tokens_ref, gain_ref, sems):
        loads = [pltpu.make_async_copy(tokens_hbm, tokens_ref, sems.at[0]),
                 pltpu.make_async_copy(gain_hbm, gain_ref, sems.at[1])]
        for copy in loads:
            copy.start()
        for copy in loads:
            copy.wait()
        inputs = tokens_ref[...].astype(F32)
        centred = inputs - jnp.mean(inputs, axis=-1, keepdims=True)
        variance = jnp.mean(centred * centred, axis=-1, keepdims=True)
        normed = (centred * lax.rsqrt(variance + EPSILON) * gain_ref[...]).astype(BF16)
        out_ref[...] = normed
        long_ref[:rows, :] = normed
        row = lax.broadcasted_iota(jnp.int32, (16, model), 0)
        spread = jnp.zeros((16, model), F32)
        for head in range(4):
            spread = jnp.where(row % 4 == head, slopes_ref[head], spread)
        high, middle, low = three_addends(spread)
        part = jnp.where(row < 4, high, jnp.where(row < 8, middle, jnp.where(row < 12, low, 0.0)))
        long_ref[pl.ds(rows, 16), :] = part.astype(BF16)

    return pl.pallas_call(
        body,
        out_shape=(
            jax.ShapeDtypeStruct((rows, model), BF16),
            jax.ShapeDtypeStruct((rows + 16, model), BF16),
        ),
        in_specs=[SMEM, HBM, HBM],
        out_specs=(VMEM, VMEM),
        scratch_shapes=[
            pltpu.VMEM((rows, model), BF16),
            pltpu.VMEM((1, model), F32),
            pltpu.SemaphoreType.DMA((2,)),
        ],
        compiler_params=params(8),
        cost_estimate=cost(0, 2 * tokens.size * 2, tokens.size),
    )(slopes, tokens, ln_gain.reshape(1, -1))


def stage(weights):
    def body(source, out_ref, sem):
        copy = pltpu.make_async_copy(source, out_ref, sem)
        copy.start()
        copy.wait()

    return pl.pallas_call(
        body,
        out_shape=jax.ShapeDtypeStruct(weights.shape, weights.dtype),
        in_specs=[HBM],
        out_specs=VMEM,
        scratch_shapes=[pltpu.SemaphoreType.DMA],
        compiler_params=params(8),
        cost_estimate=cost(0, 2 * weights.size * 2),
    )(weights)


def pick(even_value, odd_value):
    def body(even_ref, odd_ref, out_ref):
        odd = lax.axis_index("seq") % 2 == 1

        @pl.when(odd)
        def _():
            out_ref[...] = odd_ref[...]

        @pl.when(jnp.logical_not(odd))
        def _():
            out_ref[...] = even_ref[...]

    return pl.pallas_call(
        body,
        out_shape=jax.ShapeDtypeStruct(even_value.shape, even_value.dtype),
        in_specs=[VMEM, VMEM],
        out_specs=VMEM,
        compiler_params=params(8),
        cost_estimate=cost(0, 2 * even_value.size * 2),
    )(even_value, odd_value)


def place_of(place):
    return lax.axis_index("head") ^ (0, 2, 1, 3)[place]


def set_distance(block_base, key_base, keys, dist_ref):
    row = lax.broadcasted_iota(jnp.int32, (PIECE, PIECE), 0)
    for piece in range(keys):
        dist_ref[pl.ds(piece * PIECE, PIECE), :] = (row + (key_base(piece) - block_base)).astype(F32)


def set_own_masks(seg_ref, mask_ref, dist_ref):
    lane = lax.broadcasted_iota(jnp.int32, (1, PIECE), 1)
    row = lax.broadcasted_iota(jnp.int32, (PIECE, PIECE), 0)
    set_distance(0, lambda i: place_of(i) * PIECE, 2, dist_ref)
    for piece in range(2):
        rows = pl.ds(piece * PIECE, PIECE)
        k_pos = row + place_of(piece) * PIECE
        key_seg = seg_ref[pl.ds(place_of(piece), 1), :]
        key_seg = jnp.broadcast_to(key_seg, (PIECE, PIECE)).T
        for place in range(4):
            q_pos = lane + place_of(place) * PIECE
            kept = (key_seg == seg_ref[pl.ds(place_of(place), 1), :]) & (k_pos <= q_pos)
            mask_ref[rows, pl.ds(place * PIECE, PIECE)] = jnp.where(kept, 0.0, MASKED)


def set_earlier_masks(seg_ref, start, block_base, key_base, keys, mask_ref, dist_ref):
    row = lax.broadcasted_iota(jnp.int32, (PIECE, PIECE), 0)
    set_distance(block_base, key_base, keys, dist_ref)
    first_seg = seg_ref[0:1, 0:1]
    for piece in range(keys):
        rows = pl.ds(piece * PIECE, PIECE)
        late = row + key_base(piece) >= start
        for place in range(4):
            kept = late & (seg_ref[pl.ds(place_of(place), 1), :] == first_seg)
            mask_ref[rows, pl.ds(place * PIECE, PIECE)] = jnp.where(kept, 0.0, MASKED)


def attend(group, k_rows, v_t, q_ref, slopes_ref, mask_ref, dist_ref, before, stat_ref, acc_ref):
    heads = k_rows.shape[1] // HD
    for head in range(heads):
        cols = slice(head * HD, (head + 1) * HD)
        wide = pl.ds(head * HD, HD)
        place = heads * group + head
        bias = dist_ref[...] * (slopes_ref[place : place + 1, :] * LOG2E)
        bias = jnp.concatenate([bias] * (q_ref.shape[1] // PIECE), axis=1)
        scores = dot(k_rows[:, cols], q_ref[wide, :]) * (HD**-0.5 * LOG2E)
        scores = scores + bias + mask_ref[...]
        top = jnp.max(scores, axis=0, keepdims=True)
        prev = jnp.full_like(top, NEG_FILL) if before is None else before[0][head : head + 1, :]
        row_max = jnp.maximum(prev, top)
        expo = jnp.exp2(scores - row_max)
        total = jnp.sum(expo, axis=0, keepdims=True)
        update = dot(v_t[cols, :], expo.astype(BF16))
        if before is not None:
            rescale = jnp.exp2(prev - row_max)
            total = before[0][4 + head : 5 + head, :] * rescale + total
            update = before[1][wide, :] * rescale + update
        stat_ref[head : head + 1, :] = row_max
        stat_ref[4 + head : 5 + head, :] = total
        acc_ref[wide, :] = update


def state_shapes(width, block):
    return (jax.ShapeDtypeStruct((8, block), F32), jax.ShapeDtypeStruct((width, block), F32))


def own_block(slopes, seg, pieces, w_own, w_pair):
    depth, width = w_own.shape[1:]
    block = 4 * PIECE

    def body(s0, seg_ref, a, b, c, d, w0, w1, q0, q1, stat0, acc0, stat1, acc1, k_cache, v_cache, slopes_out,
             mask, dist):
        set_own_masks(seg_ref, mask, dist)
        tail = c[PIECE : PIECE + 16, :PIECE].astype(F32)
        for head in range(4):
            slopes_out[head : head + 1, :] = jnp.full((1, PIECE), s0[head], F32)
        slopes_out[4:8, :] = tail[0:4] + tail[4:8] + tail[8:12]
        x = jnp.concatenate([a[...], b[...], c[:PIECE, :], d[...]], axis=0)
        for group, (w, q, stat, acc) in enumerate(((w0, q0, stat0, acc0), (w1, q1, stat1, acc1))):
            rows = block if group == 0 else 2 * PIECE
            q[...] = dot(x, w[0]).T.astype(BF16)
            keys = dot(x[:rows], w[1]).astype(BF16)
            values = dot(x[:rows], w[2])
            if group == 0:
                for place in range(4):
                    to = pl.ds(pl.multiple_of(place_of(place) * PIECE, PIECE), PIECE)
                    k_cache[to, :] = keys[place * PIECE : (place + 1) * PIECE]
                    v_cache[to, :] = values[place * PIECE : (place + 1) * PIECE].astype(BF16)
            v_t = values[: 2 * PIECE].T.astype(BF16)
            attend(group, keys[: 2 * PIECE], v_t, q, slopes_out, mask, dist, None, stat, acc)

    return pl.pallas_call(
        body,
        out_shape=(jax.ShapeDtypeStruct((width, block), BF16),) * 2 + state_shapes(width, block) * 2 + (
            jax.ShapeDtypeStruct((block, width), BF16),
            jax.ShapeDtypeStruct((block, width), BF16),
            jax.ShapeDtypeStruct((8, PIECE), F32),
        ),
        in_specs=[SMEM] + [VMEM] * 7,
        out_specs=(VMEM,) * 9,
        scratch_shapes=[
            pltpu.VMEM((2 * PIECE, block), F32),
            pltpu.VMEM((2 * PIECE, PIECE), F32),
        ],
        compiler_params=params(OWN_MIB),
        cost_estimate=cost(5 * block * depth * width, 2**20, 0),
    )(slopes, seg, *pieces, w_own, w_pair)


def write_closed(states, send_ref, lse_ref, out_ref):
    width, block = states[0][1].shape
    half = block // 2
    sent = []
    for group, (stat, acc) in enumerate(states):
        total = stat[4:8, :]
        some = total > 0.0
        lse = jnp.where(some, stat[0:4, :] + jnp.log2(jnp.where(some, total, 1.0)), NEG_FILL)
        scale = jnp.where(some, 1.0 / jnp.where(some, total, 1.0), 0.0)
        lse_ref[4 * group : 4 * group + 4, :] = lse[:, :half]
        sent.append(lse[:, half:])
        for head in range(4):
            rows = pl.ds(head * HD, HD)
            to = pl.ds(group * width + head * HD, HD)
            normal = acc[rows, :] * scale[head : head + 1, :]
            out_ref[to, :] = normal[:, :half]
            send_ref[to, :] = normal[:, half:].astype(BF16)
    parts = list(three_addends(jnp.concatenate(sent, axis=0)))
    parts.append(jnp.zeros_like(parts[0]))
    send_ref[pl.ds(2 * width, 32), :] = jnp.concatenate(parts, axis=0).astype(BF16)


def earlier_pieces(which, closing, slopes8, seg, segs, pieces, w_own, w_pair, q_own, q_pair, state):
    depth, width = w_own.shape[1:]
    block = 4 * PIECE
    count = len(pieces)
    rows = len(which) * PIECE
    n_out = 3 if closing else 4

    def body(slopes_ref, seg_ref, *refs):
        seg_refs, refs = refs[: len(segs)], refs[len(segs) :]
        sources, refs = refs[:count], refs[count:]
        (w0, w1, q0, q1), before, refs = refs[:4], (refs[4:6], refs[6:8]), refs[8:]
        outs, (mask, dist, *inner) = refs[:n_out], refs[n_out:]
        after = inner if closing else outs
        after = (after[0:2], after[2:4])
        block_num = lax.axis_index("seq")
        block_base = block_num * block
        same = jnp.zeros(seg_ref.shape, jnp.int32)
        for back, ref in enumerate(seg_refs, 1):
            same = same + jnp.where((ref[...] == seg_ref[0:1, 0:1]) & (block_num >= back), 1, 0)
        start = block_base - jnp.sum(same)

        def key_base(i):
            def base(back, place):
                return block_base - back * block + place_of(place) * PIECE if back else -SPAN * block

            return jnp.where(block_num % 2 == 1, base(*which[i][1]), base(*which[i][0]))

        live = key_base(0) + PIECE > start
        for i in range(1, len(which)):
            live = live | (key_base(i) + PIECE > start)

        @pl.when(live)
        def _():
            set_earlier_masks(seg_ref, start, block_base, key_base, len(which), mask, dist)
            x = jnp.concatenate([source[...] for source in sources], axis=0)
            for group, (w, q) in enumerate(((w0, q0), (w1, q1))):
                keys = dot(x, w[1]).astype(BF16)
                v_t = dot(x, w[2]).T.astype(BF16)
                attend(group, keys, v_t, q, slopes_ref, mask, dist, before[group], *after[group])

        @pl.when(jnp.logical_not(live))
        def _():
            for old, new in zip(before, after):
                new[0][...] = old[0][...]
                new[1][...] = old[1][...]

        if closing:
            write_closed(after, *outs)

    shapes = state_shapes(width, block) * 2
    scratch = [
        pltpu.VMEM((rows, block), F32),
        pltpu.VMEM((rows, PIECE), F32),
    ]
    if closing:
        scratch += [pltpu.VMEM(shape.shape, F32) for shape in shapes]
        shapes = (
            jax.ShapeDtypeStruct((2 * width + 32, block // 2), BF16),
            jax.ShapeDtypeStruct((8, block // 2), F32),
            jax.ShapeDtypeStruct((2 * width, block // 2), F32),
        )
    return pl.pallas_call(
        body,
        out_shape=shapes,
        in_specs=[VMEM] * (10 + len(segs) + count),
        out_specs=(VMEM,) * n_out,
        scratch_shapes=scratch,
        compiler_params=params(EARLIER_MIB),
        cost_estimate=cost(4 * rows * depth * width, 2**20, 0),
    )(slopes8, seg, *segs, *pieces, w_own, w_pair, q_own, q_pair, *state)


def project(place, lse, out, got, wo_own, wo_pair, tokens):
    wide = out.shape[0]
    width, model = wo_own.shape

    def body(lse_ref, out_ref, got_ref, w0, w1, *refs):
        y_ref, ctx = refs[-2:]
        lanes = pl.ds(place * PIECE, PIECE)
        other = got_ref[pl.ds(wide, 32), lanes].astype(F32)
        other = other[0:8] + other[8:16] + other[16:24]
        for head in range(8):
            swapped = (head + 4) % 8
            mine, theirs = lse_ref[head : head + 1, lanes], other[swapped : swapped + 1]
            top = jnp.maximum(mine, theirs)
            weigh, weigh_other = jnp.exp2(mine - top), jnp.exp2(theirs - top)
            joined = (out_ref[pl.ds(head * HD, HD), lanes] * weigh
                      + got_ref[pl.ds(swapped * HD, HD), lanes].astype(F32) * weigh_other)
            joined = joined / (weigh + weigh_other)
            ctx[:, head * HD : (head + 1) * HD] = joined.T.astype(BF16)
        result = dot(ctx[:, :width], w0[...]) + dot(ctx[:, width:], w1[...])
        if tokens is not None:
            result = result + refs[0][...].astype(F32)
        y_ref[...] = result.astype(y_ref.dtype)

    extra = () if tokens is None else (tokens,)
    return pl.pallas_call(
        body,
        out_shape=jax.ShapeDtypeStruct((PIECE, model), BF16 if tokens is None else F32),
        in_specs=[VMEM] * (5 + len(extra)),
        out_specs=VMEM,
        scratch_shapes=[pltpu.VMEM((PIECE, wide), BF16)],
        compiler_params=params(16),
        cost_estimate=cost(PIECE * wide * model, 2**20, 0),
    )(lse, out, got, wo_own, wo_pair, *extra)


def on_device(tokens, ln_gain, w_qkv, slopes, w_out, seg_ids):
    blocks = lax.axis_size("seq")
    block_num = lax.axis_index("seq")
    odd = (block_num % 2) == 1

    def over_core(value):
        return lax.ppermute(value, "head", [(i, i ^ 1) for i in range(4)])

    def over_x(value):
        return lax.ppermute(value, "head", [(i, i ^ 2) for i in range(4)])

    def over_seq(value, pairs):
        return lax.ppermute(value, "seq", pairs)

    two_on = [(i, i + 2) for i in range(blocks - 2)]
    even_to_odd = [(i, i + 1) for i in range(0, blocks, 2)]
    odd_to_even = [(i + 1, i) for i in range(0, blocks, 2)]

    tie = lax.optimization_barrier
    w_all = jnp.transpose(w_qkv, (1, 0, 2))
    seg = seg_ids.reshape(4, PIECE)
    w_pair = over_core(w_all)
    a0, a0_long = layer_norm(tokens, ln_gain, slopes)

    a2 = over_seq(a0, two_on)
    b0 = over_x(a0)
    a1_odd = over_seq(a0, even_to_odd)
    c0 = over_core(a0_long)
    seg_sent, w_staged, c0 = tie((seg, w_all, c0))
    w_staged = stage(w_staged)
    seg1 = over_seq(seg_sent, [(i, i + 1) for i in range(blocks - 1)])

    a2, b0, a1_odd, w_pair, w_staged, seg1 = tie((a2, b0, a1_odd, w_pair, w_staged, seg1))
    a4 = over_seq(a2, two_on)
    b2 = over_x(a2)
    crossed = over_seq(a2, even_to_odd + odd_to_even)
    d0 = over_core(b0)
    seg23 = over_seq(jnp.concatenate([seg, seg1], axis=0), two_on)
    segs = [seg1, seg23[:4], seg23[4:]]
    q_own, q_pair, *state, key_cache, value_cache, slopes8 = own_block(
        slopes, seg, (a0, b0, c0, d0), w_staged, w_pair)

    crossed, b2, a4, b0_sent, segs, wo_sent, state[0] = tie((crossed, b2, a4, b0, segs, w_out, state[0]))
    over_y = over_seq(pick(b0_sent, a4), even_to_odd + odd_to_even)
    x_third = over_x(crossed)
    b4 = over_seq(b2, two_on)
    seg4 = over_seq(segs[1], two_on)
    wo_pair = over_core(wo_sent)

    def merge(closing, segs, pieces, which, state):
        return earlier_pieces(
            which, closing, slopes8, seg, segs, pieces, w_staged, w_pair, q_own, q_pair, state)

    state = merge(
        False, segs, (a2, b2, crossed, a1_odd), (((2, 0),) * 2, ((2, 1),) * 2, ((1, 0), (3, 0)), ((0, 0), (1, 0))), state)

    over_y, x_third, b4, seg4, held = tie((over_y, x_third, b4, seg4, state[0]))
    segs = [*segs, seg4]
    state = (held, *state[1:])
    b3_top = over_x(over_y[: PIECE // 2])
    b3_rest = over_seq(b4[PIECE // 2 :], odd_to_even)
    state = merge(
        False, segs, (a4, b4, x_third, over_y), (((4, 0),) * 2, ((4, 1),) * 2, ((1, 1), (3, 1)), ((3, 0), (1, 1))), state)
    send, lse, out = merge(True, segs, (b3_top, b3_rest), (((3, 1), (0, 0)),), state)
    got = over_core(send)
    y_pair = project(1, lse, out, got, w_out, wo_pair, None)
    y_got = over_x(y_pair)
    y_own = project(0, lse, out, got, w_out, wo_pair, tokens)
    hidden = (y_own + y_got.astype(F32)).astype(BF16)
    return (hidden, key_cache, value_cache)


def solution(mesh):
    in_specs = (
        P(("seq", "head"), None),
        P(),
        P(None, None, "head"),
        P("head"),
        P("head", None),
        P("seq"),
    )
    out_specs = (P(("seq", "head"), None), P("seq", "head"), P("seq", "head"))
    return jax.shard_map(
        on_device, mesh=mesh, in_specs=in_specs, out_specs=out_specs, check_vma=False
    )
```

```python
import jax
import jax.numpy as jnp
from jax import lax
from jax.experimental import pallas as pl
from jax.experimental.pallas import tpu as pltpu
from jax.sharding import PartitionSpec as P

HD = 128
SPAN = 4
PIECE = 128
EPSILON = 1e-05
NEG_FILL = -1e30
MASKED = -2e38
OWN_MIB = 16
EARLIER_MIB = 16
LOG2E = 1.4426950408889634

BF16 = jnp.bfloat16
F32 = jnp.float32
SMEM = pl.BlockSpec(memory_space=pltpu.SMEM)
HBM = pl.BlockSpec(memory_space=pltpu.HBM)
VMEM = pl.BlockSpec(memory_space=pltpu.VMEM)


def params(mebibytes):
    return pltpu.CompilerParams(vmem_limit_bytes=mebibytes * 2**20)


def cost(macs, nbytes, exps=0):
    return pl.CostEstimate(flops=2 * macs, bytes_accessed=nbytes, transcendentals=exps)


def dot(lhs, rhs):
    return jnp.dot(lhs, rhs, preferred_element_type=F32)


def three_addends(value):
    high = value.astype(BF16).astype(F32)
    middle = (value - high).astype(BF16).astype(F32)
    return high, middle, value - high - middle


def normalise(tokens, gain):
    inputs = tokens.astype(F32)
    centred = inputs - jnp.mean(inputs, axis=-1, keepdims=True)
    variance = jnp.mean(centred * centred, axis=-1, keepdims=True)
    return (centred * lax.rsqrt(variance + EPSILON) * gain).astype(BF16)


def count_back(slopes, seg, far_seg):
    def body(slopes_ref, seg_ref, far_ref, out_ref):
        there = lax.axis_index("seq") >= lax.axis_index("head") + 1
        same = jnp.where((far_ref[...] == seg_ref[0:1, 0:1]) & there, 1, 0)
        for head in range(4):
            out_ref[head : head + 1, :] = jnp.full((1, PIECE), slopes_ref[head], F32)
        out_ref[4:8, :] = jnp.full((4, PIECE), jnp.sum(same).astype(F32), F32)

    return pl.pallas_call(
        body,
        out_shape=jax.ShapeDtypeStruct((8, PIECE), F32),
        in_specs=[SMEM, VMEM, VMEM],
        out_specs=VMEM,
        compiler_params=params(4),
        cost_estimate=cost(0, 2**13),
    )(slopes, seg, far_seg)


def add_counts(mine, other):
    def body(mine_ref, other_ref, out_ref):
        out_ref[...] = mine_ref[...] + other_ref[...]

    return pl.pallas_call(
        body,
        out_shape=jax.ShapeDtypeStruct(mine.shape, F32),
        in_specs=[VMEM, VMEM],
        out_specs=VMEM,
        compiler_params=params(4),
        cost_estimate=cost(0, 2**13),
    )(mine, other)


def stage(weights):
    def body(source, out_ref, sem):
        copy = pltpu.make_async_copy(source, out_ref, sem)
        copy.start()
        copy.wait()

    return pl.pallas_call(
        body,
        out_shape=jax.ShapeDtypeStruct(weights.shape, weights.dtype),
        in_specs=[HBM],
        out_specs=VMEM,
        scratch_shapes=[pltpu.SemaphoreType.DMA],
        compiler_params=params(8),
        cost_estimate=cost(0, 2 * weights.size * 2),
    )(weights)


def pick(even_value, odd_value):
    def body(even_ref, odd_ref, out_ref):
        odd = lax.axis_index("seq") % 2 == 1

        @pl.when(odd)
        def _():
            out_ref[...] = odd_ref[...]

        @pl.when(jnp.logical_not(odd))
        def _():
            out_ref[...] = even_ref[...]

    return pl.pallas_call(
        body,
        out_shape=jax.ShapeDtypeStruct(even_value.shape, even_value.dtype),
        in_specs=[VMEM, VMEM],
        out_specs=VMEM,
        compiler_params=params(8),
        cost_estimate=cost(0, 2 * even_value.size * 2),
    )(even_value, odd_value)


def place_of(place):
    return lax.axis_index("head") ^ (0, 2, 1, 3)[place]


def set_distance(block_base, key_base, keys, dist_ref):
    row = lax.broadcasted_iota(jnp.int32, (PIECE, PIECE), 0)
    for piece in range(keys):
        dist_ref[pl.ds(piece * PIECE, PIECE), :] = (row + (key_base(piece) - block_base)).astype(F32)


def set_own_masks(seg_ref, mask_ref, dist_ref):
    lane = lax.broadcasted_iota(jnp.int32, (1, PIECE), 1)
    row = lax.broadcasted_iota(jnp.int32, (PIECE, PIECE), 0)
    set_distance(0, lambda i: place_of(i) * PIECE, 2, dist_ref)
    for piece in range(2):
        rows = pl.ds(piece * PIECE, PIECE)
        k_pos = row + place_of(piece) * PIECE
        key_seg = seg_ref[pl.ds(place_of(piece), 1), :]
        key_seg = jnp.broadcast_to(key_seg, (PIECE, PIECE)).T
        for place in range(4):
            q_pos = lane + place_of(place) * PIECE
            kept = (key_seg == seg_ref[pl.ds(place_of(place), 1), :]) & (k_pos <= q_pos)
            mask_ref[rows, pl.ds(place * PIECE, PIECE)] = jnp.where(kept, 0.0, MASKED)


def set_earlier_masks(seg_ref, start, block_base, key_base, keys, mask_ref, dist_ref):
    row = lax.broadcasted_iota(jnp.int32, (PIECE, PIECE), 0)
    set_distance(block_base, key_base, keys, dist_ref)
    first_seg = seg_ref[0:1, 0:1]
    for piece in range(keys):
        rows = pl.ds(piece * PIECE, PIECE)
        late = row + key_base(piece) >= start
        for place in range(4):
            kept = late & (seg_ref[pl.ds(place_of(place), 1), :] == first_seg)
            mask_ref[rows, pl.ds(place * PIECE, PIECE)] = jnp.where(kept, 0.0, MASKED)


def attend(k_rows, v_t, q_ref, slopes_ref, mask_ref, dist_ref, before, stat_ref, acc_ref):
    heads = k_rows.shape[1] // HD
    for head in range(heads):
        cols = slice(head * HD, (head + 1) * HD)
        wide = pl.ds(head * HD, HD)
        bias = dist_ref[...] * (slopes_ref[head : head + 1, :] * LOG2E)
        bias = jnp.concatenate([bias] * (q_ref.shape[1] // PIECE), axis=1)
        scores = dot(k_rows[:, cols], q_ref[wide, :]) * (HD**-0.5 * LOG2E)
        scores = scores + bias + mask_ref[...]
        top = jnp.max(scores, axis=0, keepdims=True)
        prev = jnp.full_like(top, NEG_FILL) if before is None else before[0][head : head + 1, :]
        row_max = jnp.maximum(prev, top)
        expo = jnp.exp2(scores - row_max)
        total = jnp.sum(expo, axis=0, keepdims=True)
        update = dot(v_t[cols, :], expo.astype(BF16))
        if before is not None:
            rescale = jnp.exp2(prev - row_max)
            total = before[0][4 + head : 5 + head, :] * rescale + total
            update = before[1][wide, :] * rescale + update
        stat_ref[head : head + 1, :] = row_max
        stat_ref[4 + head : 5 + head, :] = total
        acc_ref[wide, :] = update


def state_shapes(width, block):
    return (jax.ShapeDtypeStruct((8, block), F32), jax.ShapeDtypeStruct((width, block), F32))


def own_block(info, info_pair, seg, gain, pieces, w_own, w_pair):
    depth, width = w_own.shape[1:]
    block = 4 * PIECE

    def body(s0, s1, seg_ref, gain_ref, a, b, c, d, w0, w1, q0, q1, stat0, acc0, stat1, acc1, k_cache, v_cache,
             x, mask, dist):
        set_own_masks(seg_ref, mask, dist)
        for place, piece in enumerate((a, b, c, d)):
            x[pl.ds(place * PIECE, PIECE), :] = normalise(piece[...], gain_ref[...])
        for group, (w, q, stat, acc) in enumerate(((w0, q0, stat0, acc0), (w1, q1, stat1, acc1))):
            rows = block if group == 0 else 2 * PIECE
            q[...] = dot(x[...], w[0]).T.astype(BF16)
            keys = dot(x[:rows, :], w[1]).astype(BF16)
            values = dot(x[:rows, :], w[2])
            if group == 0:
                for place in range(4):
                    to = pl.ds(pl.multiple_of(place_of(place) * PIECE, PIECE), PIECE)
                    k_cache[to, :] = keys[place * PIECE : (place + 1) * PIECE]
                    v_cache[to, :] = values[place * PIECE : (place + 1) * PIECE].astype(BF16)
            v_t = values[: 2 * PIECE].T.astype(BF16)
            attend(keys[: 2 * PIECE], v_t, q, (s0, s1)[group], mask, dist, None, stat, acc)

    return pl.pallas_call(
        body,
        out_shape=(jax.ShapeDtypeStruct((width, block), BF16),) * 2 + state_shapes(width, block) * 2 + (
            jax.ShapeDtypeStruct((block, width), BF16),
            jax.ShapeDtypeStruct((block, width), BF16),
        ),
        in_specs=[VMEM] * 10,
        out_specs=(VMEM,) * 8,
        scratch_shapes=[
            pltpu.VMEM((block, depth), BF16),
            pltpu.VMEM((2 * PIECE, block), F32),
            pltpu.VMEM((2 * PIECE, PIECE), F32),
        ],
        compiler_params=params(OWN_MIB),
        cost_estimate=cost(5 * block * depth * width, 2**20, 0),
    )(info, info_pair, seg, gain, *pieces, w_own, w_pair)


def write_closed(states, send_ref, lse_ref, out_ref):
    width, block = states[0][1].shape
    half = block // 2
    sent = []
    for group, (stat, acc) in enumerate(states):
        total = stat[4:8, :]
        some = total > 0.0
        lse = jnp.where(some, stat[0:4, :] + jnp.log2(jnp.where(some, total, 1.0)), NEG_FILL)
        scale = jnp.where(some, 1.0 / jnp.where(some, total, 1.0), 0.0)
        lse_ref[4 * group : 4 * group + 4, :] = lse[:, :half]
        sent.append(lse[:, half:])
        for head in range(4):
            rows = pl.ds(head * HD, HD)
            to = pl.ds(group * width + head * HD, HD)
            normal = acc[rows, :] * scale[head : head + 1, :]
            out_ref[to, :] = normal[:, :half]
            send_ref[to, :] = normal[:, half:].astype(BF16)
    parts = list(three_addends(jnp.concatenate(sent, axis=0)))
    parts.append(jnp.zeros_like(parts[0]))
    send_ref[pl.ds(2 * width, 32), :] = jnp.concatenate(parts, axis=0).astype(BF16)


def earlier_pieces(which, closing, infos, seg, gain, pieces, w_own, w_pair, q_own, q_pair, state):
    depth, width = w_own.shape[1:]
    block = 4 * PIECE
    count = len(pieces)
    rows = len(which) * PIECE
    n_out = 3 if closing else 4

    def body(s0, s1, rest_ref, seg_ref, gain_ref, *refs):
        sources, refs = refs[:count], refs[count:]
        (w0, w1, q0, q1), before, refs = refs[:4], (refs[4:6], refs[6:8]), refs[8:]
        outs, (x, mask, dist, *inner) = refs[:n_out], refs[n_out:]
        after = inner if closing else outs
        after = (after[0:2], after[2:4])
        block_num = lax.axis_index("seq")
        block_base = block_num * block
        counts = s0[4:5, :] + s1[4:5, :] + rest_ref[4:5, :]
        start = block_base - jnp.max(counts).astype(jnp.int32)

        def key_base(i):
            def base(back, place):
                return block_base - back * block + place_of(place) * PIECE if back else -SPAN * block

            return jnp.where(block_num % 2 == 1, base(*which[i][1]), base(*which[i][0]))

        live = key_base(0) + PIECE > start
        for i in range(1, len(which)):
            live = live | (key_base(i) + PIECE > start)

        @pl.when(live)
        def _():
            set_earlier_masks(seg_ref, start, block_base, key_base, len(which), mask, dist)
            first = 0
            for source in sources:
                x[pl.ds(first, source.shape[0]), :] = normalise(source[...], gain_ref[...])
                first += source.shape[0]
            for group, (w, q) in enumerate(((w0, q0), (w1, q1))):
                keys = dot(x[...], w[1]).astype(BF16)
                v_t = dot(x[...], w[2]).T.astype(BF16)
                attend(keys, v_t, q, (s0, s1)[group], mask, dist, before[group], *after[group])

        @pl.when(jnp.logical_not(live))
        def _():
            for old, new in zip(before, after):
                new[0][...] = old[0][...]
                new[1][...] = old[1][...]

        if closing:
            write_closed(after, *outs)

    shapes = state_shapes(width, block) * 2
    scratch = [
        pltpu.VMEM((rows, depth), BF16),
        pltpu.VMEM((rows, block), F32),
        pltpu.VMEM((rows, PIECE), F32),
    ]
    if closing:
        scratch += [pltpu.VMEM(shape.shape, F32) for shape in shapes]
        shapes = (
            jax.ShapeDtypeStruct((2 * width + 32, block // 2), BF16),
            jax.ShapeDtypeStruct((8, block // 2), F32),
            jax.ShapeDtypeStruct((2 * width, block // 2), F32),
        )
    return pl.pallas_call(
        body,
        out_shape=shapes,
        in_specs=[VMEM] * (13 + count),
        out_specs=(VMEM,) * n_out,
        scratch_shapes=scratch,
        compiler_params=params(EARLIER_MIB),
        cost_estimate=cost(4 * rows * depth * width, 2**20, 0),
    )(*infos, seg, gain, *pieces, w_own, w_pair, q_own, q_pair, *state)


def project(place, lse, out, got, wo_own, wo_pair, tokens):
    wide = out.shape[0]
    width, model = wo_own.shape

    def body(lse_ref, out_ref, got_ref, w0, w1, *refs):
        y_ref, ctx = refs[-2:]
        lanes = pl.ds(place * PIECE, PIECE)
        other = got_ref[pl.ds(wide, 32), lanes].astype(F32)
        other = other[0:8] + other[8:16] + other[16:24]
        for head in range(8):
            swapped = (head + 4) % 8
            mine, theirs = lse_ref[head : head + 1, lanes], other[swapped : swapped + 1]
            top = jnp.maximum(mine, theirs)
            weigh, weigh_other = jnp.exp2(mine - top), jnp.exp2(theirs - top)
            joined = (out_ref[pl.ds(head * HD, HD), lanes] * weigh
                      + got_ref[pl.ds(swapped * HD, HD), lanes].astype(F32) * weigh_other)
            joined = joined / (weigh + weigh_other)
            ctx[:, head * HD : (head + 1) * HD] = joined.T.astype(BF16)
        result = dot(ctx[:, :width], w0[...]) + dot(ctx[:, width:], w1[...])
        if tokens is not None:
            result = result + refs[0][...].astype(F32)
        y_ref[...] = result.astype(y_ref.dtype)

    extra = () if tokens is None else (tokens,)
    return pl.pallas_call(
        body,
        out_shape=jax.ShapeDtypeStruct((PIECE, model), BF16 if tokens is None else F32),
        in_specs=[VMEM] * (5 + len(extra)),
        out_specs=VMEM,
        scratch_shapes=[pltpu.VMEM((PIECE, wide), BF16)],
        compiler_params=params(16),
        cost_estimate=cost(PIECE * wide * model, 2**20, 0),
    )(lse, out, got, wo_own, wo_pair, *extra)


def on_device(tokens, ln_gain, w_qkv, slopes, w_out, seg_ids):
    blocks = lax.axis_size("seq")
    block_num = lax.axis_index("seq")
    odd = (block_num % 2) == 1

    def over_core(value):
        return lax.ppermute(value, "head", [(i, i ^ 1) for i in range(4)])

    def over_x(value):
        return lax.ppermute(value, "head", [(i, i ^ 2) for i in range(4)])

    def over_seq(value, pairs):
        return lax.ppermute(value, "seq", pairs)

    two_on = [(i, i + 2) for i in range(blocks - 2)]
    even_to_odd = [(i, i + 1) for i in range(0, blocks, 2)]
    odd_to_even = [(i + 1, i) for i in range(0, blocks, 2)]

    tie = lax.optimization_barrier
    w_all = jnp.transpose(w_qkv, (1, 0, 2))
    seg = seg_ids.reshape(4, PIECE)
    gain = ln_gain.reshape(1, -1)
    w_pair = over_core(w_all)

    a2 = over_seq(tokens, two_on)
    b0 = over_x(tokens)
    a1_odd = over_seq(tokens, even_to_odd)
    c0 = over_core(tokens)
    seg_sent, w_staged, c0 = tie((seg, w_all, c0))
    w_staged = stage(w_staged)
    far_seg = lax.ppermute(
        seg_sent, ("seq", "head"),
        [(4 * i + head, 4 * (i + head + 1) + head) for head in range(SPAN) for i in range(blocks - head - 1)])
    info = count_back(slopes, seg, far_seg)
    info_pair = over_core(info)
    infos = [info, info_pair, over_x(add_counts(info, info_pair))]

    a2, b0, a1_odd, w_pair, w_staged, infos = tie((a2, b0, a1_odd, w_pair, w_staged, infos))
    a4 = over_seq(a2, two_on)
    b2 = over_x(a2)
    crossed = over_seq(a2, even_to_odd + odd_to_even)
    d0 = over_core(b0)
    q_own, q_pair, *state, key_cache, value_cache = own_block(
        *infos[:2], seg, gain, (tokens, b0, c0, d0), w_staged, w_pair)

    crossed, b2, a4, b0_sent, wo_sent, state[0] = tie((crossed, b2, a4, b0, w_out, state[0]))
    over_y = over_seq(pick(b0_sent, a4), even_to_odd + odd_to_even)
    x_third = over_x(crossed)
    b4 = over_seq(b2, two_on)
    wo_pair = over_core(wo_sent)

    def merge(closing, pieces, which, state):
        return earlier_pieces(
            which, closing, infos, seg, gain, pieces, w_staged, w_pair, q_own, q_pair, state)

    state = merge(
        False, (a2, b2, a4, crossed, a1_odd),
        (((2, 0),) * 2, ((2, 1),) * 2, ((4, 0),) * 2, ((1, 0), (3, 0)), ((0, 0), (1, 0))), state)

    over_y, x_third, b4, held = tie((over_y, x_third, b4, state[0]))
    state = (held, *state[1:])
    b3_top = over_x(over_y[: PIECE // 2])
    b3_rest = over_seq(b4[PIECE // 2 :], odd_to_even)
    state = merge(
        False, (b4, x_third, over_y), (((4, 1),) * 2, ((1, 1), (3, 1)), ((3, 0), (1, 1))), state)
    send, lse, out = merge(True, (b3_top, b3_rest), (((3, 1), (0, 0)),), state)
    got = over_core(send)
    y_pair = project(1, lse, out, got, w_out, wo_pair, None)
    y_got = over_x(y_pair)
    y_own = project(0, lse, out, got, w_out, wo_pair, tokens)
    hidden = (y_own + y_got.astype(F32)).astype(BF16)
    return (hidden, key_cache, value_cache)


def solution(mesh):
    in_specs = (
        P(("seq", "head"), None),
        P(),
        P(None, None, "head"),
        P("head"),
        P("head", None),
        P("seq"),
    )
    out_specs = (P(("seq", "head"), None), P("seq", "head"), P("seq", "head"))
    return jax.shard_map(
        on_device, mesh=mesh, in_specs=in_specs, out_specs=out_specs, check_vma=False
    )
```

```python
import jax
import jax.numpy as jnp
from jax import lax
from jax.experimental import pallas as pl
from jax.experimental.pallas import tpu as pltpu
from jax.sharding import PartitionSpec as P

HD = 128
SPAN = 4
PIECE = 128
EPSILON = 1e-05
NEG_FILL = -1e30
MASKED = -2e38
OWN_MIB = 16
EARLIER_MIB = 16
LOG2E = 1.4426950408889634

BF16 = jnp.bfloat16
F32 = jnp.float32
SMEM = pl.BlockSpec(memory_space=pltpu.SMEM)
HBM = pl.BlockSpec(memory_space=pltpu.HBM)
VMEM = pl.BlockSpec(memory_space=pltpu.VMEM)


def params(mebibytes):
    return pltpu.CompilerParams(vmem_limit_bytes=mebibytes * 2**20)


def cost(macs, nbytes, exps=0):
    return pl.CostEstimate(flops=2 * macs, bytes_accessed=nbytes, transcendentals=exps)


def dot(lhs, rhs):
    return jnp.dot(lhs, rhs, preferred_element_type=F32)


def three_addends(value):
    high = value.astype(BF16).astype(F32)
    middle = (value - high).astype(BF16).astype(F32)
    return high, middle, value - high - middle


def normalise(tokens, gain):
    inputs = tokens.astype(F32)
    centred = inputs - jnp.mean(inputs, axis=-1, keepdims=True)
    variance = jnp.mean(centred * centred, axis=-1, keepdims=True)
    return (centred * lax.rsqrt(variance + EPSILON) * gain).astype(BF16)


def count_back(slopes, seg, far_seg):
    def body(slopes_ref, seg_ref, far_ref, out_ref):
        there = lax.axis_index("seq") >= lax.axis_index("head") + 1
        same = jnp.where((far_ref[...] == seg_ref[0:1, 0:1]) & there, 1, 0)
        for head in range(4):
            out_ref[head : head + 1, :] = jnp.full((1, PIECE), slopes_ref[head], F32)
        out_ref[4:8, :] = jnp.full((4, PIECE), jnp.sum(same).astype(F32), F32)

    return pl.pallas_call(
        body,
        out_shape=jax.ShapeDtypeStruct((8, PIECE), F32),
        in_specs=[SMEM, VMEM, VMEM],
        out_specs=VMEM,
        compiler_params=params(4),
        cost_estimate=cost(0, 2**13),
    )(slopes, seg, far_seg)


def add_counts(mine, other):
    def body(mine_ref, other_ref, out_ref):
        out_ref[0:4, :] = mine_ref[0:4, :]
        out_ref[4:8, :] = mine_ref[4:8, :] + other_ref[4:8, :]

    return pl.pallas_call(
        body,
        out_shape=jax.ShapeDtypeStruct(mine.shape, F32),
        in_specs=[VMEM, VMEM],
        out_specs=VMEM,
        compiler_params=params(4),
        cost_estimate=cost(0, 2**13),
    )(mine, other)


def stage(weights):
    def body(source, out_ref, sem):
        copy = pltpu.make_async_copy(source, out_ref, sem)
        copy.start()
        copy.wait()

    return pl.pallas_call(
        body,
        out_shape=jax.ShapeDtypeStruct(weights.shape, weights.dtype),
        in_specs=[HBM],
        out_specs=VMEM,
        scratch_shapes=[pltpu.SemaphoreType.DMA],
        compiler_params=params(8),
        cost_estimate=cost(0, 2 * weights.size * 2),
    )(weights)


def pick(even_value, odd_value):
    def body(even_ref, odd_ref, out_ref):
        odd = lax.axis_index("seq") % 2 == 1

        @pl.when(odd)
        def _():
            out_ref[...] = odd_ref[...]

        @pl.when(jnp.logical_not(odd))
        def _():
            out_ref[...] = even_ref[...]

    return pl.pallas_call(
        body,
        out_shape=jax.ShapeDtypeStruct(even_value.shape, even_value.dtype),
        in_specs=[VMEM, VMEM],
        out_specs=VMEM,
        compiler_params=params(8),
        cost_estimate=cost(0, 2 * even_value.size * 2),
    )(even_value, odd_value)


def place_of(place):
    return lax.axis_index("head") ^ (0, 2, 1, 3)[place]


def set_distance(block_base, key_base, keys, dist_ref):
    row = lax.broadcasted_iota(jnp.int32, (PIECE, PIECE), 0)
    for piece in range(keys):
        dist_ref[pl.ds(piece * PIECE, PIECE), :] = (row + (key_base(piece) - block_base)).astype(F32)


def set_own_masks(seg_ref, mask_ref, dist_ref):
    lane = lax.broadcasted_iota(jnp.int32, (1, PIECE), 1)
    row = lax.broadcasted_iota(jnp.int32, (PIECE, PIECE), 0)
    set_distance(0, lambda i: place_of(i) * PIECE, 2, dist_ref)
    for piece in range(2):
        rows = pl.ds(piece * PIECE, PIECE)
        k_pos = row + place_of(piece) * PIECE
        key_seg = seg_ref[pl.ds(place_of(piece), 1), :]
        key_seg = jnp.broadcast_to(key_seg, (PIECE, PIECE)).T
        for place in range(4):
            q_pos = lane + place_of(place) * PIECE
            kept = (key_seg == seg_ref[pl.ds(place_of(place), 1), :]) & (k_pos <= q_pos)
            mask_ref[rows, pl.ds(place * PIECE, PIECE)] = jnp.where(kept, 0.0, MASKED)


def set_earlier_masks(seg_ref, start, block_base, key_base, keys, mask_ref, dist_ref):
    row = lax.broadcasted_iota(jnp.int32, (PIECE, PIECE), 0)
    set_distance(block_base, key_base, keys, dist_ref)
    first_seg = seg_ref[0:1, 0:1]
    for piece in range(keys):
        rows = pl.ds(piece * PIECE, PIECE)
        late = row + key_base(piece) >= start
        for place in range(4):
            kept = late & (seg_ref[pl.ds(place_of(place), 1), :] == first_seg)
            mask_ref[rows, pl.ds(place * PIECE, PIECE)] = jnp.where(kept, 0.0, MASKED)


def attend(k_rows, v_t, q_ref, slopes_ref, mask_ref, dist_ref, before, stat_ref, acc_ref):
    heads = k_rows.shape[1] // HD
    for head in range(heads):
        cols = slice(head * HD, (head + 1) * HD)
        wide = pl.ds(head * HD, HD)
        bias = dist_ref[...] * (slopes_ref[head : head + 1, :] * LOG2E)
        bias = jnp.concatenate([bias] * (q_ref.shape[1] // PIECE), axis=1)
        scores = dot(k_rows[:, cols], q_ref[wide, :]) * (HD**-0.5 * LOG2E)
        scores = scores + bias + mask_ref[...]
        top = jnp.max(scores, axis=0, keepdims=True)
        prev = jnp.full_like(top, NEG_FILL) if before is None else before[0][head : head + 1, :]
        row_max = jnp.maximum(prev, top)
        expo = jnp.exp2(scores - row_max)
        total = jnp.sum(expo, axis=0, keepdims=True)
        update = dot(v_t[cols, :], expo.astype(BF16))
        if before is not None:
            rescale = jnp.exp2(prev - row_max)
            total = before[0][4 + head : 5 + head, :] * rescale + total
            update = before[1][wide, :] * rescale + update
        stat_ref[head : head + 1, :] = row_max
        stat_ref[4 + head : 5 + head, :] = total
        acc_ref[wide, :] = update


def state_shapes(width, block):
    return (jax.ShapeDtypeStruct((8, block), F32), jax.ShapeDtypeStruct((width, block), F32))


def own_block(info, info_pair, seg, gain, pieces, w_own, w_pair):
    depth, width = w_own.shape[1:]
    block = 4 * PIECE

    def body(s0, s1, seg_ref, gain_ref, a, b, c, d, w0, w1, q0, q1, stat0, acc0, stat1, acc1, k_cache, v_cache,
             x, mask, dist):
        set_own_masks(seg_ref, mask, dist)
        for place, piece in enumerate((a, b, c, d)):
            x[pl.ds(place * PIECE, PIECE), :] = normalise(piece[...], gain_ref[...])
        for group, (w, q, stat, acc) in enumerate(((w0, q0, stat0, acc0), (w1, q1, stat1, acc1))):
            rows = block if group == 0 else 2 * PIECE
            q[...] = dot(x[...], w[0]).T.astype(BF16)
            keys = dot(x[:rows, :], w[1]).astype(BF16)
            values = dot(x[:rows, :], w[2])
            if group == 0:
                for place in range(4):
                    to = pl.ds(pl.multiple_of(place_of(place) * PIECE, PIECE), PIECE)
                    k_cache[to, :] = keys[place * PIECE : (place + 1) * PIECE]
                    v_cache[to, :] = values[place * PIECE : (place + 1) * PIECE].astype(BF16)
            v_t = values[: 2 * PIECE].T.astype(BF16)
            attend(keys[: 2 * PIECE], v_t, q, (s0, s1)[group], mask, dist, None, stat, acc)

    return pl.pallas_call(
        body,
        out_shape=(jax.ShapeDtypeStruct((width, block), BF16),) * 2 + state_shapes(width, block) * 2 + (
            jax.ShapeDtypeStruct((block, width), BF16),
            jax.ShapeDtypeStruct((block, width), BF16),
        ),
        in_specs=[VMEM] * 10,
        out_specs=(VMEM,) * 8,
        scratch_shapes=[
            pltpu.VMEM((block, depth), BF16),
            pltpu.VMEM((2 * PIECE, block), F32),
            pltpu.VMEM((2 * PIECE, PIECE), F32),
        ],
        compiler_params=params(OWN_MIB),
        cost_estimate=cost(5 * block * depth * width, 2**20, 0),
    )(info, info_pair, seg, gain, *pieces, w_own, w_pair)


def write_closed(states, send_ref, lse_ref, out_ref):
    width, block = states[0][1].shape
    half = block // 2
    sent = []
    for group, (stat, acc) in enumerate(states):
        total = stat[4:8, :]
        some = total > 0.0
        lse = jnp.where(some, stat[0:4, :] + jnp.log2(jnp.where(some, total, 1.0)), NEG_FILL)
        scale = jnp.where(some, 1.0 / jnp.where(some, total, 1.0), 0.0)
        lse_ref[4 * group : 4 * group + 4, :] = lse[:, :half]
        sent.append(lse[:, half:])
        for head in range(4):
            rows = pl.ds(head * HD, HD)
            to = pl.ds(group * width + head * HD, HD)
            normal = acc[rows, :] * scale[head : head + 1, :]
            out_ref[to, :] = normal[:, :half]
            send_ref[to, :] = normal[:, half:].astype(BF16)
    parts = list(three_addends(jnp.concatenate(sent, axis=0)))
    parts.append(jnp.zeros_like(parts[0]))
    send_ref[pl.ds(2 * width, 32), :] = jnp.concatenate(parts, axis=0).astype(BF16)


def earlier_pieces(which, closing, infos, seg, gain, pieces, w_own, w_pair, q_own, q_pair, state):
    depth, width = w_own.shape[1:]
    block = 4 * PIECE
    count = len(pieces)
    rows = len(which) * PIECE
    n_out = 3 if closing else 4

    def body(s0, s1, seg_ref, gain_ref, *refs):
        sources, refs = refs[:count], refs[count:]
        (w0, w1, q0, q1), before, refs = refs[:4], (refs[4:6], refs[6:8]), refs[8:]
        outs, (x, mask, dist, *inner) = refs[:n_out], refs[n_out:]
        after = inner if closing else outs
        after = (after[0:2], after[2:4])
        block_num = lax.axis_index("seq")
        block_base = block_num * block
        counts = s0[4:5, :] + s1[4:5, :]
        start = block_base - jnp.max(counts).astype(jnp.int32)

        def key_base(i):
            def base(back, place):
                return block_base - back * block + place_of(place) * PIECE if back else -SPAN * block

            return jnp.where(block_num % 2 == 1, base(*which[i][1]), base(*which[i][0]))

        live = key_base(0) + PIECE > start
        for i in range(1, len(which)):
            live = live | (key_base(i) + PIECE > start)

        @pl.when(live)
        def _():
            set_earlier_masks(seg_ref, start, block_base, key_base, len(which), mask, dist)
            first = 0
            for source in sources:
                x[pl.ds(first, source.shape[0]), :] = normalise(source[...], gain_ref[...])
                first += source.shape[0]
            for group, (w, q) in enumerate(((w0, q0), (w1, q1))):
                keys = dot(x[...], w[1]).astype(BF16)
                v_t = dot(x[...], w[2]).T.astype(BF16)
                attend(keys, v_t, q, (s0, s1)[group], mask, dist, before[group], *after[group])

        @pl.when(jnp.logical_not(live))
        def _():
            for old, new in zip(before, after):
                new[0][...] = old[0][...]
                new[1][...] = old[1][...]

        if closing:
            write_closed(after, *outs)

    shapes = state_shapes(width, block) * 2
    scratch = [
        pltpu.VMEM((rows, depth), BF16),
        pltpu.VMEM((rows, block), F32),
        pltpu.VMEM((rows, PIECE), F32),
    ]
    if closing:
        scratch += [pltpu.VMEM(shape.shape, F32) for shape in shapes]
        shapes = (
            jax.ShapeDtypeStruct((2 * width + 32, block // 2), BF16),
            jax.ShapeDtypeStruct((8, block // 2), F32),
            jax.ShapeDtypeStruct((2 * width, block // 2), F32),
        )
    return pl.pallas_call(
        body,
        out_shape=shapes,
        in_specs=[VMEM] * (12 + count),
        out_specs=(VMEM,) * n_out,
        scratch_shapes=scratch,
        compiler_params=params(EARLIER_MIB),
        cost_estimate=cost(4 * rows * depth * width, 2**20, 0),
    )(*infos, seg, gain, *pieces, w_own, w_pair, q_own, q_pair, *state)


def project(place, lse, out, got, wo_own, wo_pair, tokens):
    wide = out.shape[0]
    width, model = wo_own.shape

    def body(lse_ref, out_ref, got_ref, w0, w1, *refs):
        y_ref, ctx = refs[-2:]
        lanes = pl.ds(place * PIECE, PIECE)
        other = got_ref[pl.ds(wide, 32), lanes].astype(F32)
        other = other[0:8] + other[8:16] + other[16:24]
        for head in range(8):
            swapped = (head + 4) % 8
            mine, theirs = lse_ref[head : head + 1, lanes], other[swapped : swapped + 1]
            top = jnp.maximum(mine, theirs)
            weigh, weigh_other = jnp.exp2(mine - top), jnp.exp2(theirs - top)
            joined = (out_ref[pl.ds(head * HD, HD), lanes] * weigh
                      + got_ref[pl.ds(swapped * HD, HD), lanes].astype(F32) * weigh_other)
            joined = joined / (weigh + weigh_other)
            ctx[:, head * HD : (head + 1) * HD] = joined.T.astype(BF16)
        result = dot(ctx[:, :width], w0[...]) + dot(ctx[:, width:], w1[...])
        if tokens is not None:
            result = result + refs[0][...].astype(F32)
        y_ref[...] = result.astype(y_ref.dtype)

    extra = () if tokens is None else (tokens,)
    return pl.pallas_call(
        body,
        out_shape=jax.ShapeDtypeStruct((PIECE, model), BF16 if tokens is None else F32),
        in_specs=[VMEM] * (5 + len(extra)),
        out_specs=VMEM,
        scratch_shapes=[pltpu.VMEM((PIECE, wide), BF16)],
        compiler_params=params(16),
        cost_estimate=cost(PIECE * wide * model, 2**20, 0),
    )(lse, out, got, wo_own, wo_pair, *extra)


def on_device(tokens, ln_gain, w_qkv, slopes, w_out, seg_ids):
    blocks = lax.axis_size("seq")
    block_num = lax.axis_index("seq")
    odd = (block_num % 2) == 1

    def over_core(value):
        return lax.ppermute(value, "head", [(i, i ^ 1) for i in range(4)])

    def over_x(value):
        return lax.ppermute(value, "head", [(i, i ^ 2) for i in range(4)])

    def over_seq(value, pairs):
        return lax.ppermute(value, "seq", pairs)

    two_on = [(i, i + 2) for i in range(blocks - 2)]
    even_to_odd = [(i, i + 1) for i in range(0, blocks, 2)]
    odd_to_even = [(i + 1, i) for i in range(0, blocks, 2)]

    tie = lax.optimization_barrier
    w_all = jnp.transpose(w_qkv, (1, 0, 2))
    seg = seg_ids.reshape(4, PIECE)
    gain = ln_gain.reshape(1, -1)
    far_seg = lax.ppermute(
        seg, ("seq", "head"),
        [(4 * i + head, 4 * (i + head + 1) + head) for head in range(SPAN) for i in range(blocks - head - 1)])
    w_pair = over_core(w_all)

    a2 = over_seq(tokens, two_on)
    b0 = over_x(tokens)
    a1_odd = over_seq(tokens, even_to_odd)
    c0 = over_core(tokens)
    info = count_back(slopes, seg, far_seg)
    info_x = over_x(info)
    info_x, w_staged = tie((info_x, w_all))
    w_staged = stage(w_staged)
    info = add_counts(info, info_x)
    infos = [info, over_core(info)]

    a2, b0, a1_odd, w_pair, w_staged, infos = tie((a2, b0, a1_odd, w_pair, w_staged, infos))
    a4 = over_seq(a2, two_on)
    b2 = over_x(a2)
    crossed = over_seq(a2, even_to_odd + odd_to_even)
    d0 = over_core(b0)
    q_own, q_pair, *state, key_cache, value_cache = own_block(
        *infos, seg, gain, (tokens, b0, c0, d0), w_staged, w_pair)

    crossed, b2, a4, b0_sent, wo_sent, state[0] = tie((crossed, b2, a4, b0, w_out, state[0]))
    over_y = over_seq(pick(b0_sent, a4), even_to_odd + odd_to_even)
    x_third = over_x(crossed)
    b4 = over_seq(b2, two_on)
    wo_pair = over_core(wo_sent)

    def merge(closing, pieces, which, state):
        return earlier_pieces(
            which, closing, infos, seg, gain, pieces, w_staged, w_pair, q_own, q_pair, state)

    state = merge(
        False, (a2, b2, a4, crossed, a1_odd),
        (((2, 0),) * 2, ((2, 1),) * 2, ((4, 0),) * 2, ((1, 0), (3, 0)), ((0, 0), (1, 0))), state)

    over_y, x_third, b4, held = tie((over_y, x_third, b4, state[0]))
    state = (held, *state[1:])
    b3_top = over_x(over_y[: PIECE // 2])
    b3_rest = over_seq(b4[PIECE // 2 :], odd_to_even)
    state = merge(
        False, (b4, x_third, over_y), (((4, 1),) * 2, ((1, 1), (3, 1)), ((3, 0), (1, 1))), state)
    send, lse, out = merge(True, (b3_top, b3_rest), (((3, 1), (0, 0)),), state)
    got = over_core(send)
    y_pair = project(1, lse, out, got, w_out, wo_pair, None)
    y_got = over_x(y_pair)
    y_own = project(0, lse, out, got, w_out, wo_pair, tokens)
    hidden = (y_own + y_got.astype(F32)).astype(BF16)
    return (hidden, key_cache, value_cache)


def solution(mesh):
    in_specs = (
        P(("seq", "head"), None),
        P(),
        P(None, None, "head"),
        P("head"),
        P("head", None),
        P("seq"),
    )
    out_specs = (P(("seq", "head"), None), P("seq", "head"), P("seq", "head"))
    return jax.shard_map(
        on_device, mesh=mesh, in_specs=in_specs, out_specs=out_specs, check_vma=False
    )
```

```python
import jax
import jax.numpy as jnp
from jax import lax
from jax.experimental import pallas as pl
from jax.experimental.pallas import tpu as pltpu
from jax.sharding import PartitionSpec as P

HD = 128
SPAN = 4
PIECE = 128
EPSILON = 1e-05
NEG_FILL = -1e30
MASKED = -2e38
OWN_MIB = 16
EARLIER_MIB = 16
LOG2E = 1.4426950408889634

BF16 = jnp.bfloat16
F32 = jnp.float32
SMEM = pl.BlockSpec(memory_space=pltpu.SMEM)
HBM = pl.BlockSpec(memory_space=pltpu.HBM)
VMEM = pl.BlockSpec(memory_space=pltpu.VMEM)


def params(mebibytes):
    return pltpu.CompilerParams(vmem_limit_bytes=mebibytes * 2**20)


def cost(macs, nbytes, exps=0):
    return pl.CostEstimate(flops=2 * macs, bytes_accessed=nbytes, transcendentals=exps)


def dot(lhs, rhs):
    return jnp.dot(lhs, rhs, preferred_element_type=F32)


def three_addends(value):
    high = value.astype(BF16).astype(F32)
    middle = (value - high).astype(BF16).astype(F32)
    return high, middle, value - high - middle


def normalise(tokens, gain):
    inputs = tokens.astype(F32)
    centred = inputs - jnp.mean(inputs, axis=-1, keepdims=True)
    variance = jnp.mean(centred * centred, axis=-1, keepdims=True)
    return (centred * lax.rsqrt(variance + EPSILON) * gain).astype(BF16)


def stage(weights):
    def body(source, out_ref, sem):
        copy = pltpu.make_async_copy(source, out_ref, sem)
        copy.start()
        copy.wait()

    return pl.pallas_call(
        body,
        out_shape=jax.ShapeDtypeStruct(weights.shape, weights.dtype),
        in_specs=[HBM],
        out_specs=VMEM,
        scratch_shapes=[pltpu.SemaphoreType.DMA],
        compiler_params=params(8),
        cost_estimate=cost(0, 2 * weights.size * 2),
    )(weights)


def pick(even_value, odd_value):
    def body(even_ref, odd_ref, out_ref):
        odd = lax.axis_index("seq") % 2 == 1

        @pl.when(odd)
        def _():
            out_ref[...] = odd_ref[...]

        @pl.when(jnp.logical_not(odd))
        def _():
            out_ref[...] = even_ref[...]

    return pl.pallas_call(
        body,
        out_shape=jax.ShapeDtypeStruct(even_value.shape, even_value.dtype),
        in_specs=[VMEM, VMEM],
        out_specs=VMEM,
        compiler_params=params(8),
        cost_estimate=cost(0, 2 * even_value.size * 2),
    )(even_value, odd_value)


def place_of(place):
    return lax.axis_index("head") ^ (0, 2, 1, 3)[place]


def set_distance(block_base, key_base, keys, dist_ref):
    row = lax.broadcasted_iota(jnp.int32, (PIECE, PIECE), 0)
    for piece in range(keys):
        dist_ref[pl.ds(piece * PIECE, PIECE), :] = (row + (key_base(piece) - block_base)).astype(F32)


def set_own_masks(seg_ref, mask_ref, dist_ref):
    lane = lax.broadcasted_iota(jnp.int32, (1, PIECE), 1)
    row = lax.broadcasted_iota(jnp.int32, (PIECE, PIECE), 0)
    set_distance(0, lambda i: place_of(i) * PIECE, 2, dist_ref)
    for piece in range(2):
        rows = pl.ds(piece * PIECE, PIECE)
        k_pos = row + place_of(piece) * PIECE
        key_seg = seg_ref[pl.ds(place_of(piece), 1), :]
        key_seg = jnp.broadcast_to(key_seg, (PIECE, PIECE)).T
        for place in range(4):
            q_pos = lane + place_of(place) * PIECE
            kept = (key_seg == seg_ref[pl.ds(place_of(place), 1), :]) & (k_pos <= q_pos)
            mask_ref[rows, pl.ds(place * PIECE, PIECE)] = jnp.where(kept, 0.0, MASKED)


def set_earlier_masks(seg_ref, start, block_base, key_base, keys, mask_ref, dist_ref):
    row = lax.broadcasted_iota(jnp.int32, (PIECE, PIECE), 0)
    set_distance(block_base, key_base, keys, dist_ref)
    first_seg = seg_ref[0:1, 0:1]
    for piece in range(keys):
        rows = pl.ds(piece * PIECE, PIECE)
        late = row + key_base(piece) >= start
        for place in range(4):
            kept = late & (seg_ref[pl.ds(place_of(place), 1), :] == first_seg)
            mask_ref[rows, pl.ds(place * PIECE, PIECE)] = jnp.where(kept, 0.0, MASKED)


def attend(k_rows, v_t, q_ref, slopes_ref, mask_ref, dist_ref, before, stat_ref, acc_ref):
    heads = k_rows.shape[1] // HD
    for head in range(heads):
        cols = slice(head * HD, (head + 1) * HD)
        wide = pl.ds(head * HD, HD)
        bias = dist_ref[...] * (slopes_ref[head] * LOG2E)
        bias = jnp.concatenate([bias] * (q_ref.shape[1] // PIECE), axis=1)
        scores = dot(k_rows[:, cols], q_ref[wide, :]) * (HD**-0.5 * LOG2E)
        scores = scores + bias + mask_ref[...]
        top = jnp.max(scores, axis=0, keepdims=True)
        prev = jnp.full_like(top, NEG_FILL) if before is None else before[0][head : head + 1, :]
        row_max = jnp.maximum(prev, top)
        expo = jnp.exp2(scores - row_max)
        total = jnp.sum(expo, axis=0, keepdims=True)
        update = dot(v_t[cols, :], expo.astype(BF16))
        if before is not None:
            rescale = jnp.exp2(prev - row_max)
            total = before[0][4 + head : 5 + head, :] * rescale + total
            update = before[1][wide, :] * rescale + update
        stat_ref[head : head + 1, :] = row_max
        stat_ref[4 + head : 5 + head, :] = total
        acc_ref[wide, :] = update


def state_shapes(width, block):
    return (jax.ShapeDtypeStruct((8, block), F32), jax.ShapeDtypeStruct((width, block), F32))


def own_block(slopes, slopes_pair, seg, gain, pieces, w_own, w_pair):
    depth, width = w_own.shape[1:]
    block = 4 * PIECE

    def body(s0, s1, seg_ref, gain_ref, a, b, c, d, w0, w1, q0, q1, stat0, acc0, stat1, acc1, k_cache, v_cache,
             x, mask, dist):
        set_own_masks(seg_ref, mask, dist)
        for place, piece in enumerate((a, b, c, d)):
            x[pl.ds(place * PIECE, PIECE), :] = normalise(piece[...], gain_ref[...])
        for group, (w, q, stat, acc) in enumerate(((w0, q0, stat0, acc0), (w1, q1, stat1, acc1))):
            rows = block if group == 0 else 2 * PIECE
            q[...] = dot(x[...], w[0]).T.astype(BF16)
            keys = dot(x[:rows, :], w[1]).astype(BF16)
            values = dot(x[:rows, :], w[2])
            if group == 0:
                for place in range(4):
                    to = pl.ds(pl.multiple_of(place_of(place) * PIECE, PIECE), PIECE)
                    k_cache[to, :] = keys[place * PIECE : (place + 1) * PIECE]
                    v_cache[to, :] = values[place * PIECE : (place + 1) * PIECE].astype(BF16)
            v_t = values[: 2 * PIECE].T.astype(BF16)
            attend(keys[: 2 * PIECE], v_t, q, (s0, s1)[group], mask, dist, None, stat, acc)

    return pl.pallas_call(
        body,
        out_shape=(jax.ShapeDtypeStruct((width, block), BF16),) * 2 + state_shapes(width, block) * 2 + (
            jax.ShapeDtypeStruct((block, width), BF16),
            jax.ShapeDtypeStruct((block, width), BF16),
        ),
        in_specs=[SMEM] * 2 + [VMEM] * 8,
        out_specs=(VMEM,) * 8,
        scratch_shapes=[
            pltpu.VMEM((block, depth), BF16),
            pltpu.VMEM((2 * PIECE, block), F32),
            pltpu.VMEM((2 * PIECE, PIECE), F32),
        ],
        compiler_params=params(OWN_MIB),
        cost_estimate=cost(5 * block * depth * width, 2**20, 0),
    )(slopes, slopes_pair, seg, gain, *pieces, w_own, w_pair)


def write_closed(states, send_ref, lse_ref, out_ref):
    width, block = states[0][1].shape
    half = block // 2
    sent = []
    for group, (stat, acc) in enumerate(states):
        total = stat[4:8, :]
        some = total > 0.0
        lse = jnp.where(some, stat[0:4, :] + jnp.log2(jnp.where(some, total, 1.0)), NEG_FILL)
        scale = jnp.where(some, 1.0 / jnp.where(some, total, 1.0), 0.0)
        lse_ref[4 * group : 4 * group + 4, :] = lse[:, :half]
        sent.append(lse[:, half:])
        for head in range(4):
            rows = pl.ds(head * HD, HD)
            to = pl.ds(group * width + head * HD, HD)
            normal = acc[rows, :] * scale[head : head + 1, :]
            out_ref[to, :] = normal[:, :half]
            send_ref[to, :] = normal[:, half:].astype(BF16)
    parts = list(three_addends(jnp.concatenate(sent, axis=0)))
    parts.append(jnp.zeros_like(parts[0]))
    send_ref[pl.ds(2 * width, 32), :] = jnp.concatenate(parts, axis=0).astype(BF16)


def earlier_pieces(which, closing, slopes, slopes_pair, seg, segs, gain, pieces, w_own, w_pair, q_own, q_pair, state):
    depth, width = w_own.shape[1:]
    block = 4 * PIECE
    count = len(pieces)
    rows = len(which) * PIECE
    n_out = 3 if closing else 4

    def body(s0, s1, seg_ref, gain_ref, *refs):
        seg_refs, refs = refs[: len(segs)], refs[len(segs) :]
        sources, refs = refs[:count], refs[count:]
        (w0, w1, q0, q1), before, refs = refs[:4], (refs[4:6], refs[6:8]), refs[8:]
        outs, (x, mask, dist, *inner) = refs[:n_out], refs[n_out:]
        after = inner if closing else outs
        after = (after[0:2], after[2:4])
        block_num = lax.axis_index("seq")
        block_base = block_num * block
        same = jnp.zeros(seg_ref.shape, jnp.int32)
        for back, ref in enumerate(seg_refs, 1):
            same = same + jnp.where((ref[...] == seg_ref[0:1, 0:1]) & (block_num >= back), 1, 0)
        start = block_base - jnp.sum(same)

        def key_base(i):
            def base(back, place):
                return block_base - back * block + place_of(place) * PIECE if back else -SPAN * block

            return jnp.where(block_num % 2 == 1, base(*which[i][1]), base(*which[i][0]))

        live = key_base(0) + PIECE > start
        for i in range(1, len(which)):
            live = live | (key_base(i) + PIECE > start)

        @pl.when(live)
        def _():
            set_earlier_masks(seg_ref, start, block_base, key_base, len(which), mask, dist)
            first = 0
            for source in sources:
                x[pl.ds(first, source.shape[0]), :] = normalise(source[...], gain_ref[...])
                first += source.shape[0]
            for group, (w, q) in enumerate(((w0, q0), (w1, q1))):
                keys = dot(x[...], w[1]).astype(BF16)
                v_t = dot(x[...], w[2]).T.astype(BF16)
                attend(keys, v_t, q, (s0, s1)[group], mask, dist, before[group], *after[group])

        @pl.when(jnp.logical_not(live))
        def _():
            for old, new in zip(before, after):
                new[0][...] = old[0][...]
                new[1][...] = old[1][...]

        if closing:
            write_closed(after, *outs)

    shapes = state_shapes(width, block) * 2
    scratch = [
        pltpu.VMEM((rows, depth), BF16),
        pltpu.VMEM((rows, block), F32),
        pltpu.VMEM((rows, PIECE), F32),
    ]
    if closing:
        scratch += [pltpu.VMEM(shape.shape, F32) for shape in shapes]
        shapes = (
            jax.ShapeDtypeStruct((2 * width + 32, block // 2), BF16),
            jax.ShapeDtypeStruct((8, block // 2), F32),
            jax.ShapeDtypeStruct((2 * width, block // 2), F32),
        )
    return pl.pallas_call(
        body,
        out_shape=shapes,
        in_specs=[SMEM] * 2 + [VMEM] * (10 + len(segs) + count),
        out_specs=(VMEM,) * n_out,
        scratch_shapes=scratch,
        compiler_params=params(EARLIER_MIB),
        cost_estimate=cost(4 * rows * depth * width, 2**20, 0),
    )(slopes, slopes_pair, seg, gain, *segs, *pieces, w_own, w_pair, q_own, q_pair, *state)


def project(place, lse, out, got, wo_own, wo_pair, tokens):
    wide = out.shape[0]
    width, model = wo_own.shape

    def body(lse_ref, out_ref, got_ref, w0, w1, *refs):
        y_ref, ctx = refs[-2:]
        lanes = pl.ds(place * PIECE, PIECE)
        other = got_ref[pl.ds(wide, 32), lanes].astype(F32)
        other = other[0:8] + other[8:16] + other[16:24]
        for head in range(8):
            swapped = (head + 4) % 8
            mine, theirs = lse_ref[head : head + 1, lanes], other[swapped : swapped + 1]
            top = jnp.maximum(mine, theirs)
            weigh, weigh_other = jnp.exp2(mine - top), jnp.exp2(theirs - top)
            joined = (out_ref[pl.ds(head * HD, HD), lanes] * weigh
                      + got_ref[pl.ds(swapped * HD, HD), lanes].astype(F32) * weigh_other)
            joined = joined / (weigh + weigh_other)
            ctx[:, head * HD : (head + 1) * HD] = joined.T.astype(BF16)
        result = dot(ctx[:, :width], w0[...]) + dot(ctx[:, width:], w1[...])
        if tokens is not None:
            result = result + refs[0][...].astype(F32)
        y_ref[...] = result.astype(y_ref.dtype)

    extra = () if tokens is None else (tokens,)
    return pl.pallas_call(
        body,
        out_shape=jax.ShapeDtypeStruct((PIECE, model), BF16 if tokens is None else F32),
        in_specs=[VMEM] * (5 + len(extra)),
        out_specs=VMEM,
        scratch_shapes=[pltpu.VMEM((PIECE, wide), BF16)],
        compiler_params=params(16),
        cost_estimate=cost(PIECE * wide * model, 2**20, 0),
    )(lse, out, got, wo_own, wo_pair, *extra)


def on_device(tokens, ln_gain, w_qkv, slopes, w_out, seg_ids):
    blocks = lax.axis_size("seq")
    block_num = lax.axis_index("seq")
    odd = (block_num % 2) == 1

    def over_core(value):
        return lax.ppermute(value, "head", [(i, i ^ 1) for i in range(4)])

    def over_x(value):
        return lax.ppermute(value, "head", [(i, i ^ 2) for i in range(4)])

    def over_seq(value, pairs):
        return lax.ppermute(value, "seq", pairs)

    two_on = [(i, i + 2) for i in range(blocks - 2)]
    even_to_odd = [(i, i + 1) for i in range(0, blocks, 2)]
    odd_to_even = [(i + 1, i) for i in range(0, blocks, 2)]

    tie = lax.optimization_barrier
    w_all = jnp.transpose(w_qkv, (1, 0, 2))
    seg = seg_ids.reshape(4, PIECE)
    gain = ln_gain.reshape(1, -1)
    w_pair = over_core(w_all)

    a2 = over_seq(tokens, two_on)
    b0 = over_x(tokens)
    a1_odd = over_seq(tokens, even_to_odd)
    c0 = over_core(tokens)
    slopes_sent, w_staged, c0 = tie((slopes, w_all, c0))
    slopes_pair = over_core(slopes_sent)
    seg_sent, slopes_pair = tie((seg, slopes_pair))
    seg1 = over_seq(seg_sent, [(i, i + 1) for i in range(blocks - 1)])
    w_staged = stage(w_staged)

    a2, b0, a1_odd, w_pair, w_staged, slopes_pair, seg1 = tie(
        (a2, b0, a1_odd, w_pair, w_staged, slopes_pair, seg1))
    a4 = over_seq(a2, two_on)
    b2 = over_x(a2)
    crossed = over_seq(a2, even_to_odd + odd_to_even)
    d0 = over_core(b0)
    seg23 = over_seq(jnp.concatenate([seg, seg1], axis=0), two_on)
    segs = [seg1, seg23[:4], seg23[4:]]
    q_own, q_pair, *state, key_cache, value_cache = own_block(
        slopes, slopes_pair, seg, gain, (tokens, b0, c0, d0), w_staged, w_pair)

    crossed, b2, a4, b0_sent, wo_sent, segs, state[0] = tie((crossed, b2, a4, b0, w_out, segs, state[0]))
    over_y = over_seq(pick(b0_sent, a4), even_to_odd + odd_to_even)
    x_third = over_x(crossed)
    b4 = over_seq(b2, two_on)
    seg4 = over_seq(segs[1], two_on)
    wo_pair = over_core(wo_sent)

    def merge(closing, segs, pieces, which, state):
        return earlier_pieces(
            which, closing, slopes, slopes_pair, seg, segs, gain, pieces, w_staged, w_pair, q_own, q_pair, state)

    state = merge(
        False, segs, (a2, b2, crossed, a1_odd),
        (((2, 0),) * 2, ((2, 1),) * 2, ((1, 0), (3, 0)), ((0, 0), (1, 0))), state)

    over_y, x_third, b4, seg4, held = tie((over_y, x_third, b4, seg4, state[0]))
    segs = [*segs, seg4]
    state = (held, *state[1:])
    b3_top = over_x(over_y[: PIECE // 2])
    b3_rest = over_seq(b4[PIECE // 2 :], odd_to_even)
    state = merge(
        False, segs, (a4, b4, x_third, over_y),
        (((4, 0),) * 2, ((4, 1),) * 2, ((1, 1), (3, 1)), ((3, 0), (1, 1))), state)
    send, lse, out = merge(True, segs, (b3_top, b3_rest), (((3, 1), (0, 0)),), state)
    got = over_core(send)
    y_pair = project(1, lse, out, got, w_out, wo_pair, None)
    y_got = over_x(y_pair)
    y_own = project(0, lse, out, got, w_out, wo_pair, tokens)
    hidden = (y_own + y_got.astype(F32)).astype(BF16)
    return (hidden, key_cache, value_cache)


def solution(mesh):
    in_specs = (
        P(("seq", "head"), None),
        P(),
        P(None, None, "head"),
        P("head"),
        P("head", None),
        P("seq"),
    )
    out_specs = (P(("seq", "head"), None), P("seq", "head"), P("seq", "head"))
    return jax.shard_map(
        on_device, mesh=mesh, in_specs=in_specs, out_specs=out_specs, check_vma=False
    )
```

```python
import jax
import jax.numpy as jnp
from jax import lax
from jax.experimental import pallas as pl
from jax.experimental.pallas import tpu as pltpu
from jax.sharding import PartitionSpec as P

HD = 128
SPAN = 4
PIECE = 128
EPSILON = 1e-05
NEG_FILL = -1e30
MASKED = -2e38
OWN_MIB = 16
EARLIER_MIB = 16
LOG2E = 1.4426950408889634

BF16 = jnp.bfloat16
F32 = jnp.float32
SMEM = pl.BlockSpec(memory_space=pltpu.SMEM)
HBM = pl.BlockSpec(memory_space=pltpu.HBM)
VMEM = pl.BlockSpec(memory_space=pltpu.VMEM)


def params(mebibytes):
    return pltpu.CompilerParams(vmem_limit_bytes=mebibytes * 2**20)


def cost(macs, nbytes, exps=0):
    return pl.CostEstimate(flops=2 * macs, bytes_accessed=nbytes, transcendentals=exps)


def dot(lhs, rhs):
    return jnp.dot(lhs, rhs, preferred_element_type=F32)


def three_addends(value):
    high = value.astype(BF16).astype(F32)
    middle = (value - high).astype(BF16).astype(F32)
    return high, middle, value - high - middle


def normalise(tokens, gain):
    inputs = tokens.astype(F32)
    centred = inputs - jnp.mean(inputs, axis=-1, keepdims=True)
    variance = jnp.mean(centred * centred, axis=-1, keepdims=True)
    return (centred * lax.rsqrt(variance + EPSILON) * gain).astype(BF16)


def stage(weights):
    def body(source, out_ref, sem):
        copy = pltpu.make_async_copy(source, out_ref, sem)
        copy.start()
        copy.wait()

    return pl.pallas_call(
        body,
        out_shape=jax.ShapeDtypeStruct(weights.shape, weights.dtype),
        in_specs=[HBM],
        out_specs=VMEM,
        scratch_shapes=[pltpu.SemaphoreType.DMA],
        compiler_params=params(8),
        cost_estimate=cost(0, 2 * weights.size * 2),
    )(weights)


def pick(even_value, odd_value):
    def body(even_ref, odd_ref, out_ref):
        odd = lax.axis_index("seq") % 2 == 1

        @pl.when(odd)
        def _():
            out_ref[...] = odd_ref[...]

        @pl.when(jnp.logical_not(odd))
        def _():
            out_ref[...] = even_ref[...]

    return pl.pallas_call(
        body,
        out_shape=jax.ShapeDtypeStruct(even_value.shape, even_value.dtype),
        in_specs=[VMEM, VMEM],
        out_specs=VMEM,
        compiler_params=params(8),
        cost_estimate=cost(0, 2 * even_value.size * 2),
    )(even_value, odd_value)


def place_of(place):
    return lax.axis_index("head") ^ (0, 2, 1, 3)[place]


def set_distance(block_base, key_base, keys, dist_ref):
    row = lax.broadcasted_iota(jnp.int32, (PIECE, PIECE), 0)
    for piece in range(keys):
        dist_ref[pl.ds(piece * PIECE, PIECE), :] = (row + (key_base(piece) - block_base)).astype(F32)


def set_own_masks(seg_ref, mask_ref, dist_ref):
    lane = lax.broadcasted_iota(jnp.int32, (1, PIECE), 1)
    row = lax.broadcasted_iota(jnp.int32, (PIECE, PIECE), 0)
    set_distance(0, lambda i: place_of(i) * PIECE, 2, dist_ref)
    for piece in range(2):
        rows = pl.ds(piece * PIECE, PIECE)
        k_pos = row + place_of(piece) * PIECE
        key_seg = seg_ref[pl.ds(place_of(piece), 1), :]
        key_seg = jnp.broadcast_to(key_seg, (PIECE, PIECE)).T
        for place in range(4):
            q_pos = lane + place_of(place) * PIECE
            kept = (key_seg == seg_ref[pl.ds(place_of(place), 1), :]) & (k_pos <= q_pos)
            mask_ref[rows, pl.ds(place * PIECE, PIECE)] = jnp.where(kept, 0.0, MASKED)


def set_earlier_masks(seg_ref, start, block_base, key_base, keys, mask_ref, dist_ref):
    row = lax.broadcasted_iota(jnp.int32, (PIECE, PIECE), 0)
    set_distance(block_base, key_base, keys, dist_ref)
    first_seg = seg_ref[0:1, 0:1]
    for piece in range(keys):
        rows = pl.ds(piece * PIECE, PIECE)
        late = row + key_base(piece) >= start
        for place in range(4):
            kept = late & (seg_ref[pl.ds(place_of(place), 1), :] == first_seg)
            mask_ref[rows, pl.ds(place * PIECE, PIECE)] = jnp.where(kept, 0.0, MASKED)


def attend(k_rows, v_t, q_ref, slopes_ref, mask_ref, dist_ref, before, stat_ref, acc_ref):
    heads = k_rows.shape[1] // HD
    for head in range(heads):
        cols = slice(head * HD, (head + 1) * HD)
        wide = pl.ds(head * HD, HD)
        bias = dist_ref[...] * (slopes_ref[head : head + 1, :] * LOG2E)
        bias = jnp.concatenate([bias] * (q_ref.shape[1] // PIECE), axis=1)
        scores = dot(k_rows[:, cols], q_ref[wide, :]) * (HD**-0.5 * LOG2E)
        scores = scores + bias + mask_ref[...]
        top = jnp.max(scores, axis=0, keepdims=True)
        prev = jnp.full_like(top, NEG_FILL) if before is None else before[0][head : head + 1, :]
        row_max = jnp.maximum(prev, top)
        expo = jnp.exp2(scores - row_max)
        total = jnp.sum(expo, axis=0, keepdims=True)
        update = dot(v_t[cols, :], expo.astype(BF16))
        if before is not None:
            rescale = jnp.exp2(prev - row_max)
            total = before[0][4 + head : 5 + head, :] * rescale + total
            update = before[1][wide, :] * rescale + update
        stat_ref[head : head + 1, :] = row_max
        stat_ref[4 + head : 5 + head, :] = total
        acc_ref[wide, :] = update


def state_shapes(width, block):
    return (jax.ShapeDtypeStruct((8, block), F32), jax.ShapeDtypeStruct((width, block), F32))


def own_block(slopes, slopes_pair, seg, gain, pieces, w_own, w_pair):
    depth, width = w_own.shape[1:]
    block = 4 * PIECE

    def body(s0, s1, seg_ref, gain_ref, a, b, c, d, w0, w1, q0, q1, stat0, acc0, stat1, acc1, k_cache, v_cache,
             slopes_out, x, mask, dist):
        set_own_masks(seg_ref, mask, dist)
        for head in range(4):
            slopes_out[head : head + 1, :] = jnp.full((1, PIECE), s0[head], F32)
            slopes_out[4 + head : 5 + head, :] = jnp.full((1, PIECE), s1[head], F32)
        for place, piece in enumerate((a, b, c, d)):
            x[pl.ds(place * PIECE, PIECE), :] = normalise(piece[...], gain_ref[...])
        for group, (w, q, stat, acc) in enumerate(((w0, q0, stat0, acc0), (w1, q1, stat1, acc1))):
            rows = block if group == 0 else 2 * PIECE
            q[...] = dot(x[...], w[0]).T.astype(BF16)
            keys = dot(x[:rows, :], w[1]).astype(BF16)
            values = dot(x[:rows, :], w[2])
            if group == 0:
                for place in range(4):
                    to = pl.ds(pl.multiple_of(place_of(place) * PIECE, PIECE), PIECE)
                    k_cache[to, :] = keys[place * PIECE : (place + 1) * PIECE]
                    v_cache[to, :] = values[place * PIECE : (place + 1) * PIECE].astype(BF16)
            v_t = values[: 2 * PIECE].T.astype(BF16)
            attend(keys[: 2 * PIECE], v_t, q, slopes_out.at[pl.ds(4 * group, 4)], mask, dist, None, stat, acc)

    return pl.pallas_call(
        body,
        out_shape=(jax.ShapeDtypeStruct((width, block), BF16),) * 2 + state_shapes(width, block) * 2 + (
            jax.ShapeDtypeStruct((block, width), BF16),
            jax.ShapeDtypeStruct((block, width), BF16),
            jax.ShapeDtypeStruct((8, PIECE), F32),
        ),
        in_specs=[SMEM] * 2 + [VMEM] * 8,
        out_specs=(VMEM,) * 9,
        scratch_shapes=[
            pltpu.VMEM((block, depth), BF16),
            pltpu.VMEM((2 * PIECE, block), F32),
            pltpu.VMEM((2 * PIECE, PIECE), F32),
        ],
        compiler_params=params(OWN_MIB),
        cost_estimate=cost(5 * block * depth * width, 2**20, 0),
    )(slopes, slopes_pair, seg, gain, *pieces, w_own, w_pair)


def write_closed(states, send_ref, lse_ref, out_ref):
    width, block = states[0][1].shape
    half = block // 2
    sent = []
    for group, (stat, acc) in enumerate(states):
        total = stat[4:8, :]
        some = total > 0.0
        lse = jnp.where(some, stat[0:4, :] + jnp.log2(jnp.where(some, total, 1.0)), NEG_FILL)
        scale = jnp.where(some, 1.0 / jnp.where(some, total, 1.0), 0.0)
        lse_ref[4 * group : 4 * group + 4, :] = lse[:, :half]
        sent.append(lse[:, half:])
        for head in range(4):
            rows = pl.ds(head * HD, HD)
            to = pl.ds(group * width + head * HD, HD)
            normal = acc[rows, :] * scale[head : head + 1, :]
            out_ref[to, :] = normal[:, :half]
            send_ref[to, :] = normal[:, half:].astype(BF16)
    parts = list(three_addends(jnp.concatenate(sent, axis=0)))
    parts.append(jnp.zeros_like(parts[0]))
    send_ref[pl.ds(2 * width, 32), :] = jnp.concatenate(parts, axis=0).astype(BF16)


def earlier_pieces(which, closing, slopes8, seg, segs, gain, pieces, w_own, w_pair, q_own, q_pair, state):
    depth, width = w_own.shape[1:]
    block = 4 * PIECE
    count = len(pieces)
    rows = len(which) * PIECE
    n_out = 3 if closing else 4

    def body(slopes_ref, seg_ref, gain_ref, *refs):
        seg_refs, refs = refs[: len(segs)], refs[len(segs) :]
        sources, refs = refs[:count], refs[count:]
        (w0, w1, q0, q1), before, refs = refs[:4], (refs[4:6], refs[6:8]), refs[8:]
        outs, (x, mask, dist, *inner) = refs[:n_out], refs[n_out:]
        after = inner if closing else outs
        after = (after[0:2], after[2:4])
        block_num = lax.axis_index("seq")
        block_base = block_num * block
        same = jnp.zeros(seg_ref.shape, jnp.int32)
        for back, ref in enumerate(seg_refs, 1):
            same = same + jnp.where((ref[...] == seg_ref[0:1, 0:1]) & (block_num >= back), 1, 0)
        start = block_base - jnp.sum(same)

        def key_base(i):
            def base(back, place):
                return block_base - back * block + place_of(place) * PIECE if back else -SPAN * block

            return jnp.where(block_num % 2 == 1, base(*which[i][1]), base(*which[i][0]))

        live = key_base(0) + PIECE > start
        for i in range(1, len(which)):
            live = live | (key_base(i) + PIECE > start)

        @pl.when(live)
        def _():
            set_earlier_masks(seg_ref, start, block_base, key_base, len(which), mask, dist)
            first = 0
            for source in sources:
                x[pl.ds(first, source.shape[0]), :] = normalise(source[...], gain_ref[...])
                first += source.shape[0]
            for group, (w, q) in enumerate(((w0, q0), (w1, q1))):
                keys = dot(x[...], w[1]).astype(BF16)
                v_t = dot(x[...], w[2]).T.astype(BF16)
                attend(keys, v_t, q, slopes_ref.at[pl.ds(4 * group, 4)], mask, dist, before[group], *after[group])

        @pl.when(jnp.logical_not(live))
        def _():
            for old, new in zip(before, after):
                new[0][...] = old[0][...]
                new[1][...] = old[1][...]

        if closing:
            write_closed(after, *outs)

    shapes = state_shapes(width, block) * 2
    scratch = [
        pltpu.VMEM((rows, depth), BF16),
        pltpu.VMEM((rows, block), F32),
        pltpu.VMEM((rows, PIECE), F32),
    ]
    if closing:
        scratch += [pltpu.VMEM(shape.shape, F32) for shape in shapes]
        shapes = (
            jax.ShapeDtypeStruct((2 * width + 32, block // 2), BF16),
            jax.ShapeDtypeStruct((8, block // 2), F32),
            jax.ShapeDtypeStruct((2 * width, block // 2), F32),
        )
    return pl.pallas_call(
        body,
        out_shape=shapes,
        in_specs=[VMEM] * (11 + len(segs) + count),
        out_specs=(VMEM,) * n_out,
        scratch_shapes=scratch,
        compiler_params=params(EARLIER_MIB),
        cost_estimate=cost(4 * rows * depth * width, 2**20, 0),
    )(slopes8, seg, gain, *segs, *pieces, w_own, w_pair, q_own, q_pair, *state)


def project(place, lse, out, got, wo_own, wo_pair, tokens):
    wide = out.shape[0]
    width, model = wo_own.shape

    def body(lse_ref, out_ref, got_ref, w0, w1, *refs):
        y_ref, ctx = refs[-2:]
        lanes = pl.ds(place * PIECE, PIECE)
        other = got_ref[pl.ds(wide, 32), lanes].astype(F32)
        other = other[0:8] + other[8:16] + other[16:24]
        for head in range(8):
            swapped = (head + 4) % 8
            mine, theirs = lse_ref[head : head + 1, lanes], other[swapped : swapped + 1]
            top = jnp.maximum(mine, theirs)
            weigh, weigh_other = jnp.exp2(mine - top), jnp.exp2(theirs - top)
            joined = (out_ref[pl.ds(head * HD, HD), lanes] * weigh
                      + got_ref[pl.ds(swapped * HD, HD), lanes].astype(F32) * weigh_other)
            joined = joined / (weigh + weigh_other)
            ctx[:, head * HD : (head + 1) * HD] = joined.T.astype(BF16)
        result = dot(ctx[:, :width], w0[...]) + dot(ctx[:, width:], w1[...])
        if tokens is not None:
            result = result + refs[0][...].astype(F32)
        y_ref[...] = result.astype(y_ref.dtype)

    extra = () if tokens is None else (tokens,)
    return pl.pallas_call(
        body,
        out_shape=jax.ShapeDtypeStruct((PIECE, model), BF16 if tokens is None else F32),
        in_specs=[VMEM] * (5 + len(extra)),
        out_specs=VMEM,
        scratch_shapes=[pltpu.VMEM((PIECE, wide), BF16)],
        compiler_params=params(16),
        cost_estimate=cost(PIECE * wide * model, 2**20, 0),
    )(lse, out, got, wo_own, wo_pair, *extra)


def on_device(tokens, ln_gain, w_qkv, slopes, w_out, seg_ids):
    blocks = lax.axis_size("seq")
    block_num = lax.axis_index("seq")
    odd = (block_num % 2) == 1

    def over_core(value):
        return lax.ppermute(value, "head", [(i, i ^ 1) for i in range(4)])

    def over_x(value):
        return lax.ppermute(value, "head", [(i, i ^ 2) for i in range(4)])

    def over_seq(value, pairs):
        return lax.ppermute(value, "seq", pairs)

    two_on = [(i, i + 2) for i in range(blocks - 2)]
    even_to_odd = [(i, i + 1) for i in range(0, blocks, 2)]
    odd_to_even = [(i + 1, i) for i in range(0, blocks, 2)]

    tie = lax.optimization_barrier
    w_all = jnp.transpose(w_qkv, (1, 0, 2))
    seg = seg_ids.reshape(4, PIECE)
    gain = ln_gain.reshape(1, -1)
    w_pair = over_core(w_all)

    a2 = over_seq(tokens, two_on)
    b0 = over_x(tokens)
    a1_odd = over_seq(tokens, even_to_odd)
    c0 = over_core(tokens)
    slopes_sent, w_staged, c0 = tie((slopes, w_all, c0))
    slopes_pair = over_core(slopes_sent)
    seg_sent, slopes_pair = tie((seg, slopes_pair))
    seg1 = over_seq(seg_sent, [(i, i + 1) for i in range(blocks - 1)])
    w_staged = stage(w_staged)

    a2, b0, a1_odd, w_pair, w_staged, slopes_pair, seg1 = tie(
        (a2, b0, a1_odd, w_pair, w_staged, slopes_pair, seg1))
    a4 = over_seq(a2, two_on)
    b2 = over_x(a2)
    crossed = over_seq(a2, even_to_odd + odd_to_even)
    d0 = over_core(b0)
    seg1_sent, wo_sent, d0 = tie((seg1, w_out, d0))
    seg23 = over_seq(jnp.concatenate([seg, seg1_sent], axis=0), two_on)
    wo_pair = over_core(wo_sent)
    segs = [seg1, seg23[:4], seg23[4:]]
    q_own, q_pair, *state, key_cache, value_cache, slopes8 = own_block(
        slopes, slopes_pair, seg, gain, (tokens, b0, c0, d0), w_staged, w_pair)

    crossed, b2, a4, b0_sent, segs, state[0] = tie((crossed, b2, a4, b0, segs, state[0]))
    over_y = over_seq(pick(b0_sent, a4), even_to_odd + odd_to_even)
    x_third = over_x(crossed)
    b4 = over_seq(b2, two_on)
    seg4 = over_seq(segs[1], two_on)

    def merge(closing, segs, pieces, which, state):
        return earlier_pieces(
            which, closing, slopes8, seg, segs, gain, pieces, w_staged, w_pair, q_own, q_pair, state)

    state = merge(
        False, segs, (a2, b2, crossed, a1_odd),
        (((2, 0),) * 2, ((2, 1),) * 2, ((1, 0), (3, 0)), ((0, 0), (1, 0))), state)

    over_y, x_third, b4, seg4, held = tie((over_y, x_third, b4, seg4, state[0]))
    segs = [*segs, seg4]
    state = (held, *state[1:])
    b3_top = over_x(over_y[: PIECE // 2])
    b3_rest = over_seq(b4[PIECE // 2 :], odd_to_even)
    state = merge(
        False, segs, (a4, b4, x_third, over_y),
        (((4, 0),) * 2, ((4, 1),) * 2, ((1, 1), (3, 1)), ((3, 0), (1, 1))), state)
    send, lse, out = merge(True, segs, (b3_top, b3_rest), (((3, 1), (0, 0)),), state)
    got = over_core(send)
    y_pair = project(1, lse, out, got, w_out, wo_pair, None)
    y_got = over_x(y_pair)
    y_own = project(0, lse, out, got, w_out, wo_pair, tokens)
    hidden = (y_own + y_got.astype(F32)).astype(BF16)
    return (hidden, key_cache, value_cache)


def solution(mesh):
    in_specs = (
        P(("seq", "head"), None),
        P(),
        P(None, None, "head"),
        P("head"),
        P("head", None),
        P("seq"),
    )
    out_specs = (P(("seq", "head"), None), P("seq", "head"), P("seq", "head"))
    return jax.shard_map(
        on_device, mesh=mesh, in_specs=in_specs, out_specs=out_specs, check_vma=False
    )
```

```python
import jax
import jax.numpy as jnp
from jax import lax
from jax.experimental import pallas as pl
from jax.experimental.pallas import tpu as pltpu
from jax.sharding import PartitionSpec as P

HD = 128
SPAN = 4
PIECE = 128
EPSILON = 1e-05
NEG_FILL = -1e30
MASKED = -2e38
OWN_MIB = 16
EARLIER_MIB = 16
LOG2E = 1.4426950408889634

BF16 = jnp.bfloat16
F32 = jnp.float32
SMEM = pl.BlockSpec(memory_space=pltpu.SMEM)
HBM = pl.BlockSpec(memory_space=pltpu.HBM)
VMEM = pl.BlockSpec(memory_space=pltpu.VMEM)


def params(mebibytes):
    return pltpu.CompilerParams(vmem_limit_bytes=mebibytes * 2**20)


def cost(macs, nbytes, exps=0):
    return pl.CostEstimate(flops=2 * macs, bytes_accessed=nbytes, transcendentals=exps)


def dot(lhs, rhs):
    return jnp.dot(lhs, rhs, preferred_element_type=F32)


def three_addends(value):
    high = value.astype(BF16).astype(F32)
    middle = (value - high).astype(BF16).astype(F32)
    return high, middle, value - high - middle


def normalise(tokens, gain):
    inputs = tokens.astype(F32)
    centred = inputs - jnp.mean(inputs, axis=-1, keepdims=True)
    variance = jnp.mean(centred * centred, axis=-1, keepdims=True)
    return (centred * lax.rsqrt(variance + EPSILON) * gain).astype(BF16)


def stage(weights):
    def body(source, out_ref, sem):
        copy = pltpu.make_async_copy(source, out_ref, sem)
        copy.start()
        copy.wait()

    return pl.pallas_call(
        body,
        out_shape=jax.ShapeDtypeStruct(weights.shape, weights.dtype),
        in_specs=[HBM],
        out_specs=VMEM,
        scratch_shapes=[pltpu.SemaphoreType.DMA],
        compiler_params=params(8),
        cost_estimate=cost(0, 2 * weights.size * 2),
    )(weights)


def pick(even_value, odd_value):
    def body(even_ref, odd_ref, out_ref):
        odd = lax.axis_index("seq") % 2 == 1

        @pl.when(odd)
        def _():
            out_ref[...] = odd_ref[...]

        @pl.when(jnp.logical_not(odd))
        def _():
            out_ref[...] = even_ref[...]

    return pl.pallas_call(
        body,
        out_shape=jax.ShapeDtypeStruct(even_value.shape, even_value.dtype),
        in_specs=[VMEM, VMEM],
        out_specs=VMEM,
        compiler_params=params(8),
        cost_estimate=cost(0, 2 * even_value.size * 2),
    )(even_value, odd_value)


def place_of(place):
    return lax.axis_index("head") ^ (0, 2, 1, 3)[place]


def set_distance(block_base, key_base, keys, dist_ref):
    row = lax.broadcasted_iota(jnp.int32, (PIECE, PIECE), 0)
    for piece in range(keys):
        dist_ref[pl.ds(piece * PIECE, PIECE), :] = (row + (key_base(piece) - block_base)).astype(F32)


def set_own_masks(seg_ref, mask_ref, dist_ref):
    lane = lax.broadcasted_iota(jnp.int32, (1, PIECE), 1)
    row = lax.broadcasted_iota(jnp.int32, (PIECE, PIECE), 0)
    set_distance(0, lambda i: place_of(i) * PIECE, 2, dist_ref)
    for piece in range(2):
        rows = pl.ds(piece * PIECE, PIECE)
        k_pos = row + place_of(piece) * PIECE
        key_seg = seg_ref[pl.ds(place_of(piece), 1), :]
        key_seg = jnp.broadcast_to(key_seg, (PIECE, PIECE)).T
        for place in range(4):
            q_pos = lane + place_of(place) * PIECE
            kept = (key_seg == seg_ref[pl.ds(place_of(place), 1), :]) & (k_pos <= q_pos)
            mask_ref[rows, pl.ds(place * PIECE, PIECE)] = jnp.where(kept, 0.0, MASKED)


def set_earlier_masks(seg_ref, start, block_base, key_base, keys, mask_ref, dist_ref):
    row = lax.broadcasted_iota(jnp.int32, (PIECE, PIECE), 0)
    set_distance(block_base, key_base, keys, dist_ref)
    first_seg = seg_ref[0:1, 0:1]
    for piece in range(keys):
        rows = pl.ds(piece * PIECE, PIECE)
        late = row + key_base(piece) >= start
        for place in range(4):
            kept = late & (seg_ref[pl.ds(place_of(place), 1), :] == first_seg)
            mask_ref[rows, pl.ds(place * PIECE, PIECE)] = jnp.where(kept, 0.0, MASKED)


def attend(k_rows, v_t, q_ref, slopes_ref, mask_ref, dist_ref, before, stat_ref, acc_ref):
    heads = k_rows.shape[1] // HD
    for head in range(heads):
        cols = slice(head * HD, (head + 1) * HD)
        wide = pl.ds(head * HD, HD)
        bias = dist_ref[...] * (slopes_ref[head : head + 1, :] * LOG2E)
        bias = jnp.concatenate([bias] * (q_ref.shape[1] // PIECE), axis=1)
        scores = dot(k_rows[:, cols], q_ref[wide, :]) * (HD**-0.5 * LOG2E)
        scores = scores + bias + mask_ref[...]
        top = jnp.max(scores, axis=0, keepdims=True)
        prev = jnp.full_like(top, NEG_FILL) if before is None else before[0][head : head + 1, :]
        row_max = jnp.maximum(prev, top)
        expo = jnp.exp2(scores - row_max)
        total = jnp.sum(expo, axis=0, keepdims=True)
        update = dot(v_t[cols, :], expo.astype(BF16))
        if before is not None:
            rescale = jnp.exp2(prev - row_max)
            total = before[0][4 + head : 5 + head, :] * rescale + total
            update = before[1][wide, :] * rescale + update
        stat_ref[head : head + 1, :] = row_max
        stat_ref[4 + head : 5 + head, :] = total
        acc_ref[wide, :] = update


def state_shapes(width, block):
    return (jax.ShapeDtypeStruct((8, block), F32), jax.ShapeDtypeStruct((width, block), F32))


def own_block(slopes, slopes_pair, seg, gain, pieces, w_own, w_pair):
    depth, width = w_own.shape[1:]
    block = 4 * PIECE

    def body(s0, s1, seg_ref, gain_ref, a, b, c, d, w0, w1, q0, q1, stat0, acc0, stat1, acc1, k_cache, v_cache,
             slopes_out, x, mask, dist):
        set_own_masks(seg_ref, mask, dist)
        for head in range(4):
            slopes_out[head : head + 1, :] = jnp.full((1, PIECE), s0[head], F32)
            slopes_out[4 + head : 5 + head, :] = jnp.full((1, PIECE), s1[head], F32)
        for place, piece in enumerate((a, b, c, d)):
            x[pl.ds(place * PIECE, PIECE), :] = normalise(piece[...], gain_ref[...])
        for group, (w, q, stat, acc) in enumerate(((w0, q0, stat0, acc0), (w1, q1, stat1, acc1))):
            rows = block if group == 0 else 2 * PIECE
            q[...] = dot(x[...], w[0]).T.astype(BF16)
            keys = dot(x[:rows, :], w[1]).astype(BF16)
            values = dot(x[:rows, :], w[2])
            if group == 0:
                for place in range(4):
                    to = pl.ds(pl.multiple_of(place_of(place) * PIECE, PIECE), PIECE)
                    k_cache[to, :] = keys[place * PIECE : (place + 1) * PIECE]
                    v_cache[to, :] = values[place * PIECE : (place + 1) * PIECE].astype(BF16)
            v_t = values[: 2 * PIECE].T.astype(BF16)
            attend(keys[: 2 * PIECE], v_t, q, slopes_out.at[pl.ds(4 * group, 4)], mask, dist, None, stat, acc)

    return pl.pallas_call(
        body,
        out_shape=(jax.ShapeDtypeStruct((width, block), BF16),) * 2 + state_shapes(width, block) * 2 + (
            jax.ShapeDtypeStruct((block, width), BF16),
            jax.ShapeDtypeStruct((block, width), BF16),
            jax.ShapeDtypeStruct((8, PIECE), F32),
        ),
        in_specs=[SMEM] * 2 + [VMEM] * 8,
        out_specs=(VMEM,) * 9,
        scratch_shapes=[
            pltpu.VMEM((block, depth), BF16),
            pltpu.VMEM((2 * PIECE, block), F32),
            pltpu.VMEM((2 * PIECE, PIECE), F32),
        ],
        compiler_params=params(OWN_MIB),
        cost_estimate=cost(5 * block * depth * width, 2**20, 0),
    )(slopes, slopes_pair, seg, gain, *pieces, w_own, w_pair)


def write_closed(states, send_ref, lse_ref, out_ref):
    width, block = states[0][1].shape
    half = block // 2
    sent = []
    for group, (stat, acc) in enumerate(states):
        total = stat[4:8, :]
        some = total > 0.0
        lse = jnp.where(some, stat[0:4, :] + jnp.log2(jnp.where(some, total, 1.0)), NEG_FILL)
        scale = jnp.where(some, 1.0 / jnp.where(some, total, 1.0), 0.0)
        lse_ref[4 * group : 4 * group + 4, :] = lse[:, :half]
        sent.append(lse[:, half:])
        for head in range(4):
            rows = pl.ds(head * HD, HD)
            to = pl.ds(group * width + head * HD, HD)
            normal = acc[rows, :] * scale[head : head + 1, :]
            out_ref[to, :] = normal[:, :half]
            send_ref[to, :] = normal[:, half:].astype(BF16)
    parts = list(three_addends(jnp.concatenate(sent, axis=0)))
    parts.append(jnp.zeros_like(parts[0]))
    send_ref[pl.ds(2 * width, 32), :] = jnp.concatenate(parts, axis=0).astype(BF16)


def earlier_pieces(which, closing, slopes8, seg, segs, gain, pieces, w_own, w_pair, q_own, q_pair, state):
    depth, width = w_own.shape[1:]
    block = 4 * PIECE
    count = len(pieces)
    rows = len(which) * PIECE
    n_out = 3 if closing else 4

    def body(slopes_ref, seg_ref, gain_ref, *refs):
        seg_refs, refs = refs[: len(segs)], refs[len(segs) :]
        sources, refs = refs[:count], refs[count:]
        (w0, w1, q0, q1), before, refs = refs[:4], (refs[4:6], refs[6:8]), refs[8:]
        outs, (x, mask, dist, *inner) = refs[:n_out], refs[n_out:]
        after = inner if closing else outs
        after = (after[0:2], after[2:4])
        block_num = lax.axis_index("seq")
        block_base = block_num * block
        same = jnp.zeros(seg_ref.shape, jnp.int32)
        for back, ref in enumerate(seg_refs, 1):
            same = same + jnp.where((ref[...] == seg_ref[0:1, 0:1]) & (block_num >= back), 1, 0)
        start = block_base - jnp.sum(same)

        def key_base(i):
            def base(back, place):
                return block_base - back * block + place_of(place) * PIECE if back else -SPAN * block

            return jnp.where(block_num % 2 == 1, base(*which[i][1]), base(*which[i][0]))

        live = key_base(0) + PIECE > start
        for i in range(1, len(which)):
            live = live | (key_base(i) + PIECE > start)

        @pl.when(live)
        def _():
            set_earlier_masks(seg_ref, start, block_base, key_base, len(which), mask, dist)
            first = 0
            for source in sources:
                x[pl.ds(first, source.shape[0]), :] = normalise(source[...], gain_ref[...])
                first += source.shape[0]
            for group, (w, q) in enumerate(((w0, q0), (w1, q1))):
                keys = dot(x[...], w[1]).astype(BF16)
                v_t = dot(x[...], w[2]).T.astype(BF16)
                attend(keys, v_t, q, slopes_ref.at[pl.ds(4 * group, 4)], mask, dist, before[group], *after[group])

        @pl.when(jnp.logical_not(live))
        def _():
            for old, new in zip(before, after):
                new[0][...] = old[0][...]
                new[1][...] = old[1][...]

        if closing:
            write_closed(after, *outs)

    shapes = state_shapes(width, block) * 2
    scratch = [
        pltpu.VMEM((rows, depth), BF16),
        pltpu.VMEM((rows, block), F32),
        pltpu.VMEM((rows, PIECE), F32),
    ]
    if closing:
        scratch += [pltpu.VMEM(shape.shape, F32) for shape in shapes]
        shapes = (
            jax.ShapeDtypeStruct((2 * width + 32, block // 2), BF16),
            jax.ShapeDtypeStruct((8, block // 2), F32),
            jax.ShapeDtypeStruct((2 * width, block // 2), F32),
        )
    return pl.pallas_call(
        body,
        out_shape=shapes,
        in_specs=[VMEM] * (11 + len(segs) + count),
        out_specs=(VMEM,) * n_out,
        scratch_shapes=scratch,
        compiler_params=params(EARLIER_MIB),
        cost_estimate=cost(4 * rows * depth * width, 2**20, 0),
    )(slopes8, seg, gain, *segs, *pieces, w_own, w_pair, q_own, q_pair, *state)


def project(place, lse, out, got, wo_own, wo_pair, tokens):
    wide = out.shape[0]
    width, model = wo_own.shape

    def body(lse_ref, out_ref, got_ref, w0, w1, *refs):
        y_ref, ctx = refs[-2:]
        lanes = pl.ds(place * PIECE, PIECE)
        other = got_ref[pl.ds(wide, 32), lanes].astype(F32)
        other = other[0:8] + other[8:16] + other[16:24]
        for head in range(8):
            swapped = (head + 4) % 8
            mine, theirs = lse_ref[head : head + 1, lanes], other[swapped : swapped + 1]
            top = jnp.maximum(mine, theirs)
            weigh, weigh_other = jnp.exp2(mine - top), jnp.exp2(theirs - top)
            joined = (out_ref[pl.ds(head * HD, HD), lanes] * weigh
                      + got_ref[pl.ds(swapped * HD, HD), lanes].astype(F32) * weigh_other)
            joined = joined / (weigh + weigh_other)
            ctx[:, head * HD : (head + 1) * HD] = joined.T.astype(BF16)
        result = dot(ctx[:, :width], w0[...]) + dot(ctx[:, width:], w1[...])
        if tokens is not None:
            result = result + refs[0][...].astype(F32)
        y_ref[...] = result.astype(y_ref.dtype)

    extra = () if tokens is None else (tokens,)
    return pl.pallas_call(
        body,
        out_shape=jax.ShapeDtypeStruct((PIECE, model), BF16 if tokens is None else F32),
        in_specs=[VMEM] * (5 + len(extra)),
        out_specs=VMEM,
        scratch_shapes=[pltpu.VMEM((PIECE, wide), BF16)],
        compiler_params=params(16),
        cost_estimate=cost(PIECE * wide * model, 2**20, 0),
    )(lse, out, got, wo_own, wo_pair, *extra)


def on_device(tokens, ln_gain, w_qkv, slopes, w_out, seg_ids):
    blocks = lax.axis_size("seq")
    block_num = lax.axis_index("seq")
    odd = (block_num % 2) == 1

    def over_core(value):
        return lax.ppermute(value, "head", [(i, i ^ 1) for i in range(4)])

    def over_x(value):
        return lax.ppermute(value, "head", [(i, i ^ 2) for i in range(4)])

    def over_seq(value, pairs):
        return lax.ppermute(value, "seq", pairs)

    two_on = [(i, i + 2) for i in range(blocks - 2)]
    even_to_odd = [(i, i + 1) for i in range(0, blocks, 2)]
    odd_to_even = [(i + 1, i) for i in range(0, blocks, 2)]

    tie = lax.optimization_barrier
    w_all = jnp.transpose(w_qkv, (1, 0, 2))
    seg = seg_ids.reshape(4, PIECE)
    gain = ln_gain.reshape(1, -1)
    w_pair = over_core(w_all)

    a2 = over_seq(tokens, two_on)
    b0 = over_x(tokens)
    a1_odd = over_seq(tokens, even_to_odd)
    c0 = over_core(tokens)
    slopes_sent, w_staged, c0 = tie((slopes, stage(w_all), c0))
    slopes_pair = over_core(slopes_sent)
    seg_sent, slopes_pair = tie((seg, slopes_pair))
    seg1 = over_seq(seg_sent, [(i, i + 1) for i in range(blocks - 1)])

    a2, b0, a1_odd, w_pair, w_staged, slopes_pair, seg1 = tie(
        (a2, b0, a1_odd, w_pair, w_staged, slopes_pair, seg1))
    a4 = over_seq(a2, two_on)
    b2 = over_x(a2)
    crossed = over_seq(a2, even_to_odd + odd_to_even)
    d0 = over_core(b0)
    seg1_sent, seg_sent, d0 = tie((seg1, seg, d0))
    seg23 = over_seq(jnp.concatenate([seg, seg1_sent], axis=0), two_on)
    seg4 = over_seq(seg_sent, [(i, i + SPAN) for i in range(blocks - SPAN)])
    segs = [seg1, seg23[:4], seg23[4:], seg4]
    q_own, q_pair, *state, key_cache, value_cache, slopes8 = own_block(
        slopes, slopes_pair, seg, gain, (tokens, b0, c0, d0), w_staged, w_pair)

    crossed, b2, a4, b0_sent, segs, state[0] = tie((crossed, b2, a4, b0, segs, state[0]))
    picked = pick(b0_sent, a4)
    over_y = over_seq(picked, even_to_odd + odd_to_even)
    x_third = over_x(crossed)
    b4 = over_seq(b2, two_on)
    wo_sent, picked = tie((w_out, picked))
    wo_pair = over_core(wo_sent)

    def merge(closing, segs, pieces, which, state):
        return earlier_pieces(
            which, closing, slopes8, seg, segs, gain, pieces, w_staged, w_pair, q_own, q_pair, state)

    state = merge(
        False, segs, (a2, b2, a4, crossed, a1_odd),
        (((2, 0),) * 2, ((2, 1),) * 2, ((4, 0),) * 2, ((1, 0), (3, 0)), ((0, 0), (1, 0))), state)

    over_y, x_third, b4, held = tie((over_y, x_third, b4, state[0]))
    state = (held, *state[1:])
    b3_top = over_x(over_y[: PIECE // 2])
    b3_rest = over_seq(b4[PIECE // 2 :], odd_to_even)
    state = merge(
        False, segs, (b4, x_third, over_y), (((4, 1),) * 2, ((1, 1), (3, 1)), ((3, 0), (1, 1))), state)
    send, lse, out = merge(True, segs, (b3_top, b3_rest), (((3, 1), (0, 0)),), state)
    got = over_core(send)
    y_pair = project(1, lse, out, got, w_out, wo_pair, None)
    y_got = over_x(y_pair)
    y_own = project(0, lse, out, got, w_out, wo_pair, tokens)
    hidden = (y_own + y_got.astype(F32)).astype(BF16)
    return (hidden, key_cache, value_cache)


def solution(mesh):
    in_specs = (
        P(("seq", "head"), None),
        P(),
        P(None, None, "head"),
        P("head"),
        P("head", None),
        P("seq"),
    )
    out_specs = (P(("seq", "head"), None), P("seq", "head"), P("seq", "head"))
    return jax.shard_map(
        on_device, mesh=mesh, in_specs=in_specs, out_specs=out_specs, check_vma=False
    )
```

```python
import jax
import jax.numpy as jnp
from jax import lax
from jax.experimental import pallas as pl
from jax.experimental.pallas import tpu as pltpu
from jax.sharding import PartitionSpec as P

HD = 128
SPAN = 4
PIECE = 128
EPSILON = 1e-05
NEG_FILL = -1e30
MASKED = -2e38
OWN_MIB = 16
EARLIER_MIB = 16
LOG2E = 1.4426950408889634

BF16 = jnp.bfloat16
F32 = jnp.float32
HBM = pl.BlockSpec(memory_space=pltpu.HBM)
VMEM = pl.BlockSpec(memory_space=pltpu.VMEM)


def params(mebibytes):
    return pltpu.CompilerParams(vmem_limit_bytes=mebibytes * 2**20)


def cost(macs, nbytes, exps=0):
    return pl.CostEstimate(flops=2 * macs, bytes_accessed=nbytes, transcendentals=exps)


def dot(lhs, rhs):
    return jnp.dot(lhs, rhs, preferred_element_type=F32)


def three_addends(value):
    high = value.astype(BF16).astype(F32)
    middle = (value - high).astype(BF16).astype(F32)
    return high, middle, value - high - middle


def normalise(tokens, gain):
    inputs = tokens.astype(F32)
    centred = inputs - jnp.mean(inputs, axis=-1, keepdims=True)
    variance = jnp.mean(centred * centred, axis=-1, keepdims=True)
    return (centred * lax.rsqrt(variance + EPSILON) * gain).astype(BF16)


def stage(weights):
    def body(source, out_ref, sem):
        copy = pltpu.make_async_copy(source, out_ref, sem)
        copy.start()
        copy.wait()

    return pl.pallas_call(
        body,
        out_shape=jax.ShapeDtypeStruct(weights.shape, weights.dtype),
        in_specs=[HBM],
        out_specs=VMEM,
        scratch_shapes=[pltpu.SemaphoreType.DMA],
        compiler_params=params(8),
        cost_estimate=cost(0, 2 * weights.size * 2),
    )(weights)


def pick(even_value, odd_value):
    def body(even_ref, odd_ref, out_ref):
        odd = lax.axis_index("seq") % 2 == 1

        @pl.when(odd)
        def _():
            out_ref[...] = odd_ref[...]

        @pl.when(jnp.logical_not(odd))
        def _():
            out_ref[...] = even_ref[...]

    return pl.pallas_call(
        body,
        out_shape=jax.ShapeDtypeStruct(even_value.shape, even_value.dtype),
        in_specs=[VMEM, VMEM],
        out_specs=VMEM,
        compiler_params=params(8),
        cost_estimate=cost(0, 2 * even_value.size * 2),
    )(even_value, odd_value)


def place_of(place):
    return lax.axis_index("head") ^ (0, 2, 1, 3)[place]


def set_distance(block_base, key_base, keys, dist_ref):
    row = lax.broadcasted_iota(jnp.int32, (PIECE, PIECE), 0)
    for piece in range(keys):
        dist_ref[pl.ds(piece * PIECE, PIECE), :] = (row + (key_base(piece) - block_base)).astype(F32)


def set_own_masks(seg_ref, mask_ref, dist_ref):
    lane = lax.broadcasted_iota(jnp.int32, (1, PIECE), 1)
    row = lax.broadcasted_iota(jnp.int32, (PIECE, PIECE), 0)
    set_distance(0, lambda i: place_of(i) * PIECE, 2, dist_ref)
    for piece in range(2):
        rows = pl.ds(piece * PIECE, PIECE)
        k_pos = row + place_of(piece) * PIECE
        key_seg = seg_ref[pl.ds(place_of(piece), 1), :]
        key_seg = jnp.broadcast_to(key_seg, (PIECE, PIECE)).T
        for place in range(4):
            q_pos = lane + place_of(place) * PIECE
            kept = (key_seg == seg_ref[pl.ds(place_of(place), 1), :]) & (k_pos <= q_pos)
            mask_ref[rows, pl.ds(place * PIECE, PIECE)] = jnp.where(kept, 0.0, MASKED)


def set_earlier_masks(seg_ref, start, block_base, key_base, keys, mask_ref, dist_ref):
    row = lax.broadcasted_iota(jnp.int32, (PIECE, PIECE), 0)
    set_distance(block_base, key_base, keys, dist_ref)
    first_seg = seg_ref[0:1, 0:1]
    for piece in range(keys):
        rows = pl.ds(piece * PIECE, PIECE)
        late = row + key_base(piece) >= start
        for place in range(4):
            kept = late & (seg_ref[pl.ds(place_of(place), 1), :] == first_seg)
            mask_ref[rows, pl.ds(place * PIECE, PIECE)] = jnp.where(kept, 0.0, MASKED)


def attend(k_rows, v_t, q_ref, slopes_ref, mask_ref, dist_ref, before, stat_ref, acc_ref):
    heads = k_rows.shape[1] // HD
    for head in range(heads):
        cols = slice(head * HD, (head + 1) * HD)
        wide = pl.ds(head * HD, HD)
        bias = dist_ref[...] * (slopes_ref[head : head + 1, :] * LOG2E)
        bias = jnp.concatenate([bias] * (q_ref.shape[1] // PIECE), axis=1)
        scores = dot(k_rows[:, cols], q_ref[wide, :]) * (HD**-0.5 * LOG2E)
        scores = scores + bias + mask_ref[...]
        top = jnp.max(scores, axis=0, keepdims=True)
        prev = jnp.full_like(top, NEG_FILL) if before is None else before[0][head : head + 1, :]
        row_max = jnp.maximum(prev, top)
        expo = jnp.exp2(scores - row_max)
        total = jnp.sum(expo, axis=0, keepdims=True)
        update = dot(v_t[cols, :], expo.astype(BF16))
        if before is not None:
            rescale = jnp.exp2(prev - row_max)
            total = before[0][4 + head : 5 + head, :] * rescale + total
            update = before[1][wide, :] * rescale + update
        stat_ref[head : head + 1, :] = row_max
        stat_ref[4 + head : 5 + head, :] = total
        acc_ref[wide, :] = update


def state_shapes(width, block):
    return (jax.ShapeDtypeStruct((8, block), F32), jax.ShapeDtypeStruct((width, block), F32))


def own_block(slopes, slopes_pair, seg, gain, pieces, w_own, w_pair):
    depth, width = w_own.shape[1:]
    block = 4 * PIECE

    def body(s0, s1, seg_ref, gain_ref, a, b, c, d, w0, w1, q0, q1, stat0, acc0, stat1, acc1, k_cache, v_cache,
             slopes_out, x, mask, dist):
        set_own_masks(seg_ref, mask, dist)
        for head in range(4):
            slopes_out[head : head + 1, :] = jnp.broadcast_to(s0[0:1, head : head + 1], (1, PIECE))
            slopes_out[4 + head : 5 + head, :] = jnp.broadcast_to(s1[0:1, head : head + 1], (1, PIECE))
        for place, piece in enumerate((a, b, c, d)):
            x[pl.ds(place * PIECE, PIECE), :] = normalise(piece[...], gain_ref[...])
        for group, (w, q, stat, acc) in enumerate(((w0, q0, stat0, acc0), (w1, q1, stat1, acc1))):
            rows = block if group == 0 else 2 * PIECE
            q[...] = dot(x[...], w[0]).T.astype(BF16)
            keys = dot(x[:rows, :], w[1]).astype(BF16)
            values = dot(x[:rows, :], w[2])
            if group == 0:
                for place in range(4):
                    to = pl.ds(pl.multiple_of(place_of(place) * PIECE, PIECE), PIECE)
                    k_cache[to, :] = keys[place * PIECE : (place + 1) * PIECE]
                    v_cache[to, :] = values[place * PIECE : (place + 1) * PIECE].astype(BF16)
            v_t = values[: 2 * PIECE].T.astype(BF16)
            attend(keys[: 2 * PIECE], v_t, q, slopes_out.at[pl.ds(4 * group, 4)], mask, dist, None, stat, acc)

    return pl.pallas_call(
        body,
        out_shape=(jax.ShapeDtypeStruct((width, block), BF16),) * 2 + state_shapes(width, block) * 2 + (
            jax.ShapeDtypeStruct((block, width), BF16),
            jax.ShapeDtypeStruct((block, width), BF16),
            jax.ShapeDtypeStruct((8, PIECE), F32),
        ),
        in_specs=[VMEM] * 10,
        out_specs=(VMEM,) * 9,
        scratch_shapes=[
            pltpu.VMEM((block, depth), BF16),
            pltpu.VMEM((2 * PIECE, block), F32),
            pltpu.VMEM((2 * PIECE, PIECE), F32),
        ],
        compiler_params=params(OWN_MIB),
        cost_estimate=cost(5 * block * depth * width, 2**20, 0),
    )(slopes, slopes_pair, seg, gain, *pieces, w_own, w_pair)


def write_closed(states, send_ref, lse_ref, out_ref):
    width, block = states[0][1].shape
    half = block // 2
    sent = []
    for group, (stat, acc) in enumerate(states):
        total = stat[4:8, :]
        some = total > 0.0
        lse = jnp.where(some, stat[0:4, :] + jnp.log2(jnp.where(some, total, 1.0)), NEG_FILL)
        scale = jnp.where(some, 1.0 / jnp.where(some, total, 1.0), 0.0)
        lse_ref[4 * group : 4 * group + 4, :] = lse[:, :half]
        sent.append(lse[:, half:])
        for head in range(4):
            rows = pl.ds(head * HD, HD)
            to = pl.ds(group * width + head * HD, HD)
            normal = acc[rows, :] * scale[head : head + 1, :]
            out_ref[to, :] = normal[:, :half]
            send_ref[to, :] = normal[:, half:].astype(BF16)
    parts = list(three_addends(jnp.concatenate(sent, axis=0)))
    parts.append(jnp.zeros_like(parts[0]))
    send_ref[pl.ds(2 * width, 32), :] = jnp.concatenate(parts, axis=0).astype(BF16)


def earlier_pieces(which, closing, slopes8, seg, segs, gain, pieces, w_own, w_pair, q_own, q_pair, state):
    depth, width = w_own.shape[1:]
    block = 4 * PIECE
    count = len(pieces)
    rows = len(which) * PIECE
    n_out = 3 if closing else 4

    def body(slopes_ref, seg_ref, gain_ref, *refs):
        seg_refs, refs = refs[: len(segs)], refs[len(segs) :]
        sources, refs = refs[:count], refs[count:]
        (w0, w1, q0, q1), before, refs = refs[:4], (refs[4:6], refs[6:8]), refs[8:]
        outs, (x, mask, dist, *inner) = refs[:n_out], refs[n_out:]
        after = inner if closing else outs
        after = (after[0:2], after[2:4])
        block_num = lax.axis_index("seq")
        block_base = block_num * block
        same = jnp.zeros(seg_ref.shape, jnp.int32)
        for back, ref in enumerate(seg_refs, 1):
            same = same + jnp.where((ref[...] == seg_ref[0:1, 0:1]) & (block_num >= back), 1, 0)
        start = block_base - jnp.sum(same)

        def key_base(i):
            def base(back, place):
                return block_base - back * block + place_of(place) * PIECE if back else -SPAN * block

            return jnp.where(block_num % 2 == 1, base(*which[i][1]), base(*which[i][0]))

        live = key_base(0) + PIECE > start
        for i in range(1, len(which)):
            live = live | (key_base(i) + PIECE > start)

        @pl.when(live)
        def _():
            set_earlier_masks(seg_ref, start, block_base, key_base, len(which), mask, dist)
            first = 0
            for source in sources:
                x[pl.ds(first, source.shape[0]), :] = normalise(source[...], gain_ref[...])
                first += source.shape[0]
            for group, (w, q) in enumerate(((w0, q0), (w1, q1))):
                keys = dot(x[...], w[1]).astype(BF16)
                v_t = dot(x[...], w[2]).T.astype(BF16)
                attend(keys, v_t, q, slopes_ref.at[pl.ds(4 * group, 4)], mask, dist, before[group], *after[group])

        @pl.when(jnp.logical_not(live))
        def _():
            for old, new in zip(before, after):
                new[0][...] = old[0][...]
                new[1][...] = old[1][...]

        if closing:
            write_closed(after, *outs)

    shapes = state_shapes(width, block) * 2
    scratch = [
        pltpu.VMEM((rows, depth), BF16),
        pltpu.VMEM((rows, block), F32),
        pltpu.VMEM((rows, PIECE), F32),
    ]
    if closing:
        scratch += [pltpu.VMEM(shape.shape, F32) for shape in shapes]
        shapes = (
            jax.ShapeDtypeStruct((2 * width + 32, block // 2), BF16),
            jax.ShapeDtypeStruct((8, block // 2), F32),
            jax.ShapeDtypeStruct((2 * width, block // 2), F32),
        )
    return pl.pallas_call(
        body,
        out_shape=shapes,
        in_specs=[VMEM] * (11 + len(segs) + count),
        out_specs=(VMEM,) * n_out,
        scratch_shapes=scratch,
        compiler_params=params(EARLIER_MIB),
        cost_estimate=cost(4 * rows * depth * width, 2**20, 0),
    )(slopes8, seg, gain, *segs, *pieces, w_own, w_pair, q_own, q_pair, *state)


def project(place, lse, out, got, wo_own, wo_pair, tokens):
    wide = out.shape[0]
    width, model = wo_own.shape

    def body(lse_ref, out_ref, got_ref, w0, w1, *refs):
        y_ref, ctx = refs[-2:]
        lanes = pl.ds(place * PIECE, PIECE)
        other = got_ref[pl.ds(wide, 32), lanes].astype(F32)
        other = other[0:8] + other[8:16] + other[16:24]
        for head in range(8):
            swapped = (head + 4) % 8
            mine, theirs = lse_ref[head : head + 1, lanes], other[swapped : swapped + 1]
            top = jnp.maximum(mine, theirs)
            weigh, weigh_other = jnp.exp2(mine - top), jnp.exp2(theirs - top)
            joined = (out_ref[pl.ds(head * HD, HD), lanes] * weigh
                      + got_ref[pl.ds(swapped * HD, HD), lanes].astype(F32) * weigh_other)
            joined = joined / (weigh + weigh_other)
            ctx[:, head * HD : (head + 1) * HD] = joined.T.astype(BF16)
        result = dot(ctx[:, :width], w0[...]) + dot(ctx[:, width:], w1[...])
        if tokens is not None:
            result = result + refs[0][...].astype(F32)
        y_ref[...] = result.astype(y_ref.dtype)

    extra = () if tokens is None else (tokens,)
    return pl.pallas_call(
        body,
        out_shape=jax.ShapeDtypeStruct((PIECE, model), BF16 if tokens is None else F32),
        in_specs=[VMEM] * (5 + len(extra)),
        out_specs=VMEM,
        scratch_shapes=[pltpu.VMEM((PIECE, wide), BF16)],
        compiler_params=params(16),
        cost_estimate=cost(PIECE * wide * model, 2**20, 0),
    )(lse, out, got, wo_own, wo_pair, *extra)


def on_device(tokens, ln_gain, w_qkv, slopes, w_out, seg_ids):
    blocks = lax.axis_size("seq")
    block_num = lax.axis_index("seq")
    odd = (block_num % 2) == 1

    def over_core(value):
        return lax.ppermute(value, "head", [(i, i ^ 1) for i in range(4)])

    def over_x(value):
        return lax.ppermute(value, "head", [(i, i ^ 2) for i in range(4)])

    def over_seq(value, pairs):
        return lax.ppermute(value, "seq", pairs)

    two_on = [(i, i + 2) for i in range(blocks - 2)]
    even_to_odd = [(i, i + 1) for i in range(0, blocks, 2)]
    odd_to_even = [(i + 1, i) for i in range(0, blocks, 2)]

    tie = lax.optimization_barrier
    w_all = jnp.transpose(w_qkv, (1, 0, 2))
    seg = seg_ids.reshape(4, PIECE)
    slopes = slopes.reshape(1, -1)
    gain = ln_gain.reshape(1, -1)
    w_pair = over_core(w_all)

    a2 = over_seq(tokens, two_on)
    b0 = over_x(tokens)
    a1_odd = over_seq(tokens, even_to_odd)
    c0 = over_core(tokens)
    slopes_sent, w_staged, c0 = tie((slopes, stage(w_all), c0))
    slopes_pair = over_core(slopes_sent)
    seg_sent, slopes_pair = tie((seg, slopes_pair))
    seg1 = over_seq(seg_sent, [(i, i + 1) for i in range(blocks - 1)])

    a2, b0, a1_odd, w_pair, w_staged, slopes_pair, seg1 = tie(
        (a2, b0, a1_odd, w_pair, w_staged, slopes_pair, seg1))
    a4 = over_seq(a2, two_on)
    b2 = over_x(a2)
    crossed = over_seq(a2, even_to_odd + odd_to_even)
    d0 = over_core(b0)
    seg1_sent, seg_sent, d0 = tie((seg1, seg, d0))
    seg23 = over_seq(jnp.concatenate([seg, seg1_sent], axis=0), two_on)
    seg4 = over_seq(seg_sent, [(i, i + SPAN) for i in range(blocks - SPAN)])
    segs = [seg1, seg23[:4], seg23[4:], seg4]
    q_own, q_pair, *state, key_cache, value_cache, slopes8 = own_block(
        slopes, slopes_pair, seg, gain, (tokens, b0, c0, d0), w_staged, w_pair)

    crossed, b2, a4, b0_sent, segs, state[0] = tie((crossed, b2, a4, b0, segs, state[0]))
    picked = pick(b0_sent, a4)
    over_y = over_seq(picked, even_to_odd + odd_to_even)
    x_third = over_x(crossed)
    b4 = over_seq(b2, two_on)

    def merge(closing, segs, pieces, which, state):
        return earlier_pieces(
            which, closing, slopes8, seg, segs, gain, pieces, w_staged, w_pair, q_own, q_pair, state)

    state = merge(
        False, segs, (a2, b2, a4, crossed, a1_odd),
        (((2, 0),) * 2, ((2, 1),) * 2, ((4, 0),) * 2, ((1, 0), (3, 0)), ((0, 0), (1, 0))), state)

    over_y, x_third, b4, wo_sent, held = tie((over_y, x_third, b4, w_out, state[0]))
    state = (held, *state[1:])
    b3_top = over_x(over_y[: PIECE // 2])
    b3_rest = over_seq(b4[PIECE // 2 :], odd_to_even)
    wo_pair = over_core(wo_sent)
    state = merge(
        False, segs, (b4, x_third, over_y), (((4, 1),) * 2, ((1, 1), (3, 1)), ((3, 0), (1, 1))), state)
    send, lse, out = merge(True, segs, (b3_top, b3_rest), (((3, 1), (0, 0)),), state)
    got = over_core(send)
    y_pair = project(1, lse, out, got, w_out, wo_pair, None)
    y_got = over_x(y_pair)
    y_own = project(0, lse, out, got, w_out, wo_pair, tokens)
    hidden = (y_own + y_got.astype(F32)).astype(BF16)
    return (hidden, key_cache, value_cache)


def solution(mesh):
    in_specs = (
        P(("seq", "head"), None),
        P(),
        P(None, None, "head"),
        P("head"),
        P("head", None),
        P("seq"),
    )
    out_specs = (P(("seq", "head"), None), P("seq", "head"), P("seq", "head"))
    return jax.shard_map(
        on_device, mesh=mesh, in_specs=in_specs, out_specs=out_specs, check_vma=False
    )
```

```python
import jax
import jax.numpy as jnp
from jax import lax
from jax.experimental import pallas as pl
from jax.experimental.pallas import tpu as pltpu
from jax.sharding import PartitionSpec as P

HD = 128
SPAN = 4
PIECE = 128
EPSILON = 1e-05
NEG_FILL = -1e30
MASKED = -2e38
OWN_MIB = 16
EARLIER_MIB = 16
LOG2E = 1.4426950408889634

BF16 = jnp.bfloat16
F32 = jnp.float32
HBM = pl.BlockSpec(memory_space=pltpu.HBM)
VMEM = pl.BlockSpec(memory_space=pltpu.VMEM)


def params(mebibytes):
    return pltpu.CompilerParams(vmem_limit_bytes=mebibytes * 2**20)


def cost(macs, nbytes, exps=0):
    return pl.CostEstimate(flops=2 * macs, bytes_accessed=nbytes, transcendentals=exps)


def dot(lhs, rhs):
    return jnp.dot(lhs, rhs, preferred_element_type=F32)


def three_addends(value):
    high = value.astype(BF16).astype(F32)
    middle = (value - high).astype(BF16).astype(F32)
    return high, middle, value - high - middle


def normalise(tokens, gain):
    inputs = tokens.astype(F32)
    centred = inputs - jnp.mean(inputs, axis=-1, keepdims=True)
    variance = jnp.mean(centred * centred, axis=-1, keepdims=True)
    return (centred * lax.rsqrt(variance + EPSILON) * gain).astype(BF16)


def stage(weights):
    def body(source, out_ref, sem):
        copy = pltpu.make_async_copy(source, out_ref, sem)
        copy.start()
        copy.wait()

    return pl.pallas_call(
        body,
        out_shape=jax.ShapeDtypeStruct(weights.shape, weights.dtype),
        in_specs=[HBM],
        out_specs=VMEM,
        scratch_shapes=[pltpu.SemaphoreType.DMA],
        compiler_params=params(8),
        cost_estimate=cost(0, 2 * weights.size * 2),
    )(weights)


def pick(even_value, odd_value):
    def body(even_ref, odd_ref, out_ref):
        odd = lax.axis_index("seq") % 2 == 1

        @pl.when(odd)
        def _():
            out_ref[...] = odd_ref[...]

        @pl.when(jnp.logical_not(odd))
        def _():
            out_ref[...] = even_ref[...]

    return pl.pallas_call(
        body,
        out_shape=jax.ShapeDtypeStruct(even_value.shape, even_value.dtype),
        in_specs=[VMEM, VMEM],
        out_specs=VMEM,
        compiler_params=params(8),
        cost_estimate=cost(0, 2 * even_value.size * 2),
    )(even_value, odd_value)


def place_of(place):
    return lax.axis_index("head") ^ (0, 2, 1, 3)[place]


def set_distance(block_base, key_base, keys, dist_ref):
    row = lax.broadcasted_iota(jnp.int32, (PIECE, PIECE), 0)
    for piece in range(keys):
        dist_ref[pl.ds(piece * PIECE, PIECE), :] = (row + (key_base(piece) - block_base)).astype(F32)


def set_own_masks(seg_ref, mask_ref, dist_ref):
    lane = lax.broadcasted_iota(jnp.int32, (1, PIECE), 1)
    row = lax.broadcasted_iota(jnp.int32, (PIECE, PIECE), 0)
    set_distance(0, lambda i: place_of(i) * PIECE, 2, dist_ref)
    for piece in range(2):
        rows = pl.ds(piece * PIECE, PIECE)
        k_pos = row + place_of(piece) * PIECE
        key_seg = seg_ref[pl.ds(place_of(piece), 1), :]
        key_seg = jnp.broadcast_to(key_seg, (PIECE, PIECE)).T
        for place in range(4):
            q_pos = lane + place_of(place) * PIECE
            kept = (key_seg == seg_ref[pl.ds(place_of(place), 1), :]) & (k_pos <= q_pos)
            mask_ref[rows, pl.ds(place * PIECE, PIECE)] = jnp.where(kept, 0.0, MASKED)


def set_earlier_masks(seg_ref, start, block_base, key_base, keys, mask_ref, dist_ref):
    row = lax.broadcasted_iota(jnp.int32, (PIECE, PIECE), 0)
    set_distance(block_base, key_base, keys, dist_ref)
    first_seg = seg_ref[0:1, 0:1]
    for piece in range(keys):
        rows = pl.ds(piece * PIECE, PIECE)
        late = row + key_base(piece) >= start
        for place in range(4):
            kept = late & (seg_ref[pl.ds(place_of(place), 1), :] == first_seg)
            mask_ref[rows, pl.ds(place * PIECE, PIECE)] = jnp.where(kept, 0.0, MASKED)


def attend(k_rows, v_t, q_ref, slopes_ref, mask_ref, dist_ref, before, stat_ref, acc_ref):
    heads = k_rows.shape[1] // HD
    for head in range(heads):
        cols = slice(head * HD, (head + 1) * HD)
        wide = pl.ds(head * HD, HD)
        bias = dist_ref[...] * (slopes_ref[head : head + 1, :] * LOG2E)
        bias = jnp.concatenate([bias] * (q_ref.shape[1] // PIECE), axis=1)
        scores = dot(k_rows[:, cols], q_ref[wide, :]) * (HD**-0.5 * LOG2E)
        scores = scores + bias + mask_ref[...]
        top = jnp.max(scores, axis=0, keepdims=True)
        prev = jnp.full_like(top, NEG_FILL) if before is None else before[0][head : head + 1, :]
        row_max = jnp.maximum(prev, top)
        expo = jnp.exp2(scores - row_max)
        total = jnp.sum(expo, axis=0, keepdims=True)
        update = dot(v_t[cols, :], expo.astype(BF16))
        if before is not None:
            rescale = jnp.exp2(prev - row_max)
            total = before[0][4 + head : 5 + head, :] * rescale + total
            update = before[1][wide, :] * rescale + update
        stat_ref[head : head + 1, :] = row_max
        stat_ref[4 + head : 5 + head, :] = total
        acc_ref[wide, :] = update


def state_shapes(width, block):
    return (jax.ShapeDtypeStruct((8, block), F32), jax.ShapeDtypeStruct((width, block), F32))


def own_block(slopes, slopes_pair, seg, gain, pieces, w_own, w_pair):
    depth, width = w_own.shape[1:]
    block = 4 * PIECE

    def body(s0, s1, seg_ref, gain_ref, a, b, c, d, w0, w1, q0, q1, stat0, acc0, stat1, acc1, k_cache, v_cache,
             slopes_out, x, mask, dist):
        set_own_masks(seg_ref, mask, dist)
        for head in range(4):
            slopes_out[head : head + 1, :] = jnp.broadcast_to(s0[0:1, head : head + 1], (1, PIECE))
            slopes_out[4 + head : 5 + head, :] = jnp.broadcast_to(s1[0:1, head : head + 1], (1, PIECE))
        for place, piece in enumerate((a, b, c, d)):
            x[pl.ds(place * PIECE, PIECE), :] = normalise(piece[...], gain_ref[...])
        for group, (w, q, stat, acc) in enumerate(((w0, q0, stat0, acc0), (w1, q1, stat1, acc1))):
            rows = block if group == 0 else 2 * PIECE
            q[...] = dot(x[...], w[0]).T.astype(BF16)
            keys = dot(x[:rows, :], w[1]).astype(BF16)
            values = dot(x[:rows, :], w[2])
            if group == 0:
                for place in range(4):
                    to = pl.ds(pl.multiple_of(place_of(place) * PIECE, PIECE), PIECE)
                    k_cache[to, :] = keys[place * PIECE : (place + 1) * PIECE]
                    v_cache[to, :] = values[place * PIECE : (place + 1) * PIECE].astype(BF16)
            v_t = values[: 2 * PIECE].T.astype(BF16)
            attend(keys[: 2 * PIECE], v_t, q, slopes_out.at[pl.ds(4 * group, 4)], mask, dist, None, stat, acc)

    return pl.pallas_call(
        body,
        out_shape=(jax.ShapeDtypeStruct((width, block), BF16),) * 2 + state_shapes(width, block) * 2 + (
            jax.ShapeDtypeStruct((block, width), BF16),
            jax.ShapeDtypeStruct((block, width), BF16),
            jax.ShapeDtypeStruct((8, PIECE), F32),
        ),
        in_specs=[VMEM] * 10,
        out_specs=(VMEM,) * 9,
        scratch_shapes=[
            pltpu.VMEM((block, depth), BF16),
            pltpu.VMEM((2 * PIECE, block), F32),
            pltpu.VMEM((2 * PIECE, PIECE), F32),
        ],
        compiler_params=params(OWN_MIB),
        cost_estimate=cost(5 * block * depth * width, 2**20, 0),
    )(slopes, slopes_pair, seg, gain, *pieces, w_own, w_pair)


def write_closed(states, send_ref, lse_ref, out_ref):
    width, block = states[0][1].shape
    half = block // 2
    sent = []
    for group, (stat, acc) in enumerate(states):
        total = stat[4:8, :]
        some = total > 0.0
        lse = jnp.where(some, stat[0:4, :] + jnp.log2(jnp.where(some, total, 1.0)), NEG_FILL)
        scale = jnp.where(some, 1.0 / jnp.where(some, total, 1.0), 0.0)
        lse_ref[4 * group : 4 * group + 4, :] = lse[:, :half]
        sent.append(lse[:, half:])
        for head in range(4):
            rows = pl.ds(head * HD, HD)
            to = pl.ds(group * width + head * HD, HD)
            normal = acc[rows, :] * scale[head : head + 1, :]
            out_ref[to, :] = normal[:, :half]
            send_ref[to, :] = normal[:, half:].astype(BF16)
    parts = list(three_addends(jnp.concatenate(sent, axis=0)))
    parts.append(jnp.zeros_like(parts[0]))
    send_ref[pl.ds(2 * width, 32), :] = jnp.concatenate(parts, axis=0).astype(BF16)


def earlier_pieces(which, closing, slopes8, seg, segs, gain, pieces, w_own, w_pair, q_own, q_pair, state):
    depth, width = w_own.shape[1:]
    block = 4 * PIECE
    count = len(pieces)
    rows = len(which) * PIECE
    n_out = 3 if closing else 4

    def body(slopes_ref, seg_ref, gain_ref, *refs):
        seg_refs, refs = refs[: len(segs)], refs[len(segs) :]
        sources, refs = refs[:count], refs[count:]
        (w0, w1, q0, q1), before, refs = refs[:4], (refs[4:6], refs[6:8]), refs[8:]
        outs, (x, mask, dist, *inner) = refs[:n_out], refs[n_out:]
        after = inner if closing else outs
        after = (after[0:2], after[2:4])
        block_num = lax.axis_index("seq")
        block_base = block_num * block
        same = jnp.zeros(seg_ref.shape, jnp.int32)
        for back, ref in enumerate(seg_refs, 1):
            same = same + jnp.where((ref[...] == seg_ref[0:1, 0:1]) & (block_num >= back), 1, 0)
        start = block_base - jnp.sum(same)

        def key_base(i):
            def base(back, place):
                return block_base - back * block + place_of(place) * PIECE if back else -SPAN * block

            return jnp.where(block_num % 2 == 1, base(*which[i][1]), base(*which[i][0]))

        live = key_base(0) + PIECE > start
        for i in range(1, len(which)):
            live = live | (key_base(i) + PIECE > start)

        @pl.when(live)
        def _():
            set_earlier_masks(seg_ref, start, block_base, key_base, len(which), mask, dist)
            first = 0
            for source in sources:
                x[pl.ds(first, source.shape[0]), :] = normalise(source[...], gain_ref[...])
                first += source.shape[0]
            for group, (w, q) in enumerate(((w0, q0), (w1, q1))):
                keys = dot(x[...], w[1]).astype(BF16)
                v_t = dot(x[...], w[2]).T.astype(BF16)
                attend(keys, v_t, q, slopes_ref.at[pl.ds(4 * group, 4)], mask, dist, before[group], *after[group])

        @pl.when(jnp.logical_not(live))
        def _():
            for old, new in zip(before, after):
                new[0][...] = old[0][...]
                new[1][...] = old[1][...]

        if closing:
            write_closed(after, *outs)

    shapes = state_shapes(width, block) * 2
    scratch = [
        pltpu.VMEM((rows, depth), BF16),
        pltpu.VMEM((rows, block), F32),
        pltpu.VMEM((rows, PIECE), F32),
    ]
    if closing:
        scratch += [pltpu.VMEM(shape.shape, F32) for shape in shapes]
        shapes = (
            jax.ShapeDtypeStruct((2 * width + 32, block // 2), BF16),
            jax.ShapeDtypeStruct((8, block // 2), F32),
            jax.ShapeDtypeStruct((2 * width, block // 2), F32),
        )
    return pl.pallas_call(
        body,
        out_shape=shapes,
        in_specs=[VMEM] * (11 + len(segs) + count),
        out_specs=(VMEM,) * n_out,
        scratch_shapes=scratch,
        compiler_params=params(EARLIER_MIB),
        cost_estimate=cost(4 * rows * depth * width, 2**20, 0),
    )(slopes8, seg, gain, *segs, *pieces, w_own, w_pair, q_own, q_pair, *state)


def project(place, lse, out, got, wo_own, wo_pair, tokens):
    wide = out.shape[0]
    width, model = wo_own.shape

    def body(lse_ref, out_ref, got_ref, w0, w1, *refs):
        y_ref, ctx = refs[-2:]
        lanes = pl.ds(place * PIECE, PIECE)
        other = got_ref[pl.ds(wide, 32), lanes].astype(F32)
        other = other[0:8] + other[8:16] + other[16:24]
        for head in range(8):
            swapped = (head + 4) % 8
            mine, theirs = lse_ref[head : head + 1, lanes], other[swapped : swapped + 1]
            top = jnp.maximum(mine, theirs)
            weigh, weigh_other = jnp.exp2(mine - top), jnp.exp2(theirs - top)
            joined = (out_ref[pl.ds(head * HD, HD), lanes] * weigh
                      + got_ref[pl.ds(swapped * HD, HD), lanes].astype(F32) * weigh_other)
            joined = joined / (weigh + weigh_other)
            ctx[:, head * HD : (head + 1) * HD] = joined.T.astype(BF16)
        result = dot(ctx[:, :width], w0[...]) + dot(ctx[:, width:], w1[...])
        if tokens is not None:
            result = result + refs[0][...].astype(F32)
        y_ref[...] = result.astype(y_ref.dtype)

    extra = () if tokens is None else (tokens,)
    return pl.pallas_call(
        body,
        out_shape=jax.ShapeDtypeStruct((PIECE, model), BF16 if tokens is None else F32),
        in_specs=[VMEM] * (5 + len(extra)),
        out_specs=VMEM,
        scratch_shapes=[pltpu.VMEM((PIECE, wide), BF16)],
        compiler_params=params(16),
        cost_estimate=cost(PIECE * wide * model, 2**20, 0),
    )(lse, out, got, wo_own, wo_pair, *extra)


def on_device(tokens, ln_gain, w_qkv, slopes, w_out, seg_ids):
    blocks = lax.axis_size("seq")
    block_num = lax.axis_index("seq")
    odd = (block_num % 2) == 1

    def over_core(value):
        return lax.ppermute(value, "head", [(i, i ^ 1) for i in range(4)])

    def over_x(value):
        return lax.ppermute(value, "head", [(i, i ^ 2) for i in range(4)])

    def over_seq(value, pairs):
        return lax.ppermute(value, "seq", pairs)

    two_on = [(i, i + 2) for i in range(blocks - 2)]
    even_to_odd = [(i, i + 1) for i in range(0, blocks, 2)]
    odd_to_even = [(i + 1, i) for i in range(0, blocks, 2)]

    tie = lax.optimization_barrier
    w_all = jnp.transpose(w_qkv, (1, 0, 2))
    seg = seg_ids.reshape(4, PIECE)
    slopes = slopes.reshape(1, -1)
    gain = ln_gain.reshape(1, -1)
    w_pair = over_core(w_all)

    a2 = over_seq(tokens, two_on)
    b0 = over_x(tokens)
    a1_odd = over_seq(tokens, even_to_odd)
    c0 = over_core(tokens)
    slopes_sent, w_staged, c0 = tie((slopes, stage(w_all), c0))
    slopes_pair = over_core(slopes_sent)
    seg_sent, slopes_pair = tie((seg, slopes_pair))
    seg1 = over_seq(seg_sent, [(i, i + 1) for i in range(blocks - 1)])

    a2, b0, a1_odd, w_pair, w_staged, slopes_pair, seg1 = tie(
        (a2, b0, a1_odd, w_pair, w_staged, slopes_pair, seg1))
    a4 = over_seq(a2, two_on)
    b2 = over_x(a2)
    crossed = over_seq(a2, even_to_odd + odd_to_even)
    d0 = over_core(b0)
    seg1_sent, seg_sent, d0 = tie((seg1, seg, d0))
    seg23 = over_seq(jnp.concatenate([seg, seg1_sent], axis=0), two_on)
    seg4 = over_seq(seg_sent, [(i, i + SPAN) for i in range(blocks - SPAN)])
    segs = [seg1, seg23[:4], seg23[4:], seg4]
    q_own, q_pair, *state, key_cache, value_cache, slopes8 = own_block(
        slopes, slopes_pair, seg, gain, (tokens, b0, c0, d0), w_staged, w_pair)

    crossed, b2, a4, b0_sent, segs, state[0] = tie((crossed, b2, a4, b0, segs, state[0]))
    picked = pick(b0_sent, a4)
    over_y = over_seq(picked, even_to_odd + odd_to_even)
    x_third = over_x(crossed)
    b4 = over_seq(b2, two_on)

    def merge(closing, segs, pieces, which, state):
        return earlier_pieces(
            which, closing, slopes8, seg, segs, gain, pieces, w_staged, w_pair, q_own, q_pair, state)

    state = merge(
        False, segs, (a2, b2, a4, crossed, a1_odd),
        (((2, 0),) * 2, ((2, 1),) * 2, ((4, 0),) * 2, ((1, 0), (3, 0)), ((0, 0), (1, 0))), state)

    over_y, x_third, b4, wo_sent, held = tie((over_y, x_third, b4, w_out, state[0]))
    state = (held, *state[1:])
    b3_top = lax.ppermute(
        over_y[: PIECE // 2], ("seq", "head"),
        [(4 * i + head, 4 * i + (head ^ 2)) for i in range(0, blocks, 2) for head in range(4)])
    b3_rest = over_seq(b4[PIECE // 2 :], odd_to_even)
    wo_pair = over_core(wo_sent)
    state = merge(
        False, segs, (b4, x_third, over_y), (((4, 1),) * 2, ((1, 1), (3, 1)), ((3, 0), (1, 1))), state)
    send, lse, out = merge(True, segs, (b3_top, b3_rest), (((3, 1), (0, 0)),), state)
    got = over_core(send)
    y_pair = project(1, lse, out, got, w_out, wo_pair, None)
    y_got = over_x(y_pair)
    y_own = project(0, lse, out, got, w_out, wo_pair, tokens)
    hidden = (y_own + y_got.astype(F32)).astype(BF16)
    return (hidden, key_cache, value_cache)


def solution(mesh):
    in_specs = (
        P(("seq", "head"), None),
        P(),
        P(None, None, "head"),
        P("head"),
        P("head", None),
        P("seq"),
    )
    out_specs = (P(("seq", "head"), None), P("seq", "head"), P("seq", "head"))
    return jax.shard_map(
        on_device, mesh=mesh, in_specs=in_specs, out_specs=out_specs, check_vma=False
    )
```
